256 devices in a mesh: ctx: 32 (over y, z_hi, core), section: 8 (over z_lo, x).
Axes of the slice: x: 4, y: 4, z: 8 (z_hi: 4, z_lo: 2; z = z_hi * 2 + z_lo), core: 2. Of those that a mesh axis runs over, the one named last changes fastest.
Arguments:
- hidden: bfloat16 [8192, 5120], P('ctx'), may hold values from -6 to 6
- k_cache: bfloat16 [8192, 1024], P('ctx', 'section'), may hold values from -200 to 200
- v_cache: bfloat16 [8192, 1024], P('ctx', 'section'), may hold values from -6 to 6
- segment: int32 [8192], P('ctx'), may hold values from 0 to 15, never falling along the last dimension, each value on 1 to 6144 neighbouring positions
- w_query: bfloat16 [5120, 4096], P(None, 'section'), may hold values from -0.078125 to 0.078125
- w_out: bfloat16 [4096, 5120], P('section'), may hold values from -0.25 to 0.25
Outputs:
- mixed: bfloat16 [8192, 5120], P('ctx', 'section')
The draws below stay inside these ranges and needn't reach their ends.
Inputs may be any that keep to these rules, and one draw needn't show every extreme that they name: `segment`: document ids never fall along the tokens.
All inputs are finite; a program needn't handle non-finite values.
Results may differ from the reference program's by a relative error of at most 0.018.
The reference program's roundings to bfloat16 on the way count: a program that leaves them out, or rounds other values in their place, can miss the bound.
Values may be sent and summed in bfloat16 or wider, within the bound.
No kernel may reach another device: no remote copies, remote signals or barrier semaphores. Data moves between devices by JAX's collectives and lax.ppermute only.
A program may use at most 128 MiB of HBM per device.

```python
import math
import jax
import jax.numpy as jnp
import numpy as np
from jax import lax

D = 5120
HEADS = 32
KV_HEADS = 8
HEAD_DIM = 128
TOKENS = 8192
N_SECTION = 8


def draw_k_cache(key, part):
    base = jax.random.normal(jax.random.fold_in(key, 11), (TOKENS, KV_HEADS * HEAD_DIM), jnp.float32)
    base = jnp.clip(base, -5.0, 5.0)
    return base.astype(jnp.bfloat16)


def block_scale(own_key, shape, pieces, smallest, high):
    loudness = 1.0
    for axis_at, blocks in pieces:
        draws = jax.random.uniform(jax.random.fold_in(jax.random.fold_in(own_key, 6), axis_at), (blocks,), jnp.float32, smallest / len(pieces), high / len(pieces))
        loudness = loudness * jnp.repeat(jnp.exp(draws), shape[axis_at] // blocks).reshape((-1,) + (1,) * (len(shape) - 1 - axis_at))
    return loudness


def profile(count, total, bound, lean):
    weights = [(1 << 20) // math.isqrt(rank ** lean) + 1 for rank in range(2, count + 1)]
    surplus, given = total - bound - (count - 1), [1] * (count - 1)
    while surplus > 0:
        candidates = [i for i in range(count - 1) if given[i] < bound]
        mass, remaining = sum([weights[i] for i in candidates]), surplus
        for i in candidates:
            addition = min(bound - given[i], max(1, remaining * weights[i] // mass), surplus)
            given[i] = given[i] + addition
            surplus = surplus - addition
    return np.array([bound] + given)


def uneven_parts(key, number_of, total, reach, lean):
    if number_of == 2:
        one = jax.random.randint(key, (), max(1, total - reach), min(reach, total - 1) + 1)
        return jnp.stack([one, total - one])
    lengths = jnp.asarray(profile(number_of, total, reach, lean), jnp.int32)
    twos = (number_of - 1) // 2
    giver, sink = lengths[1:1 + 2 * twos:2], lengths[2:2 + 2 * twos:2]
    room = jnp.minimum(giver - 1, reach - sink)
    passed = jax.random.randint(jax.random.fold_in(key, 1), (twos,), 0, 1 << 20) % (room + 1)
    lengths = lengths.at[1:1 + 2 * twos:2].set(giver - passed).at[2:2 + 2 * twos:2].set(sink + passed)
    return lengths[jax.random.permutation(jax.random.fold_in(key, 2), number_of)]


def scatter_about(own_key, dims, scale, most, pieces=(), held_as=jnp.bfloat16):
    array = jax.random.normal(own_key, dims, jnp.float32) * scale
    if len(pieces) > 0:
        array = block_scale(own_key, dims, pieces, -0.22, 0.18) * array
    return jnp.clip(array, min=-most, max=most).astype(held_as)


def setup_inputs(seed: int = 0) -> dict:
    streams_of = jax.random.split(jax.random.key(seed), 7)
    hidden = scatter_about(streams_of[0], (TOKENS, D), 1.0, 6.0, ((0, 32),))
    k_cache = draw_k_cache(jax.random.fold_in(streams_of[6], 71), 0)
    v_cache = scatter_about(streams_of[2], (TOKENS, KV_HEADS * HEAD_DIM), 1.0, 6.0, ((0, 32), (1, 8)))
    segment = jnp.searchsorted(jnp.cumsum(uneven_parts(streams_of[3], 16, TOKENS, TOKENS * 3 // 4, 2)), jnp.arange(TOKENS), side="right").astype(jnp.int32)
    w_query = scatter_about(streams_of[4], (D, HEADS * HEAD_DIM), D ** -0.5, 0.078125, ((1, 8),))
    w_out = scatter_about(streams_of[5], (HEADS * HEAD_DIM, D), (HEAD_DIM * 4) ** -0.5, 0.25, ((0, 8),))
    return {"hidden": hidden, "k_cache": k_cache, "v_cache": v_cache, "segment": segment, "w_query": w_query, "w_out": w_out}


NEG_BIG = -1e+30

def reference(hidden, k_cache, v_cache, segment, w_query, w_out):
    widened = hidden.astype(jnp.float32)
    normed = (widened * lax.rsqrt(lax.optimization_barrier(jnp.mean(widened * widened, axis=-1, keepdims=True)) + 1e-06)).astype(jnp.bfloat16)
    queries = (jnp.dot(normed, w_query, preferred_element_type=jnp.float32) * HEAD_DIM ** (-0.5)).astype(jnp.bfloat16)
    per_group = HEADS // KV_HEADS
    query_heads = queries.reshape(TOKENS, KV_HEADS, per_group, HEAD_DIM)
    key_heads = k_cache.reshape(TOKENS, KV_HEADS, HEAD_DIM).astype(jnp.float32)
    value_heads = v_cache.reshape(TOKENS, KV_HEADS, HEAD_DIM).astype(jnp.float32)
    key_pos = jnp.arange(TOKENS, dtype=jnp.int32)
    block_len = math.gcd(TOKENS, 256)

    def one_block(block_index):
        offset = (block_index * block_len).astype(jnp.int32)
        block_q = lax.dynamic_slice_in_dim(query_heads, offset, block_len, 0).astype(jnp.float32)
        query_seg = lax.dynamic_slice_in_dim(segment, offset, block_len, 0)
        query_pos = offset + jnp.arange(block_len, dtype=jnp.int32)
        visible = (key_pos[None, :] <= query_pos[:, None]) & (segment[None, :] == query_seg[:, None])
        scores = jnp.einsum('tgrd,ngd->grtn', block_q, key_heads)
        masked = jnp.where(visible, scores, NEG_BIG)
        top = lax.optimization_barrier(jnp.max(masked, axis=-1))
        weights = jnp.where(visible, jnp.exp(masked - top[..., None]), 0.0)
        totals = lax.optimization_barrier(jnp.sum(weights, axis=-1))
        rounded = lax.optimization_barrier(weights.astype(jnp.bfloat16)).astype(jnp.float32)
        summed = jnp.einsum('grtn,ngd->grtd', rounded, value_heads)
        result = summed / totals[..., None]
        return result.transpose(2, 0, 1, 3).reshape(block_len, HEADS * HEAD_DIM)
    attended = lax.map(one_block, jnp.arange(TOKENS // block_len, dtype=jnp.int32))
    attended = attended.reshape(TOKENS, HEADS * HEAD_DIM).astype(jnp.bfloat16)
    rows_per = HEADS * HEAD_DIM // N_SECTION
    summed_out = jnp.zeros((TOKENS, D), jnp.float32)
    for section_index in range(N_SECTION):
        piece = jnp.dot(attended[:, section_index * rows_per:(section_index + 1) * rows_per], w_out[section_index * rows_per:(section_index + 1) * rows_per], preferred_element_type=jnp.float32)
        piece = lax.optimization_barrier(piece.astype(jnp.bfloat16)).astype(jnp.float32)
        summed_out = summed_out + piece
    return summed_out.astype(jnp.bfloat16)
```

```python
import functools

import jax
import jax.numpy as jnp
from jax import lax
from jax.experimental import pallas as pl
from jax.experimental.pallas import tpu as pltpu
from jax.sharding import PartitionSpec as P

HEAD_DIM = 128
BLOCK = 256
PACK = 2 * BLOCK + 16
REACH = 24
COLS = 640
FLOOR = -1e30
HIDDEN = -2e30

F32 = jnp.float32
BF16 = jnp.bfloat16


def ctx_id(y, z, c):
    return ((y + 8) % 4) * 8 + ((z + 8) % 4) * 2 + c


def ctx_pairs(step, planes=None):
    pairs = []
    for y in range(4):
        for z in range(4):
            for c in range(2):
                to = step(y, z, c)
                if to is not None:
                    pairs.append((ctx_id(y, z, c), ctx_id(*to)))
    return pairs


def move(x, step):
    return lax.ppermute(x, "ctx", ctx_pairs(step))


def swap_cores(x):
    return move(x, lambda y, z, c: (y, z, 1 - c))


def along_z(x):
    return move(x, lambda y, z, c: (y, z + 1 if c == 0 else z - 1, c))


def along_y(x):
    def step(y, z, c):
        if c == 0:
            return (y + 1, z, c) if y < 3 else None
        return (3, z, c) if y == 0 else None

    return move(x, step)


def attend_block(kv_ref, at, diagonal, q_ref, hot_ref, m_ref, l_ref, acc_ref):
    k = kv_ref[at, 0:BLOCK, :]
    v_t = jnp.transpose(kv_ref[at, BLOCK : 2 * BLOCK, :])
    counts = kv_ref[at, 2 * BLOCK : PACK, :]
    first = jnp.dot(counts, hot_ref[...], preferred_element_type=F32)[0:1, :]
    row = lax.broadcasted_iota(jnp.int32, (BLOCK, BLOCK), 0)
    visible = row >= first.astype(jnp.int32)
    if diagonal:
        visible &= row <= lax.broadcasted_iota(jnp.int32, (BLOCK, BLOCK), 1)
    for h in range(4):
        rows = slice(h * HEAD_DIM, (h + 1) * HEAD_DIM)
        s = jnp.dot(k, q_ref[rows, :], preferred_element_type=F32)
        s = jnp.where(visible, s, HIDDEN)
        m_old = m_ref[h : h + 1, :]
        m_new = jnp.maximum(m_old, jnp.max(s, axis=0, keepdims=True))
        p = jnp.exp(s - m_new)
        fade = jnp.exp(m_old - m_new)
        m_ref[h : h + 1, :] = m_new
        l_ref[h : h + 1, :] = fade * l_ref[h : h + 1, :] + jnp.sum(p, axis=0, keepdims=True)
        acc_ref[rows, :] = fade * acc_ref[rows, :] + jnp.dot(v_t, p.astype(BF16), preferred_element_type=F32)


def attend_pieces(ids_ref, kv_refs, *refs):
    own = ids_ref[0]
    base = 1
    for kv_ref in kv_refs:
        n = kv_ref.shape[0]

        @pl.loop(0, n)
        def _(i, kv_ref=kv_ref, base=base):
            block = ids_ref[base + i]

            @pl.when((block < own) & (block >= own - REACH))
            def _():
                attend_block(kv_ref, i, False, *refs)

        base += n


def start_kernel(n, ids_ref, own_ref, *rest):
    kv_refs, (q_ref, hot_ref, m_ref, l_ref, acc_ref) = rest[:n], rest[n:]
    m_ref[...] = jnp.full_like(m_ref, FLOOR)
    l_ref[...] = jnp.zeros_like(l_ref)
    acc_ref[...] = jnp.zeros_like(acc_ref)
    refs = (q_ref, hot_ref, m_ref, l_ref, acc_ref)
    attend_block(own_ref, 0, True, *refs)
    attend_pieces(ids_ref, kv_refs, *refs)


def more_kernel(n, ids_ref, *rest):
    kv_refs, (q_ref, hot_ref, m_in, l_in, acc_in, m_ref, l_ref, acc_ref) = rest[:n], rest[n:]
    m_ref[...] = m_in[...]
    l_ref[...] = l_in[...]
    acc_ref[...] = acc_in[...]
    attend_pieces(ids_ref, kv_refs, q_ref, hot_ref, m_ref, l_ref, acc_ref)


def last_kernel(n, ids_ref, to_ref, *rest):
    kv_refs, rest = rest[:n], rest[n:]
    (q_ref, hot_ref, m_in, l_in, acc_in, w_hbm, b1, b0, a1, a3, a2, a0, m_ref, l_ref, acc_ref, att_ref, w_ref, sem) = rest
    copy = pltpu.make_async_copy(w_hbm, w_ref, sem)
    copy.start()
    m_ref[...] = m_in[...]
    l_ref[...] = l_in[...]
    acc_ref[...] = acc_in[...]
    attend_pieces(ids_ref, kv_refs, q_ref, hot_ref, m_ref, l_ref, acc_ref)
    for h in range(4):
        rows = slice(h * HEAD_DIM, (h + 1) * HEAD_DIM)
        att_ref[:, rows] = jnp.transpose(acc_ref[rows, :] / l_ref[h : h + 1, :]).astype(BF16)
    copy.wait()
    half = BLOCK // 2
    b_to, a_to = (b0, b1), (a0, a1, a2, a3)
    for dz in range(2):

        @pl.loop(0, 4)
        def _(dx, dz=dz):
            at = pl.multiple_of(to_ref[dz * 4 + dx] * COLS, 128)
            w = w_ref[:, pl.ds(at, COLS)]
            b_to[dz][dx] = jnp.dot(att_ref[half:, :], w, preferred_element_type=F32).astype(BF16)

    for dx in range(4):

        @pl.loop(0, 2)
        def _(dz, dx=dx):
            at = pl.multiple_of(to_ref[dz * 4 + dx] * COLS, 128)
            w = w_ref[:, pl.ds(at, COLS)]
            a_to[dx][dz] = jnp.dot(att_ref[:half, :], w, preferred_element_type=F32).astype(BF16)


VMEM = pl.BlockSpec(memory_space=pltpu.VMEM)
SMEM = pl.BlockSpec(memory_space=pltpu.SMEM)
CARRY = (
    jax.ShapeDtypeStruct((8, BLOCK), F32),
    jax.ShapeDtypeStruct((8, BLOCK), F32),
    jax.ShapeDtypeStruct((4 * HEAD_DIM, BLOCK), F32),
)
LIMIT = pltpu.CompilerParams(vmem_limit_bytes=32 * 1024 * 1024)


def cost(n):
    return pl.CostEstimate(
        flops=n * 4 * 4 * BLOCK * BLOCK * HEAD_DIM,
        bytes_accessed=n * PACK * HEAD_DIM * 2,
        transcendentals=n * 4 * BLOCK * BLOCK,
    )


def per_device(hidden, k_cache, v_cache, segment, w_query, w_out):
    ctx = lax.axis_index("ctx")
    y, z, c = ctx // 8, (ctx // 2) % 4, ctx % 2

    smaller = jnp.sum(
        (segment[:, None] < jnp.arange(HEAD_DIM, dtype=jnp.int32)[None, :]).astype(F32), axis=0
    ).astype(BF16)
    own = jnp.concatenate([k_cache, v_cache, jnp.broadcast_to(smaller[None, :], (16, HEAD_DIM))], axis=0)[None]

    other = swap_cores(own)
    z_far = move(own, lambda y, z, c: (y, z + 2, c))
    y_far = move(own, lambda y, z, c: (y + 2, z, c) if y < 2 else None)
    pair = jnp.concatenate([own, other], axis=0)
    z_near = along_z(pair)
    y_near = along_y(pair)

    widened = hidden.astype(F32)
    normed = (widened * lax.rsqrt(jnp.mean(widened * widened, axis=-1, keepdims=True) + 1e-06)).astype(BF16)
    q_t = (
        lax.dot_general(w_query, normed, (((0,), (1,)), ((), ())), preferred_element_type=F32) * HEAD_DIM ** (-0.5)
    ).astype(BF16)
    hot = (jnp.arange(HEAD_DIM, dtype=jnp.int32)[:, None] == segment[None, :]).astype(BF16)

    mine = jnp.concatenate([z_near, z_far, y_near, y_far], axis=0)
    theirs = swap_cores(mine)
    y_rest = along_y(jnp.concatenate([mine[:3], theirs[:3]], axis=0))
    across_far = move(y_far, lambda y, z, c: (y, z + 2, c) if y >= 2 else None)

    def ring_z(y, z, c):
        return (y, z + 1 if c == 0 else z - 1, c) if y >= 2 else None

    across_near = move(jnp.concatenate([y_far, theirs[5:]], axis=0), ring_z)

    def slots(c):
        d, e = 2 * c - 1, 1 - c
        mine = [
            (y, z + d, c), (y, z + d, e), (y, z + 2, c),
            (y + d, z, c), (y + d, z, e), (y + 2, z, c),
        ]
        y_rest = [
            (y + d, z + d, c), (y + d, z + d, e), (y + d, z + 2, c),
            (y + d, z - d, e), (y + d, z - d, c), (y + d, z + 2, e),
        ]
        across = [(y + 2, z + d, c), (y + 2, z + d, e), (y + 2, z + 2, c)]
        return mine, y_rest, across

    def ids_of(places):
        return jnp.stack([ctx] + [ctx_id(*p) for p in places]).astype(jnp.int32)

    mine_at, rest_at, across_at = slots(c)
    theirs_at, rest_at_2, across_at_2 = slots(1 - c)

    state = pl.pallas_call(
        functools.partial(start_kernel, 3),
        out_shape=CARRY,
        in_specs=[SMEM] + [VMEM] * 6,
        out_specs=(VMEM,) * 3,
        compiler_params=LIMIT,
        cost_estimate=cost(14),
        name="attend_row",
    )(ids_of([(y, z, 1 - c)] + mine_at + theirs_at), own, other, mine, theirs, q_t, hot)

    got = jnp.concatenate([y_rest, across_near, across_far], axis=0)
    got_2 = swap_cores(got)
    state = pl.pallas_call(
        functools.partial(more_kernel, 1),
        out_shape=CARRY,
        in_specs=[SMEM] + [VMEM] * 6,
        out_specs=(VMEM,) * 3,
        compiler_params=LIMIT,
        cost_estimate=cost(9),
        name="attend_received",
    )(ids_of(rest_at + across_at), got, q_t, hot, *state)

    section = lax.axis_index("section")
    to = jnp.stack([((section // 4 + dz) % 2) * 4 + (section % 4 + dx) % 4 for dz in range(2) for dx in range(4)])
    half = BLOCK // 2
    part = lambda n: jax.ShapeDtypeStruct((n, half, COLS), BF16)
    b1, b0, a1, a3, a2, a0 = pl.pallas_call(
        functools.partial(last_kernel, 1),
        out_shape=(part(4), part(4), part(2), part(2), part(2), part(2)),
        in_specs=[SMEM, SMEM] + [VMEM] * 6 + [pl.BlockSpec(memory_space=pl.ANY)],
        out_specs=(VMEM,) * 6,
        scratch_shapes=[
            pltpu.VMEM((8, BLOCK), F32),
            pltpu.VMEM((8, BLOCK), F32),
            pltpu.VMEM((4 * HEAD_DIM, BLOCK), F32),
            pltpu.VMEM((BLOCK, 4 * HEAD_DIM), BF16),
            pltpu.VMEM(w_out.shape, BF16),
            pltpu.SemaphoreType.DMA,
        ],
        compiler_params=LIMIT,
        cost_estimate=cost(12),
        name="attend_and_project",
    )(ids_of(rest_at_2 + across_at_2), to.astype(jnp.int32), got_2, q_t, hot, *state, w_out)

    def send_x(t, k):
        return lax.ppermute(t, "section", [(g * 4 + x, g * 4 + (x + k) % 4) for g in range(2) for x in range(4)])

    def send_z(t):
        return lax.ppermute(t, "section", [(g * 4 + x, (1 - g) * 4 + x) for g in range(2) for x in range(4)])

    b_in = send_z(b1)
    a_in = [send_x(a, k) for a, k in ((a1, 1), (a3, 3), (a2, 2))]
    b_sum = b0.astype(F32) + b_in.astype(F32)
    b_out = [send_x(b_sum[k].astype(BF16), k) for k in (1, 3, 2)]
    a_sum = a0.astype(F32) + a_in[0].astype(F32) + a_in[1].astype(F32) + a_in[2].astype(F32)
    a_out = send_z(a_sum[1].astype(BF16))
    a = a_sum[0] + a_out.astype(F32)
    b = b_sum[0] + b_out[0].astype(F32) + b_out[1].astype(F32) + b_out[2].astype(F32)
    return jnp.concatenate([a, b], axis=0).astype(BF16)


def solution(mesh):
    return jax.shard_map(
        per_device,
        mesh=mesh,
        in_specs=(
            P("ctx", None),
            P("ctx", "section"),
            P("ctx", "section"),
            P("ctx"),
            P(None, "section"),
            P("section", None),
        ),
        out_specs=P("ctx", "section"),
        check_vma=False,
    )
```

```python
import functools

import jax
import jax.numpy as jnp
from jax import lax
from jax.experimental import pallas as pl
from jax.experimental.pallas import tpu as pltpu
from jax.sharding import PartitionSpec as P
import numpy as np

HEAD_DIM = 128
BLOCK = 256
PACK = 2 * BLOCK + 16
REACH = 24
COLS = 640
FLOOR = -1e30
HIDDEN = -2e30

F32 = jnp.float32
BF16 = jnp.bfloat16


def ctx_id(y, z, c):
    return ((y + 8) % 4) * 8 + ((z + 8) % 4) * 2 + c


def ctx_pairs(step, planes=None):
    pairs = []
    for y in range(4):
        for z in range(4):
            for c in range(2):
                to = step(y, z, c)
                if to is not None:
                    pairs.append((ctx_id(y, z, c), ctx_id(*to)))
    return pairs


def move(x, step):
    return lax.ppermute(x, "ctx", ctx_pairs(step))


def swap_cores(x):
    return move(x, lambda y, z, c: (y, z, 1 - c))


def along_z(x):
    return move(x, lambda y, z, c: (y, z + 1 if c == 0 else z - 1, c))


def along_y(x):
    def step(y, z, c):
        if c == 0:
            return (y + 1, z, c) if y < 3 else None
        return (3, z, c) if y == 0 else None

    return move(x, step)


def attend_blocks(kv_ref, places, diagonal, q_ref, hot_ref, m_ref, l_ref, acc_ref):
    heads = [slice(h * HEAD_DIM, (h + 1) * HEAD_DIM) for h in range(4)]
    keys, values, visible = [], [], []
    for at, low in places:
        keys.append(kv_ref[at, 0:BLOCK, :])
        values.append(jnp.transpose(kv_ref[at, BLOCK : 2 * BLOCK, :]))
        counts = kv_ref[at, 2 * BLOCK : PACK, :]
        first = jnp.dot(counts, hot_ref[...], preferred_element_type=F32)[0:1, :].astype(jnp.int32)
        row = lax.broadcasted_iota(jnp.int32, (BLOCK, BLOCK), 0)
        seen = row >= jnp.maximum(first, low)
        if diagonal:
            seen &= row <= lax.broadcasted_iota(jnp.int32, (BLOCK, BLOCK), 1)
        visible.append(seen)
    scores = [[jnp.dot(k, q_ref[rows, :], preferred_element_type=F32) for k in keys] for rows in heads]
    old = [(m_ref[h : h + 1, :], l_ref[h : h + 1, :]) for h in range(4)]
    new = []
    for h in range(4):
        masked = [jnp.where(seen, s, HIDDEN) for seen, s in zip(visible, scores[h])]
        m_old, total = old[h]
        m_new = m_old
        for s in masked:
            m_new = jnp.maximum(m_new, jnp.max(s, axis=0, keepdims=True))
        weights = [jnp.exp(s - m_new) for s in masked]
        fade = jnp.exp(m_old - m_new)
        total = fade * total
        for p in weights:
            total = total + jnp.sum(p, axis=0, keepdims=True)
        added = sum(jnp.dot(v, p.astype(BF16), preferred_element_type=F32) for v, p in zip(values, weights))
        new.append((m_new, total, fade, added))
    for h, rows in enumerate(heads):
        m_new, total, fade, added = new[h]
        m_ref[h : h + 1, :] = m_new
        l_ref[h : h + 1, :] = total
        acc_ref[rows, :] = fade * acc_ref[rows, :] + added


def attend_pieces(ids_ref, base, kv_refs, order_ref, *refs):
    own = ids_ref[0]
    for kv_ref in kv_refs:
        n = kv_ref.shape[0]
        count = jnp.int32(0)
        for i in range(n):
            block = ids_ref[base + i]
            order_ref[count] = i
            count += ((block < own) & (block >= own - REACH)).astype(jnp.int32)

        @pl.loop(0, (count + 1) // 2)
        def _(g, kv_ref=kv_ref, count=count):
            one = order_ref[2 * g]
            both = 2 * g + 1 < count
            two = jnp.where(both, order_ref[2 * g + 1], one)
            places = [(one, 0), (two, jnp.where(both, 0, BLOCK))]
            attend_blocks(kv_ref, places, False, *refs)

        base += n


def start_kernel(n, base, ids_ref, own_ref, *rest):
    kv_refs, (q_ref, hot_ref, m_ref, l_ref, acc_ref, order_ref) = rest[:n], rest[n:]
    m_ref[...] = jnp.full_like(m_ref, FLOOR)
    l_ref[...] = jnp.zeros_like(l_ref)
    acc_ref[...] = jnp.zeros_like(acc_ref)
    refs = (q_ref, hot_ref, m_ref, l_ref, acc_ref)
    attend_blocks(own_ref, [(0, 0)], True, *refs)
    attend_pieces(ids_ref, base, kv_refs, order_ref, *refs)


def more_kernel(n, base, ids_ref, *rest):
    kv_refs, (q_ref, hot_ref, m_in, l_in, acc_in, m_ref, l_ref, acc_ref, order_ref) = rest[:n], rest[n:]
    m_ref[...] = m_in[...]
    l_ref[...] = l_in[...]
    acc_ref[...] = acc_in[...]
    attend_pieces(ids_ref, base, kv_refs, order_ref, q_ref, hot_ref, m_ref, l_ref, acc_ref)


def last_kernel(n, base, ids_ref, to_ref, *rest):
    kv_refs, rest = rest[:n], rest[n:]
    (q_ref, hot_ref, m_in, l_in, acc_in, w_hbm, b1, b0, a1, a3, a2, a0) = rest[:12]
    m_ref, l_ref, acc_ref, att_ref, w_ref, order_ref, sem = rest[12:]
    copy = pltpu.make_async_copy(w_hbm, w_ref, sem)
    copy.start()
    m_ref[...] = m_in[...]
    l_ref[...] = l_in[...]
    acc_ref[...] = acc_in[...]
    attend_pieces(ids_ref, base, kv_refs, order_ref, q_ref, hot_ref, m_ref, l_ref, acc_ref)
    for h in range(4):
        rows = slice(h * HEAD_DIM, (h + 1) * HEAD_DIM)
        att_ref[:, rows] = jnp.transpose(acc_ref[rows, :] / l_ref[h : h + 1, :]).astype(BF16)
    copy.wait()
    half = BLOCK // 2
    b_to, a_to = (b0, b1), (a0, a1, a2, a3)
    for dz in range(2):
        for dx in range(4):
            at = pl.multiple_of(to_ref[dz * 4 + dx] * COLS, 128)
            part = jnp.dot(att_ref[...], w_ref[:, pl.ds(at, COLS)], preferred_element_type=F32).astype(BF16)
            a_to[dx][dz] = part[:half]
            b_to[dz][dx] = part[half:]


VMEM = pl.BlockSpec(memory_space=pltpu.VMEM)
SMEM = pl.BlockSpec(memory_space=pltpu.SMEM)
CARRY = (
    jax.ShapeDtypeStruct((8, BLOCK), F32),
    jax.ShapeDtypeStruct((8, BLOCK), F32),
    jax.ShapeDtypeStruct((4 * HEAD_DIM, BLOCK), F32),
)
LIMIT = pltpu.CompilerParams(vmem_limit_bytes=32 * 1024 * 1024)


def cost(n):
    return pl.CostEstimate(
        flops=n * 4 * 4 * BLOCK * BLOCK * HEAD_DIM,
        bytes_accessed=n * PACK * HEAD_DIM * 2,
        transcendentals=n * 4 * BLOCK * BLOCK,
    )


def per_device(hidden, k_cache, v_cache, segment, w_query, w_out):
    ctx = lax.axis_index("ctx")
    y, z, c = ctx // 8, (ctx // 2) % 4, ctx % 2

    smaller = jnp.sum(
        (segment[:, None] < jnp.arange(HEAD_DIM, dtype=jnp.int32)[None, :]).astype(F32), axis=0
    ).astype(BF16)
    own = jnp.concatenate([k_cache, v_cache, jnp.broadcast_to(smaller[None, :], (16, HEAD_DIM))], axis=0)[None]

    other = swap_cores(own)
    z_far = move(own, lambda y, z, c: (y, z + 2, c))
    y_far = move(own, lambda y, z, c: (y + 2, z, c) if y < 2 else None)
    pair = jnp.concatenate([own, other], axis=0)
    z_near = along_z(pair)
    y_near = along_y(pair)

    widened = hidden.astype(F32)
    normed = (widened * lax.rsqrt(jnp.mean(widened * widened, axis=-1, keepdims=True) + 1e-06)).astype(BF16)
    q_t = (
        lax.dot_general(w_query, normed, (((0,), (1,)), ((), ())), preferred_element_type=F32) * HEAD_DIM ** (-0.5)
    ).astype(BF16)
    hot = (jnp.arange(HEAD_DIM, dtype=jnp.int32)[:, None] == segment[None, :]).astype(BF16)

    def slots(y, z, c):
        d, e = 2 * c - 1, 1 - c
        mine = [
            (y, z + d, c), (y, z + d, e), (y, z + 2, c),
            (y + d, z, c), (y + d, z, e), (y + 2, z, c),
        ]
        y_rest = [
            (y + d, z + d, c), (y + d, z + d, e), (y + d, z + 2, c),
            (y + d, z - d, e), (y + d, z - d, c), (y + d, z + 2, e),
        ]
        across = [(y + 2, z + d, c), (y + 2, z + d, e), (y + 2, z + 2, c)]
        return mine, y_rest + across

    def row_of(y, z, c):
        mine, later = slots(y, z, c)
        theirs, later_2 = slots(y, z, 1 - c)
        return [ctx_id(*p) for p in [(y, z, c), (y, z, 1 - c)] + mine + theirs + later + later_2]

    table = np.array([row_of(i // 8, i // 2 % 4, i % 2) for i in range(32)], np.int32)
    ids = lax.dynamic_index_in_dim(jnp.asarray(table), ctx, 0, keepdims=False)

    mine = jnp.concatenate([z_near, z_far, y_near, y_far], axis=0)
    mine, q_t = lax.optimization_barrier((mine, q_t))
    theirs = swap_cores(mine)
    y_rest = along_y(jnp.concatenate([mine[:3], theirs[:3]], axis=0))
    across_far = move(y_far, lambda y, z, c: (y, z + 2, c) if y >= 2 else None)

    def ring_z(y, z, c):
        return (y, z + 1 if c == 0 else z - 1, c) if y >= 2 else None

    across_near = move(jnp.concatenate([y_far, theirs[5:]], axis=0), ring_z)

    state = pl.pallas_call(
        functools.partial(start_kernel, 3, 1),
        out_shape=CARRY,
        in_specs=[SMEM] + [VMEM] * 6,
        out_specs=(VMEM,) * 3,
        scratch_shapes=[pltpu.SMEM((16,), jnp.int32)],
        compiler_params=LIMIT,
        cost_estimate=cost(14),
        name="attend_row",
    )(ids, own, other, mine, theirs, q_t, hot)

    got = jnp.concatenate([y_rest, across_near, across_far], axis=0)
    got, state = lax.optimization_barrier((got, state))
    got_2 = swap_cores(got)
    state = pl.pallas_call(
        functools.partial(more_kernel, 1, 14),
        out_shape=CARRY,
        in_specs=[SMEM] + [VMEM] * 6,
        out_specs=(VMEM,) * 3,
        scratch_shapes=[pltpu.SMEM((16,), jnp.int32)],
        compiler_params=LIMIT,
        cost_estimate=cost(9),
        name="attend_received",
    )(ids, got, q_t, hot, *state)

    section = lax.axis_index("section")
    place = np.array(
        [[(s // 4 + dz) % 2 * 4 + (s % 4 + dx) % 4 for dz in range(2) for dx in range(4)] for s in range(8)], np.int32
    )
    to = lax.dynamic_index_in_dim(jnp.asarray(place), section, 0, keepdims=False)
    half = BLOCK // 2
    part = lambda n: jax.ShapeDtypeStruct((n, half, COLS), BF16)
    b1, b0, a1, a3, a2, a0 = pl.pallas_call(
        functools.partial(last_kernel, 1, 23),
        out_shape=(part(4), part(4), part(2), part(2), part(2), part(2)),
        in_specs=[SMEM, SMEM] + [VMEM] * 6 + [pl.BlockSpec(memory_space=pl.ANY)],
        out_specs=(VMEM,) * 6,
        scratch_shapes=[
            pltpu.VMEM((8, BLOCK), F32),
            pltpu.VMEM((8, BLOCK), F32),
            pltpu.VMEM((4 * HEAD_DIM, BLOCK), F32),
            pltpu.VMEM((BLOCK, 4 * HEAD_DIM), BF16),
            pltpu.VMEM(w_out.shape, BF16),
            pltpu.SMEM((16,), jnp.int32),
            pltpu.SemaphoreType.DMA,
        ],
        compiler_params=LIMIT,
        cost_estimate=cost(12),
        name="attend_and_project",
    )(ids, to, got_2, q_t, hot, *state, w_out)

    def send_x(t, k):
        return lax.ppermute(t, "section", [(g * 4 + x, g * 4 + (x + k) % 4) for g in range(2) for x in range(4)])

    def send_z(t):
        return lax.ppermute(t, "section", [(g * 4 + x, (1 - g) * 4 + x) for g in range(2) for x in range(4)])

    b_in = send_z(b1)
    a_in = [send_x(a, k) for a, k in ((a1, 1), (a3, 3), (a2, 2))]
    b_sum = b0.astype(F32) + b_in.astype(F32)
    b_out = [send_x(b_sum[k].astype(BF16), k) for k in (1, 3, 2)]
    a_in, b_out = list(a_in), list(b_out)
    a_in[0], b_out[0] = lax.optimization_barrier((a_in[0], b_out[0]))
    a_sum = a0.astype(F32) + a_in[0].astype(F32) + a_in[1].astype(F32) + a_in[2].astype(F32)
    a_out = send_z(a_sum[1].astype(BF16))
    a = a_sum[0] + a_out.astype(F32)
    b = b_sum[0] + b_out[0].astype(F32) + b_out[1].astype(F32) + b_out[2].astype(F32)
    return jnp.concatenate([a, b], axis=0).astype(BF16)


def solution(mesh):
    return jax.shard_map(
        per_device,
        mesh=mesh,
        in_specs=(
            P("ctx", None),
            P("ctx", "section"),
            P("ctx", "section"),
            P("ctx"),
            P(None, "section"),
            P("section", None),
        ),
        out_specs=P("ctx", "section"),
        check_vma=False,
    )
```

```python
import functools

import jax
import jax.numpy as jnp
from jax import lax
from jax.experimental import pallas as pl
from jax.experimental.pallas import tpu as pltpu
from jax.sharding import PartitionSpec as P
import numpy as np

HEAD_DIM = 128
BLOCK = 256
PACK = 2 * BLOCK + 16
REACH = 24
HALF = BLOCK // 2
COLS = 640
FLOOR = -1e30
HIDDEN = -2e30

F32 = jnp.float32
BF16 = jnp.bfloat16


def ctx_id(y, z, c):
    return ((y + 8) % 4) * 8 + ((z + 8) % 4) * 2 + c


def ctx_pairs(step, planes=None):
    pairs = []
    for y in range(4):
        for z in range(4):
            for c in range(2):
                to = step(y, z, c)
                if to is not None:
                    pairs.append((ctx_id(y, z, c), ctx_id(*to)))
    return pairs


def move(x, step):
    return lax.ppermute(x, "ctx", ctx_pairs(step))


def swap_cores(x):
    return move(x, lambda y, z, c: (y, z, 1 - c))


def up_y(x):
    return move(x, lambda y, z, c: (y + 1, z, c) if y < 3 else None)


def round_y(x):
    return move(x, lambda y, z, c: (3, z, c) if y == 0 else None)


def first_slots(y, z, c):
    row = [(y, z - 1, c), (y, z + 1, c), (y, z + 2, c)]
    return row + [(y - 1, z, c), (y + 1, z, c), (y + 2, z, c)]


def later_slots(y, z, c):
    around = [(y - 1, z - 1, c), (y - 1, z + 1, c), (y - 1, z + 2, c)]
    around += [(y + 1, z - 1, c), (y + 1, z + 1, c), (y + 1, z + 2, c)]
    return around + [(y + 2, z - 1, c), (y + 2, z + 1, c), (y + 2, z + 2, c)]


def pair_rows(group):
    half, pair = group // 2, group % 2
    cols = slice(half * HALF, (half + 1) * HALF)
    return [(h, slice(h * HEAD_DIM, (h + 1) * HEAD_DIM), cols) for h in (2 * pair, 2 * pair + 1)]


def attend_blocks(kv_ref, places, diagonal, groups, q_ref, hot_ref, m_ref, l_ref, acc_ref):
    halves = sorted({g // 2 for g in groups})
    keys, values, visible = [], [], []
    row = lax.broadcasted_iota(jnp.int32, (BLOCK, BLOCK), 0)
    for at, low in places:
        keys.append(kv_ref[at, 0:BLOCK, :])
        values.append(jnp.transpose(kv_ref[at, BLOCK : 2 * BLOCK, :]))
        counts = kv_ref[at, 2 * BLOCK : PACK, :]
        first = jnp.dot(counts, hot_ref[...], preferred_element_type=F32)[0:1, :].astype(jnp.int32)
        first = jnp.maximum(first, low)
        seen = {}
        for half in halves:
            mine = first[:, half * HALF : (half + 1) * HALF]
            seen[half] = row >= jnp.concatenate([mine, mine], axis=1)
            if diagonal:
                token = lax.broadcasted_iota(jnp.int32, (BLOCK, BLOCK), 1) % HALF + half * HALF
                seen[half] &= row <= token
        visible.append(seen)

    def side(ref_of):
        return jnp.concatenate(ref_of, axis=1)

    scores, old = [], []
    for group in groups:
        rows = pair_rows(group)
        q = side([q_ref[r, c] for _, r, c in rows])
        scores.append([jnp.dot(k, q, preferred_element_type=F32) for k in keys])
        old.append((side([m_ref[h : h + 1, c] for h, _, c in rows]), side([l_ref[h : h + 1, c] for h, _, c in rows])))
    new = []
    for n, group in enumerate(groups):
        masked = [jnp.where(seen[group // 2], s, HIDDEN) for seen, s in zip(visible, scores[n])]
        m_old, total = old[n]
        m_new = m_old
        for s in masked:
            m_new = jnp.maximum(m_new, jnp.max(s, axis=0, keepdims=True))
        weights = [jnp.exp(s - m_new) for s in masked]
        fade = jnp.exp(m_old - m_new)
        total = fade * total
        for p in weights:
            total = total + jnp.sum(p, axis=0, keepdims=True)
        added = sum(jnp.dot(v, p.astype(BF16), preferred_element_type=F32) for v, p in zip(values, weights))
        new.append((m_new, total, fade, added))
    for n, group in enumerate(groups):
        m_new, total, fade, added = new[n]
        for i, (h, r, c) in enumerate(pair_rows(group)):
            part = slice(i * HALF, (i + 1) * HALF)
            m_ref[h : h + 1, c] = m_new[:, part]
            l_ref[h : h + 1, c] = total[:, part]
            acc_ref[r, c] = fade[:, part] * acc_ref[r, c] + added[:, part]


def attend_pieces(own, pieces, order_ref, groups, *refs):
    for kv_ref, places in pieces:
        count = jnp.int32(0)
        for i, place in enumerate(places):
            block = ctx_id(*place)
            order_ref[count] = i
            count += ((block < own) & (block >= own - REACH)).astype(jnp.int32)

        @pl.loop(0, (count + 1) // 2)
        def _(g, kv_ref=kv_ref, count=count):
            one = order_ref[2 * g]
            both = 2 * g + 1 < count
            two = jnp.where(both, order_ref[2 * g + 1], one)
            attend_blocks(kv_ref, [(one, 0), (two, jnp.where(both, 0, BLOCK))], False, groups, *refs)


def where_am_i(at_ref):
    own = at_ref[0]
    return own, own // 8, (own // 2) % 4, own % 2


def start_kernel(at_ref, own_ref, mine_ref, theirs_ref, q_ref, hot_ref, m_ref, l_ref, acc_ref, order_ref):
    own, y, z, c = where_am_i(at_ref)
    m_ref[...] = jnp.full_like(m_ref, FLOOR)
    l_ref[...] = jnp.zeros_like(l_ref)
    acc_ref[...] = jnp.zeros_like(acc_ref)
    refs = (q_ref, hot_ref, m_ref, l_ref, acc_ref)
    attend_blocks(own_ref, [(0, 0)], True, range(4), *refs)
    pieces = [
        (mine_ref, first_slots(y, z, c)),
        (theirs_ref, [(y, z, 1 - c)] + first_slots(y, z, 1 - c)),
    ]
    attend_pieces(own, pieces, order_ref, range(4), *refs)


def more_kernel(at_ref, got_ref, q_ref, hot_ref, m_in, l_in, acc_in, m_ref, l_ref, acc_ref, order_ref):
    own, y, z, c = where_am_i(at_ref)
    m_ref[...] = m_in[...]
    l_ref[...] = l_in[...]
    acc_ref[...] = acc_in[...]
    pieces = [(got_ref, later_slots(y, z, c))]
    attend_pieces(own, pieces, order_ref, range(4), q_ref, hot_ref, m_ref, l_ref, acc_ref)


def target(at_ref, dz, dx):
    section = at_ref[1]
    to = (section // 4 + dz) % 2 * 4 + (section + dx) % 4
    return pl.ds(pl.multiple_of(to * COLS, 128), COLS)


def project(at_ref, att, w_ref, dz, dx):
    return jnp.dot(att, w_ref[:, target(at_ref, dz, dx)], preferred_element_type=F32).astype(BF16)


def finish_kernel(half, places, at_ref, got_ref, q_ref, hot_ref, m_in, l_in, acc_in, w_hbm, *rest):
    att_ref, parts, (m_ref, l_ref, acc_ref, w_ref, order_ref, sem) = rest[0], rest[1:-6], rest[-6:]
    copy = pltpu.make_async_copy(w_hbm, w_ref, sem)
    copy.start()
    own, y, z, c = where_am_i(at_ref)
    m_ref[...] = m_in[...]
    l_ref[...] = l_in[...]
    acc_ref[...] = acc_in[...]
    pieces = [(got_ref, later_slots(y, z, 1 - c))]
    attend_pieces(own, pieces, order_ref, range(2 * half, 2 * half + 2), q_ref, hot_ref, m_ref, l_ref, acc_ref)
    cols = slice(half * HALF, (half + 1) * HALF)
    for h in range(4):
        rows = slice(h * HEAD_DIM, (h + 1) * HEAD_DIM)
        att_ref[:, rows] = jnp.transpose(acc_ref[rows, cols] / l_ref[h : h + 1, cols]).astype(BF16)
    copy.wait()
    for part, targets in zip(parts, places):
        for i, (dz, dx) in enumerate(targets):
            part[i] = project(at_ref, att_ref[...], w_ref, dz, dx)


def own_kernel(at_ref, att_a, att_b, w_hbm, a_ref, b_ref, w_ref, sem):
    copy = pltpu.make_async_copy(w_hbm, w_ref, sem)
    copy.start()
    copy.wait()
    for dz in range(2):
        a_ref[dz] = project(at_ref, att_a[...], w_ref, dz, 0)
    for dx in range(4):
        b_ref[dx] = project(at_ref, att_b[...], w_ref, 0, dx)


VMEM = pl.BlockSpec(memory_space=pltpu.VMEM)
SMEM = pl.BlockSpec(memory_space=pltpu.SMEM)
CARRY = (
    jax.ShapeDtypeStruct((8, BLOCK), F32),
    jax.ShapeDtypeStruct((8, BLOCK), F32),
    jax.ShapeDtypeStruct((4 * HEAD_DIM, BLOCK), F32),
)
LIMIT = pltpu.CompilerParams(vmem_limit_bytes=32 * 1024 * 1024)
WHOLE = pltpu.CompilerParams(vmem_limit_bytes=59 * 1024 * 1024)


def cost(n):
    return pl.CostEstimate(
        flops=n * 4 * 4 * BLOCK * BLOCK * HEAD_DIM,
        bytes_accessed=n * PACK * HEAD_DIM * 2,
        transcendentals=n * 4 * BLOCK * BLOCK,
    )


def per_device(hidden, k_cache, v_cache, segment, w_query, w_out):
    ctx = lax.axis_index("ctx")

    smaller = jnp.sum(
        (segment[:, None] < jnp.arange(HEAD_DIM, dtype=jnp.int32)[None, :]).astype(F32), axis=0
    ).astype(BF16)
    own = jnp.concatenate([k_cache, v_cache, jnp.broadcast_to(smaller[None, :], (16, HEAD_DIM))], axis=0)[None]

    z_1 = move(own, lambda y, z, c: (y, z + 1, c))
    z_3 = move(own, lambda y, z, c: (y, z - 1, c))
    z_2 = move(own, lambda y, z, c: (y, z + 2, c))
    y_1 = up_y(own)
    y_3 = round_y(own)
    y_2 = move(own, lambda y, z, c: (y + 2, z, c) if y < 2 else None)

    widened = hidden.astype(F32)
    normed = (widened * lax.rsqrt(jnp.mean(widened * widened, axis=-1, keepdims=True) + 1e-06)).astype(BF16)
    q_t = (
        lax.dot_general(w_query, normed, (((0,), (1,)), ((), ())), preferred_element_type=F32) * HEAD_DIM ** (-0.5)
    ).astype(BF16)
    hot = (jnp.arange(HEAD_DIM, dtype=jnp.int32)[:, None] == segment[None, :]).astype(BF16)

    far_1 = move(y_2, lambda y, z, c: (y, z + 1, c) if y >= 2 else None)
    far_3 = move(y_2, lambda y, z, c: (y, z - 1, c) if y >= 2 else None)
    far_2 = move(y_2, lambda y, z, c: (y, z + 2, c) if y >= 2 else None)
    row = jnp.concatenate([z_1, z_3, z_2], axis=0)
    up = up_y(row)
    around = round_y(row)
    mine = jnp.concatenate([row, y_1, y_3, y_2], axis=0)
    theirs = swap_cores(jnp.concatenate([own, mine], axis=0))

    at = jnp.stack([ctx, lax.axis_index("section")]).astype(jnp.int32)
    state = pl.pallas_call(
        start_kernel,
        out_shape=CARRY,
        in_specs=[SMEM] + [VMEM] * 5,
        out_specs=(VMEM,) * 3,
        scratch_shapes=[pltpu.SMEM((16,), jnp.int32)],
        compiler_params=LIMIT,
        cost_estimate=cost(1),
        name="attend_first",
    )(at, own, mine, theirs, q_t, hot)

    pieces, state = lax.optimization_barrier(((up, around, far_1, far_3, far_2), state))
    got = jnp.concatenate(pieces, axis=0)
    got_2 = swap_cores(got)
    state = pl.pallas_call(
        more_kernel,
        out_shape=CARRY,
        in_specs=[SMEM] + [VMEM] * 6,
        out_specs=(VMEM,) * 3,
        scratch_shapes=[pltpu.SMEM((16,), jnp.int32)],
        compiler_params=LIMIT,
        cost_estimate=cost(9),
        name="attend_later",
    )(at, got, q_t, hot, *state)

    part = lambda n: jax.ShapeDtypeStruct((n, HALF, COLS), BF16)
    attended = jax.ShapeDtypeStruct((HALF, 4 * HEAD_DIM), BF16)
    w_at = pl.BlockSpec(memory_space=pltpu.HBM)

    def finish(half, places):
        return pl.pallas_call(
            functools.partial(finish_kernel, half, places),
            out_shape=(attended,) + tuple(part(len(p)) for p in places),
            in_specs=[SMEM] + [VMEM] * 6 + [w_at],
            out_specs=(VMEM,) * (1 + len(places)),
            scratch_shapes=[
                pltpu.VMEM((8, BLOCK), F32),
                pltpu.VMEM((8, BLOCK), F32),
                pltpu.VMEM((4 * HEAD_DIM, BLOCK), F32),
                pltpu.VMEM(w_out.shape, BF16),
                pltpu.SMEM((16,), jnp.int32),
                pltpu.SemaphoreType.DMA,
            ],
            compiler_params=WHOLE,
            cost_estimate=cost(6),
            name=f"attend_and_project_{half}",
        )(at, got_2, q_t, hot, *state, w_out)

    att_b, b1 = finish(1, [[(1, dx) for dx in range(4)]])
    att_a, a1, a3, a2 = finish(0, [[(0, dx), (1, dx)] for dx in (1, 3, 2)])
    a0, b0 = pl.pallas_call(
        own_kernel,
        out_shape=(part(2), part(4)),
        in_specs=[SMEM, VMEM, VMEM, w_at],
        out_specs=(VMEM,) * 2,
        scratch_shapes=[pltpu.VMEM(w_out.shape, BF16), pltpu.SemaphoreType.DMA],
        compiler_params=WHOLE,
        cost_estimate=cost(4),
        name="project_own",
    )(at, att_a, att_b, w_out)

    def send_x(t, k):
        return lax.ppermute(t, "section", [(g * 4 + x, g * 4 + (x + k) % 4) for g in range(2) for x in range(4)])

    def send_z(t):
        return lax.ppermute(t, "section", [(g * 4 + x, (1 - g) * 4 + x) for g in range(2) for x in range(4)])

    b_in = send_z(b1)
    a_in = [send_x(a, k) for a, k in ((a1, 1), (a3, 3), (a2, 2))]
    b_sum = b0.astype(F32) + b_in.astype(F32)
    a_in = list(a_in)
    b_sum, a_in[0] = lax.optimization_barrier((b_sum, a_in[0]))
    b_out = [send_x(b_sum[k].astype(BF16), k) for k in (1, 3, 2)]
    a_sum = a0.astype(F32) + a_in[0].astype(F32) + a_in[1].astype(F32) + a_in[2].astype(F32)
    a_out = send_z(a_sum[1].astype(BF16))
    a = a_sum[0] + a_out.astype(F32)
    b = b_sum[0] + b_out[0].astype(F32) + b_out[1].astype(F32) + b_out[2].astype(F32)
    return jnp.concatenate([a, b], axis=0).astype(BF16)


def solution(mesh):
    return jax.shard_map(
        per_device,
        mesh=mesh,
        in_specs=(
            P("ctx", None),
            P("ctx", "section"),
            P("ctx", "section"),
            P("ctx"),
            P(None, "section"),
            P("section", None),
        ),
        out_specs=P("ctx", "section"),
        check_vma=False,
    )
```

```python
import functools

import jax
import jax.numpy as jnp
from jax import lax
from jax.experimental import pallas as pl
from jax.experimental.pallas import tpu as pltpu
from jax.sharding import PartitionSpec as P
import numpy as np

HEAD_DIM = 128
BLOCK = 256
PACK = 2 * BLOCK + 16
REACH = 24
HALF = BLOCK // 2
COLS = 640
FLOOR = -1e30
HIDDEN = -2e30

F32 = jnp.float32
BF16 = jnp.bfloat16


def ctx_id(y, z, c):
    return ((y + 8) % 4) * 8 + ((z + 8) % 4) * 2 + c


def ctx_pairs(step, planes=None):
    pairs = []
    for y in range(4):
        for z in range(4):
            for c in range(2):
                to = step(y, z, c)
                if to is not None:
                    pairs.append((ctx_id(y, z, c), ctx_id(*to)))
    return pairs


def move(x, step):
    return lax.ppermute(x, "ctx", ctx_pairs(step))


def swap_cores(x):
    return move(x, lambda y, z, c: (y, z, 1 - c))


def along_z(x, first_plane=0):
    def step(y, z, c):
        return (y, z + 1 if c == 0 else z - 1, c) if y >= first_plane else None

    return move(x, step)


def along_y(x):
    def step(y, z, c):
        if c == 0:
            return (y + 1, z, c) if y < 3 else None
        return (3, z, c) if y == 0 else None

    return move(x, step)


def up_y(x):
    return move(x, lambda y, z, c: (y + 1, z, c) if y < 3 else None)


def round_y(x):
    return move(x, lambda y, z, c: (3, z, c) if y == 0 else None)


def first_slots(y, z, c):
    d = 2 * c - 1
    return [[(y, z + d, c), (y, z + d, 1 - c)], [(y, z + 2, c)], [(y + d, z, c), (y + d, z, 1 - c)]]


def far_slots(y, z, c):
    d = 2 * c - 1
    return [[(y + 2, z, c)], [(y + 2, z + d, c), (y + 2, z + d, 1 - c)], [(y + 2, z + 2, c)]]


def later_slots(y, z, c):
    d = 2 * c - 1
    return [[(y + e, z + d, c), (y + e, z + d, 1 - c), (y + e, z + 2, c)] for e in (-1, 1)]


def attend_blocks(kv_ref, places, diagonal, q_ref, hot_ref, m_ref, l_ref, acc_ref):
    heads = [slice(h * HEAD_DIM, (h + 1) * HEAD_DIM) for h in range(4)]
    keys, values, visible = [], [], []
    for at, low in places:
        keys.append(kv_ref[at, 0:BLOCK, :])
        values.append(jnp.transpose(kv_ref[at, BLOCK : 2 * BLOCK, :]))
        counts = kv_ref[at, 2 * BLOCK : PACK, :]
        first = jnp.dot(counts, hot_ref[...], preferred_element_type=F32)[0:1, :].astype(jnp.int32)
        row = lax.broadcasted_iota(jnp.int32, (BLOCK, BLOCK), 0)
        seen = row >= jnp.maximum(first, low)
        if diagonal:
            seen &= row <= lax.broadcasted_iota(jnp.int32, (BLOCK, BLOCK), 1)
        visible.append(seen)
    scores = [[jnp.dot(k, q_ref[rows, :], preferred_element_type=F32) for k in keys] for rows in heads]
    old = [(m_ref[h : h + 1, :], l_ref[h : h + 1, :]) for h in range(4)]
    new = []
    for h in range(4):
        masked = [jnp.where(seen, s, HIDDEN) for seen, s in zip(visible, scores[h])]
        m_old, total = old[h]
        m_new = m_old
        for s in masked:
            m_new = jnp.maximum(m_new, jnp.max(s, axis=0, keepdims=True))
        weights = [jnp.exp(s - m_new) for s in masked]
        fade = jnp.exp(m_old - m_new)
        total = fade * total
        for p in weights:
            total = total + jnp.sum(p, axis=0, keepdims=True)
        added = sum(jnp.dot(v, p.astype(BF16), preferred_element_type=F32) for v, p in zip(values, weights))
        new.append((m_new, total, fade, added))
    for h, rows in enumerate(heads):
        m_new, total, fade, added = new[h]
        m_ref[h : h + 1, :] = m_new
        l_ref[h : h + 1, :] = total
        acc_ref[rows, :] = fade * acc_ref[rows, :] + added


def attend_pieces(at_ref, slots, piece_refs, all_ref, order_ref, *refs):
    own, y, z, c = where_am_i(at_ref)
    places = slots(y, z, c)
    count = jnp.int32(0)
    n = 0
    for piece_ref, places_of in zip(piece_refs, places):
        for i, place in enumerate(places_of):
            block = ctx_id(*place)
            all_ref[n] = piece_ref[i]
            order_ref[count] = n
            count += ((block < own) & (block >= own - REACH)).astype(jnp.int32)
            n += 1

    @pl.loop(0, (count + 1) // 2)
    def _(g):
        one = order_ref[2 * g]
        both = 2 * g + 1 < count
        two = jnp.where(both, order_ref[2 * g + 1], one)
        attend_blocks(all_ref, [(one, 0), (two, jnp.where(both, 0, BLOCK))], False, *refs)


def where_am_i(at_ref):
    own = at_ref[0]
    return own, own // 8, (own // 2) % 4, own % 2


def start_kernel(slots, n, at_ref, own_ref, *rest):
    pieces, (q_ref, hot_ref, m_ref, l_ref, acc_ref, all_ref, order_ref) = rest[:n], rest[n:]
    m_ref[...] = jnp.full_like(m_ref, FLOOR)
    l_ref[...] = jnp.zeros_like(l_ref)
    acc_ref[...] = jnp.zeros_like(acc_ref)
    refs = (q_ref, hot_ref, m_ref, l_ref, acc_ref)
    attend_blocks(own_ref, [(0, 0)], True, *refs)
    attend_pieces(at_ref, slots, pieces, all_ref, order_ref, *refs)


def more_kernel(slots, n, at_ref, *rest):
    pieces, (q_ref, hot_ref, m_in, l_in, acc_in, m_ref, l_ref, acc_ref, all_ref, order_ref) = rest[:n], rest[n:]
    m_ref[...] = m_in[...]
    l_ref[...] = l_in[...]
    acc_ref[...] = acc_in[...]
    attend_pieces(at_ref, slots, pieces, all_ref, order_ref, q_ref, hot_ref, m_ref, l_ref, acc_ref)


def last_kernel(slots, n, at_ref, *rest):
    pieces, (q_ref, hot_ref, m_in, l_in, acc_in, w_ref, b1, b0, a1, a3, a2, a0) = rest[:n], rest[n : n + 12]
    m_ref, l_ref, acc_ref, all_ref, order_ref, att_ref = rest[n + 12 :]
    m_ref[...] = m_in[...]
    l_ref[...] = l_in[...]
    acc_ref[...] = acc_in[...]
    attend_pieces(at_ref, slots, pieces, all_ref, order_ref, q_ref, hot_ref, m_ref, l_ref, acc_ref)
    for h in range(4):
        rows = slice(h * HEAD_DIM, (h + 1) * HEAD_DIM)
        att_ref[:, rows] = jnp.transpose(acc_ref[rows, :] / l_ref[h : h + 1, :]).astype(BF16)
    b_to, a_to = (b0, b1), (a0, a1, a2, a3)
    section = at_ref[1]
    for dz in range(2):
        for dx in range(4):
            to = (section // 4 + dz) % 2 * 4 + (section + dx) % 4
            cols = pl.ds(pl.multiple_of(to * COLS, 128), COLS)
            part = jnp.dot(att_ref[...], w_ref[:, cols], preferred_element_type=F32).astype(BF16)
            a_to[dx][dz] = part[:HALF]
            b_to[dz][dx] = part[HALF:]


def fetch_kernel(from_ref, to_ref, sem):
    copy = pltpu.make_async_copy(from_ref, to_ref, sem)
    copy.start()
    copy.wait()


VMEM = pl.BlockSpec(memory_space=pltpu.VMEM)
SMEM = pl.BlockSpec(memory_space=pltpu.SMEM)
CARRY = (
    jax.ShapeDtypeStruct((8, BLOCK), F32),
    jax.ShapeDtypeStruct((8, BLOCK), F32),
    jax.ShapeDtypeStruct((4 * HEAD_DIM, BLOCK), F32),
)
LIMIT = pltpu.CompilerParams(vmem_limit_bytes=24 * 1024 * 1024)


def cost(n):
    return pl.CostEstimate(
        flops=n * 4 * 4 * BLOCK * BLOCK * HEAD_DIM,
        bytes_accessed=n * PACK * HEAD_DIM * 2,
        transcendentals=n * 4 * BLOCK * BLOCK,
    )


def per_device(hidden, k_cache, v_cache, segment, w_query, w_out):
    ctx = lax.axis_index("ctx")

    smaller = jnp.sum(
        (segment[:, None] < jnp.arange(HEAD_DIM, dtype=jnp.int32)[None, :]).astype(F32), axis=0
    ).astype(BF16)
    own = jnp.concatenate([k_cache, v_cache, jnp.broadcast_to(smaller[None, :], (16, HEAD_DIM))], axis=0)[None]

    y_far = move(own, lambda y, z, c: (y + 2, z, c) if y < 2 else None)
    other = swap_cores(own)
    pair = jnp.concatenate([own, other], axis=0)
    z_near = along_z(pair)
    y_near = along_y(pair)
    z_far = along_z(z_near[:1])

    widened = hidden.astype(F32)
    normed = (widened * lax.rsqrt(jnp.mean(widened * widened, axis=-1, keepdims=True) + 1e-06)).astype(BF16)
    q_t = (
        lax.dot_general(w_query, normed, (((0,), (1,)), ((), ())), preferred_element_type=F32) * HEAD_DIM ** (-0.5)
    ).astype(BF16)
    hot = (jnp.arange(HEAD_DIM, dtype=jnp.int32)[:, None] == segment[None, :]).astype(BF16)
    w_held = pl.pallas_call(
        fetch_kernel,
        out_shape=jax.ShapeDtypeStruct(w_out.shape, w_out.dtype),
        in_specs=[pl.BlockSpec(memory_space=pltpu.HBM)],
        out_specs=VMEM,
        scratch_shapes=[pltpu.SemaphoreType.DMA],
        compiler_params=LIMIT,
        name="fetch_w_out",
    )(w_out)
    q_t, w_held = lax.optimization_barrier((q_t, w_held))

    row = jnp.concatenate([z_near, z_far], axis=0)
    up = up_y(row)
    around = round_y(row)
    far_other = swap_cores(y_far)
    far_pair, _ = lax.optimization_barrier((jnp.concatenate([y_far, far_other], axis=0), z_far))
    far_near = along_z(far_pair, 2)

    at = jnp.stack([ctx, lax.axis_index("section")]).astype(jnp.int32)

    def scratch(n):
        return [pltpu.VMEM((n, PACK, HEAD_DIM), BF16), pltpu.SMEM((16,), jnp.int32)]

    def attend(kernel, slots, n, pieces, state, name):
        return pl.pallas_call(
            functools.partial(kernel, slots, len(pieces) - (not state)),
            out_shape=CARRY,
            in_specs=[SMEM] + [VMEM] * (len(pieces) + 2 + len(state)),
            out_specs=(VMEM,) * 3,
            scratch_shapes=scratch(n),
            compiler_params=LIMIT,
            cost_estimate=cost(1),
            name=name,
        )(at, *pieces, q_t, hot, *state)

    def slots_1(y, z, c):
        mine, theirs = first_slots(y, z, c), first_slots(y, z, 1 - c)
        return [[(y, z, 1 - c)]] + mine + theirs + far_slots(y, z, c)[:1] + far_slots(y, z, 1 - c)[:1]

    def slots_2(y, z, c):
        return later_slots(y, z, c) + far_slots(y, z, c)[1:2] + far_slots(y, z, 1 - c)[1:2]

    def slots_3(y, z, c):
        return later_slots(y, z, 1 - c)

    def slots_4(y, z, c):
        return far_slots(y, z, c)[2:] + far_slots(y, z, 1 - c)[2:]

    firsts = [z_near, z_far, y_near]
    pieces = [own, other] + firsts + [swap_cores(t) for t in firsts] + [y_far, far_other]
    state = attend(start_kernel, slots_1, 13, pieces, (), "attend_first")

    far_near, state = lax.optimization_barrier((far_near, state))
    far_far = along_z(far_near[:1], 2)
    far_near_other = swap_cores(far_near)
    (up, around), state = lax.optimization_barrier(((up, around), state))
    up_other, around_other = swap_cores(up), swap_cores(around)
    state = attend(more_kernel, slots_2, 10, [up, around, far_near, far_near_other], state, "attend_next")
    far_far, state = lax.optimization_barrier((far_far, state))
    far_far_other = swap_cores(far_far)
    state = attend(more_kernel, slots_3, 6, [up_other, around_other], state, "attend_third")

    part = lambda n: jax.ShapeDtypeStruct((n, HALF, COLS), BF16)
    b1, b0, a1, a3, a2, a0 = pl.pallas_call(
        functools.partial(last_kernel, slots_4, 2),
        out_shape=(part(4), part(4), part(2), part(2), part(2), part(2)),
        in_specs=[SMEM] + [VMEM] * 8,
        out_specs=(VMEM,) * 6,
        scratch_shapes=[
            pltpu.VMEM((8, BLOCK), F32),
            pltpu.VMEM((8, BLOCK), F32),
            pltpu.VMEM((4 * HEAD_DIM, BLOCK), F32),
            *scratch(2),
            pltpu.VMEM((BLOCK, 4 * HEAD_DIM), BF16),
        ],
        compiler_params=LIMIT,
        cost_estimate=cost(12),
        name="attend_and_project",
    )(at, far_far, far_far_other, q_t, hot, *state, w_held)

    def send_x(t, k):
        return lax.ppermute(t, "section", [(g * 4 + x, g * 4 + (x + k) % 4) for g in range(2) for x in range(4)])

    def send_z(t):
        return lax.ppermute(t, "section", [(g * 4 + x, (1 - g) * 4 + x) for g in range(2) for x in range(4)])

    b_in = send_z(b1)
    a_in = [send_x(a, k) for a, k in ((a1, 1), (a3, 3), (a2, 2))]
    b_sum = b0.astype(F32) + b_in.astype(F32)
    b_out = [send_x(b_sum[k].astype(BF16), k) for k in (1, 3, 2)]
    a_in[0], b_out[0] = lax.optimization_barrier((a_in[0], b_out[0]))
    a_sum = a0.astype(F32) + a_in[0].astype(F32) + a_in[1].astype(F32) + a_in[2].astype(F32)
    a_out = send_z(a_sum[1].astype(BF16))
    a = a_sum[0] + a_out.astype(F32)
    b = b_sum[0] + b_out[0].astype(F32) + b_out[1].astype(F32) + b_out[2].astype(F32)
    return jnp.concatenate([a, b], axis=0).astype(BF16)


def solution(mesh):
    return jax.shard_map(
        per_device,
        mesh=mesh,
        in_specs=(
            P("ctx", None),
            P("ctx", "section"),
            P("ctx", "section"),
            P("ctx"),
            P(None, "section"),
            P("section", None),
        ),
        out_specs=P("ctx", "section"),
        check_vma=False,
    )
```

```python
import functools
import itertools

import jax
import jax.numpy as jnp
from jax import lax
from jax.experimental import pallas as pl
from jax.experimental.pallas import tpu as pltpu
from jax.sharding import PartitionSpec as P
import numpy as np

HEAD_DIM = 128
BLOCK = 256
PACK = 2 * BLOCK + 16
CHAINS = ((slice(0, 96), (1, 3, 4)), (slice(96, 176), (3, 4, 1)), (slice(176, 256), (4, 1, 3)))
REACH = 24
COLS = 640
FLOOR = -1e30
HIDDEN = -2e30

F32 = jnp.float32
BF16 = jnp.bfloat16


def ctx_id(y, z, c):
    return ((y + 8) % 4) * 8 + ((z + 8) % 4) * 2 + c


def ctx_pairs(step, planes=None):
    pairs = []
    for y in range(4):
        for z in range(4):
            for c in range(2):
                to = step(y, z, c)
                if to is not None:
                    pairs.append((ctx_id(y, z, c), ctx_id(*to)))
    return pairs


def move(x, step):
    return lax.ppermute(x, "ctx", ctx_pairs(step))


def swap_cores(x):
    return move(x, lambda y, z, c: (y, z, 1 - c))


def along_z(x, first_plane=0):
    def step(y, z, c):
        return (y, z + 1 if c == 0 else z - 1, c) if y >= first_plane else None

    return move(x, step)


def along_y(x):
    def step(y, z, c):
        if c == 0:
            return (y + 1, z, c) if y < 3 else None
        return (3, z, c) if y == 0 else None

    return move(x, step)


def up_y(x):
    return move(x, lambda y, z, c: (y + 1, z, c) if y < 3 else None)


def round_y(x):
    return move(x, lambda y, z, c: (3, z, c) if y == 0 else None)


def first_slots(y, z, c):
    d = 2 * c - 1
    return [[(y, z + d, c), (y, z + d, 1 - c)], [(y, z + 2, c)], [(y + d, z, c), (y + d, z, 1 - c)]]


def far_slots(y, z, c):
    d = 2 * c - 1
    return [[(y + 2, z, c)], [(y + 2, z + d, c), (y + 2, z + d, 1 - c)], [(y + 2, z + 2, c)]]


def next_slots(y, z, c):
    d = 2 * c - 1
    near = [[(y + e, z + d, c), (y + e, z + d, 1 - c)] for e in (-1, 1)]
    return near + [[(y + e, z + 2, c)] for e in (-1, 1)]


def attend_blocks(kv_ref, places, diagonal, q_ref, hot_ref, m_ref, l_ref, acc_ref):
    heads = [slice(h * HEAD_DIM, (h + 1) * HEAD_DIM) for h in range(4)]
    keys, values, visible = [], [], []
    for at, low in places:
        keys.append(kv_ref[at, 0:BLOCK, :])
        values.append(jnp.transpose(kv_ref[at, BLOCK : 2 * BLOCK, :]))
        counts = kv_ref[at, 2 * BLOCK : PACK, :]
        first = jnp.dot(counts, hot_ref[...], preferred_element_type=F32)[0:1, :].astype(jnp.int32)
        row = lax.broadcasted_iota(jnp.int32, (BLOCK, BLOCK), 0)
        seen = row >= jnp.maximum(first, low)
        if diagonal:
            seen &= row <= lax.broadcasted_iota(jnp.int32, (BLOCK, BLOCK), 1)
        visible.append(seen)
    scores = [[jnp.dot(k, q_ref[rows, :], preferred_element_type=F32) for k in keys] for rows in heads]
    old = [(m_ref[h : h + 1, :], l_ref[h : h + 1, :]) for h in range(4)]
    new = []
    for h in range(4):
        masked = [jnp.where(seen, s, HIDDEN) for seen, s in zip(visible, scores[h])]
        m_old, total = old[h]
        m_new = m_old
        for s in masked:
            m_new = jnp.maximum(m_new, jnp.max(s, axis=0, keepdims=True))
        weights = [jnp.exp(s - m_new) for s in masked]
        fade = jnp.exp(m_old - m_new)
        total = fade * total
        for p in weights:
            total = total + jnp.sum(p, axis=0, keepdims=True)
        added = sum(jnp.dot(v, p.astype(BF16), preferred_element_type=F32) for v, p in zip(values, weights))
        new.append((m_new, total, fade, added))
    for h, rows in enumerate(heads):
        m_new, total, fade, added = new[h]
        m_ref[h : h + 1, :] = m_new
        l_ref[h : h + 1, :] = total
        acc_ref[rows, :] = fade * acc_ref[rows, :] + added


def attend_pieces(at_ref, slots, piece_refs, all_ref, order_ref, *refs):
    own, y, z, c = where_am_i(at_ref)
    places = slots(y, z, c)
    count = jnp.int32(0)
    n = 0
    for piece_ref, places_of in zip(piece_refs, places):
        for i, place in enumerate(places_of):
            block = ctx_id(*place)
            all_ref[n] = piece_ref[i]
            order_ref[count] = n
            count += ((block < own) & (block >= own - REACH)).astype(jnp.int32)
            n += 1

    @pl.loop(0, (count + 1) // 2)
    def _(g):
        one = order_ref[2 * g]
        both = 2 * g + 1 < count
        two = jnp.where(both, order_ref[2 * g + 1], one)
        attend_blocks(all_ref, [(one, 0), (two, jnp.where(both, 0, BLOCK))], False, *refs)


def where_am_i(at_ref):
    own = at_ref[0]
    return own, own // 8, (own // 2) % 4, own % 2


def start_kernel(slots, n, at_ref, own_ref, *rest):
    pieces, (q_ref, hot_ref, m_ref, l_ref, acc_ref, all_ref, order_ref) = rest[:n], rest[n:]
    m_ref[...] = jnp.full_like(m_ref, FLOOR)
    l_ref[...] = jnp.zeros_like(l_ref)
    acc_ref[...] = jnp.zeros_like(acc_ref)
    refs = (q_ref, hot_ref, m_ref, l_ref, acc_ref)
    attend_blocks(own_ref, [(0, 0)], True, *refs)
    attend_pieces(at_ref, slots, pieces, all_ref, order_ref, *refs)


def more_kernel(slots, n, at_ref, *rest):
    pieces, (q_ref, hot_ref, m_in, l_in, acc_in, m_ref, l_ref, acc_ref, all_ref, order_ref) = rest[:n], rest[n:]
    m_ref[...] = m_in[...]
    l_ref[...] = l_in[...]
    acc_ref[...] = acc_in[...]
    attend_pieces(at_ref, slots, pieces, all_ref, order_ref, q_ref, hot_ref, m_ref, l_ref, acc_ref)


def last_kernel(slots, n, at_ref, *rest):
    pieces, (q_ref, hot_ref, m_in, l_in, acc_in, w_ref), outs = rest[:n], rest[n : n + 6], rest[n + 6 : n + 12]
    m_ref, l_ref, acc_ref, all_ref, order_ref, att_ref = rest[n + 12 :]
    m_ref[...] = m_in[...]
    l_ref[...] = l_in[...]
    acc_ref[...] = acc_in[...]
    attend_pieces(at_ref, slots, pieces, all_ref, order_ref, q_ref, hot_ref, m_ref, l_ref, acc_ref)
    for h in range(4):
        rows = slice(h * HEAD_DIM, (h + 1) * HEAD_DIM)
        att_ref[:, rows] = jnp.transpose(acc_ref[rows, :] / l_ref[h : h + 1, :]).astype(BF16)
    section = at_ref[1]
    for sides in itertools.product((0, 1), repeat=3):
        away = 0
        for step, side in zip(CHAINS[0][1], sides):
            away ^= step * side
        cols = pl.ds(pl.multiple_of((section ^ away) * COLS, 128), COLS)
        part = jnp.dot(att_ref[...], w_ref[:, cols], preferred_element_type=F32).astype(BF16)
        crossed = dict(zip(CHAINS[0][1], sides))
        for i, (rows, order) in enumerate(CHAINS):
            first, second, third = (crossed[step] for step in order)
            outs[2 * i + 1 - first][2 * second + third] = part[rows]


VMEM = pl.BlockSpec(memory_space=pltpu.VMEM)
SMEM = pl.BlockSpec(memory_space=pltpu.SMEM)
CARRY = (
    jax.ShapeDtypeStruct((8, BLOCK), F32),
    jax.ShapeDtypeStruct((8, BLOCK), F32),
    jax.ShapeDtypeStruct((4 * HEAD_DIM, BLOCK), F32),
)
LIMIT = pltpu.CompilerParams(vmem_limit_bytes=24 * 1024 * 1024)


def cost(n):
    return pl.CostEstimate(
        flops=n * 4 * 4 * BLOCK * BLOCK * HEAD_DIM,
        bytes_accessed=n * PACK * HEAD_DIM * 2,
        transcendentals=n * 4 * BLOCK * BLOCK,
    )


def per_device(hidden, k_cache, v_cache, segment, w_query, w_out):
    ctx = lax.axis_index("ctx")

    smaller = jnp.sum(
        (segment[:, None] < jnp.arange(HEAD_DIM, dtype=jnp.int32)[None, :]).astype(F32), axis=0
    ).astype(BF16)
    own = jnp.concatenate([k_cache, v_cache, jnp.broadcast_to(smaller[None, :], (16, HEAD_DIM))], axis=0)[None]

    y_far = move(own, lambda y, z, c: (y + 2, z, c) if y < 2 else None)
    other = swap_cores(own)
    pair = jnp.concatenate([own, other], axis=0)
    z_near = along_z(pair)
    y_near = along_y(pair)
    far_other = swap_cores(y_far)

    widened = hidden.astype(F32)
    normed = (widened * lax.rsqrt(jnp.mean(widened * widened, axis=-1, keepdims=True) + 1e-06)).astype(BF16)
    q_t = (
        lax.dot_general(w_query, normed, (((0,), (1,)), ((), ())), preferred_element_type=F32) * HEAD_DIM ** (-0.5)
    ).astype(BF16)
    hot = (jnp.arange(HEAD_DIM, dtype=jnp.int32)[:, None] == segment[None, :]).astype(BF16)

    (z_near, y_near, far_other), q_t = lax.optimization_barrier(((z_near, y_near, far_other), q_t))
    z_far = along_z(z_near[:1])
    up_near = up_y(z_near)
    around_near = round_y(z_near)

    up_far = up_y(z_far)
    around_far = round_y(z_far)
    far_pair, _ = lax.optimization_barrier((jnp.concatenate([y_far, far_other], axis=0), z_far))
    far_near = along_z(far_pair, 2)

    at = jnp.stack([ctx, lax.axis_index("section")]).astype(jnp.int32)

    def scratch(n):
        return [pltpu.VMEM((n, PACK, HEAD_DIM), BF16), pltpu.SMEM((16,), jnp.int32)]

    def attend(kernel, slots, n, pieces, state, name):
        return pl.pallas_call(
            functools.partial(kernel, slots, len(pieces) - (not state)),
            out_shape=CARRY,
            in_specs=[SMEM] + [VMEM] * (len(pieces) + 2 + len(state)),
            out_specs=(VMEM,) * 3,
            scratch_shapes=scratch(n),
            compiler_params=LIMIT,
            cost_estimate=cost(1),
            name=name,
        )(at, *pieces, q_t, hot, *state)

    def slots_1(y, z, c):
        mine, theirs = first_slots(y, z, c), first_slots(y, z, 1 - c)
        return [[(y, z, 1 - c)]] + mine + theirs + far_slots(y, z, c)[:1] + far_slots(y, z, 1 - c)[:1]

    def slots_2(y, z, c):
        return next_slots(y, z, c) + far_slots(y, z, c)[1:2] + far_slots(y, z, 1 - c)[1:2]

    def slots_3(y, z, c):
        return next_slots(y, z, 1 - c)

    def slots_4(y, z, c):
        return far_slots(y, z, c)[2:] + far_slots(y, z, 1 - c)[2:]

    firsts = [z_near, z_far, y_near]
    pieces = [own, other] + firsts + [swap_cores(t) for t in firsts] + [y_far, far_other]
    state = attend(start_kernel, slots_1, 13, pieces, (), "attend_first")

    far_near, state = lax.optimization_barrier((far_near, state))
    far_far = along_z(far_near[:1], 2)
    far_near_other = swap_cores(far_near)
    nexts = (up_near, around_near, up_far, around_far)
    nexts, state = lax.optimization_barrier((nexts, state))
    others = [swap_cores(t) for t in nexts]
    state = attend(more_kernel, slots_2, 10, [*nexts, far_near, far_near_other], state, "attend_next")
    far_far, state = lax.optimization_barrier((far_far, state))
    far_far_other = swap_cores(far_far)
    state = attend(more_kernel, slots_3, 6, others, state, "attend_third")

    out_shape = []
    for rows, _ in CHAINS:
        out_shape += [jax.ShapeDtypeStruct((4, rows.stop - rows.start, COLS), BF16)] * 2
    outs = pl.pallas_call(
        functools.partial(last_kernel, slots_4, 2),
        out_shape=tuple(out_shape),
        in_specs=[SMEM] + [VMEM] * 8,
        out_specs=(VMEM,) * 6,
        scratch_shapes=[
            pltpu.VMEM((8, BLOCK), F32),
            pltpu.VMEM((8, BLOCK), F32),
            pltpu.VMEM((4 * HEAD_DIM, BLOCK), F32),
            *scratch(2),
            pltpu.VMEM((BLOCK, 4 * HEAD_DIM), BF16),
        ],
        compiler_params=LIMIT,
        cost_estimate=cost(12),
        name="attend_and_project",
    )(at, far_far, far_far_other, q_t, hot, *state, w_out)

    def exchange(x, step):
        return lax.ppermute(x, "section", [(i, i ^ step) for i in range(8)])

    mixed = []
    for i, (_, (first, second, third)) in enumerate(CHAINS):
        sent, kept = outs[2 * i], outs[2 * i + 1]
        four = kept.astype(F32) + exchange(sent, first).astype(F32)
        two = four[:2] + exchange(four[2:].astype(BF16), second).astype(F32)
        mixed.append(two[0] + exchange(two[1].astype(BF16), third).astype(F32))
    return jnp.concatenate(mixed, axis=0).astype(BF16)


def solution(mesh):
    return jax.shard_map(
        per_device,
        mesh=mesh,
        in_specs=(
            P("ctx", None),
            P("ctx", "section"),
            P("ctx", "section"),
            P("ctx"),
            P(None, "section"),
            P("section", None),
        ),
        out_specs=P("ctx", "section"),
        check_vma=False,
    )
```

```python
import functools
import itertools

import jax
import jax.numpy as jnp
from jax import lax
from jax.experimental import pallas as pl
from jax.experimental.pallas import tpu as pltpu
from jax.sharding import PartitionSpec as P
import numpy as np

HEAD_DIM = 128
BLOCK = 256
PACK = 2 * BLOCK + 16
CHAINS = ((slice(0, 96), (1, 3, 4)), (slice(96, 176), (3, 4, 1)), (slice(176, 256), (4, 1, 3)))
REACH = 24
COLS = 640
TOP, SUM = 4 * HEAD_DIM, 4 * HEAD_DIM + 8
HOT = slice(4 * HEAD_DIM, 5 * HEAD_DIM)
FLOOR = -1e30
HIDDEN = -2e30

F32 = jnp.float32
BF16 = jnp.bfloat16


def ctx_id(y, z, c):
    return ((y + 8) % 4) * 8 + ((z + 8) % 4) * 2 + c


def ctx_pairs(step, planes=None):
    pairs = []
    for y in range(4):
        for z in range(4):
            for c in range(2):
                to = step(y, z, c)
                if to is not None:
                    pairs.append((ctx_id(y, z, c), ctx_id(*to)))
    return pairs


def move(x, step):
    return lax.ppermute(x, "ctx", ctx_pairs(step))


def swap_cores(x):
    return move(x, lambda y, z, c: (y, z, 1 - c))


def along_z(x, first_plane=0):
    def step(y, z, c):
        return (y, z + 1 if c == 0 else z - 1, c) if y >= first_plane else None

    return move(x, step)


def along_y(x):
    def step(y, z, c):
        if c == 0:
            return (y + 1, z, c) if y < 3 else None
        return (3, z, c) if y == 0 else None

    return move(x, step)


def up_y(x):
    return move(x, lambda y, z, c: (y + 1, z, c) if y < 3 else None)


def round_y(x):
    return move(x, lambda y, z, c: (3, z, c) if y == 0 else None)


def first_slots(y, z, c):
    d = 2 * c - 1
    row = [[(y, z, c)], [(y, z + d, c), (y, z + d, 1 - c)], [(y, z + 2, c)]]
    return row + [[(y + d, z, c), (y + d, z, 1 - c)], [(y + 2, z, c)]]


def next_slots(y, z, c):
    d = 2 * c - 1
    near = [[(y + e, z + d, c), (y + e, z + d, 1 - c)] for e in (-1, 1)]
    return near + [[(y + e, z + 2, c)] for e in (-1, 1)]


def far_slots(y, z, c):
    d = 2 * c - 1
    return [[(y + 2, z + d, c), (y + 2, z + d, 1 - c)], [(y + 2, z + 2, c)]]


def attend_blocks(kv_ref, places, diagonal, q_ref, state_ref):
    heads = [slice(h * HEAD_DIM, (h + 1) * HEAD_DIM) for h in range(4)]
    keys, values, visible = [], [], []
    for at, low in places:
        keys.append(kv_ref[at, 0:BLOCK, :])
        values.append(jnp.transpose(kv_ref[at, BLOCK : 2 * BLOCK, :]))
        counts = kv_ref[at, 2 * BLOCK : PACK, :]
        first = jnp.dot(counts, q_ref[HOT, :], preferred_element_type=F32)[0:1, :].astype(jnp.int32)
        row = lax.broadcasted_iota(jnp.int32, (BLOCK, BLOCK), 0)
        seen = row >= jnp.maximum(first, low)
        if diagonal:
            seen &= row <= lax.broadcasted_iota(jnp.int32, (BLOCK, BLOCK), 1)
        visible.append(seen)
    scores = [[jnp.dot(k, q_ref[rows, :], preferred_element_type=F32) for k in keys] for rows in heads]
    old = [(state_ref[TOP + h : TOP + h + 1, :], state_ref[SUM + h : SUM + h + 1, :]) for h in range(4)]
    new = []
    for h in range(4):
        masked = [jnp.where(seen, s, HIDDEN) for seen, s in zip(visible, scores[h])]
        m_old, total = old[h]
        m_new = m_old
        for s in masked:
            m_new = jnp.maximum(m_new, jnp.max(s, axis=0, keepdims=True))
        weights = [jnp.exp(s - m_new) for s in masked]
        fade = jnp.exp(m_old - m_new)
        total = fade * total
        for p in weights:
            total = total + jnp.sum(p, axis=0, keepdims=True)
        added = sum(jnp.dot(v, p.astype(BF16), preferred_element_type=F32) for v, p in zip(values, weights))
        new.append((m_new, total, fade, added))
    for h, rows in enumerate(heads):
        m_new, total, fade, added = new[h]
        state_ref[TOP + h : TOP + h + 1, :] = m_new
        state_ref[SUM + h : SUM + h + 1, :] = total
        state_ref[rows, :] = fade * state_ref[rows, :] + added


def where_am_i(at_ref):
    own = at_ref[0]
    return own // 8, (own // 2) % 4, own % 2


def attend_pieces(at_ref, slots, piece_refs, all_ref, order_ref, sets):
    y, z, c = where_am_i(at_ref)
    blocks = []
    for piece_ref, places_of in zip(piece_refs, slots(y, z, c)):
        for i, place in enumerate(places_of):
            all_ref[len(blocks)] = piece_ref[i]
            blocks.append(ctx_id(*place))
    for core, q_ref, state_ref in zip((c, 1 - c), sets[::2], sets[1::2]):
        own = ctx_id(y, z, core)
        count = jnp.int32(0)
        for n, block in enumerate(blocks):
            order_ref[count] = n
            count += ((block < own) & (block >= own - REACH)).astype(jnp.int32)

        @pl.loop(0, (count + 1) // 2)
        def _(g, count=count, q_ref=q_ref, state_ref=state_ref):
            one = order_ref[2 * g]
            both = 2 * g + 1 < count
            two = jnp.where(both, order_ref[2 * g + 1], one)
            attend_blocks(all_ref, [(one, 0), (two, jnp.where(both, 0, BLOCK))], False, q_ref, state_ref)


def start_kernel(slots, n, at_ref, *rest):
    pieces, (q_ref, q_2_ref, s_ref, s_2_ref, all_ref, order_ref) = rest[:n], rest[n:]
    for state_ref in (s_ref, s_2_ref):
        state_ref[...] = jnp.zeros_like(state_ref)
        state_ref[TOP : TOP + 8, :] = jnp.full((8, BLOCK), FLOOR, F32)
    attend_blocks(pieces[0], [(0, 0)], True, q_ref, s_ref)
    attend_pieces(at_ref, slots, pieces, all_ref, order_ref, (q_ref, s_ref, q_2_ref, s_2_ref))


def more_kernel(slots, n, at_ref, *rest):
    pieces, (q_ref, q_2_ref, s_in, s_2_in, s_ref, s_2_ref, all_ref, order_ref) = rest[:n], rest[n:]
    s_ref[...] = s_in[...]
    s_2_ref[...] = s_2_in[...]
    attend_pieces(at_ref, slots, pieces, all_ref, order_ref, (q_ref, s_ref, q_2_ref, s_2_ref))


def query_kernel(hidden_ref, w_ref, segment_ref, out_ref, normed_ref):
    @pl.loop(0, BLOCK // 16)
    def _(i):
        rows = pl.ds(pl.multiple_of(i * 16, 16), 16)
        x = hidden_ref[rows, :].astype(F32)
        normed_ref[rows, :] = (x * lax.rsqrt(jnp.mean(x * x, axis=-1, keepdims=True) + 1e-06)).astype(BF16)

    q = jnp.zeros((BLOCK, w_ref.shape[1]), F32)
    for k in range(0, w_ref.shape[0], 1024):
        q += jnp.dot(normed_ref[:, k : k + 1024], w_ref[k : k + 1024, :], preferred_element_type=F32)
    out_ref[0 : 4 * HEAD_DIM, :] = jnp.transpose(q * HEAD_DIM ** (-0.5)).astype(BF16)
    ids = lax.broadcasted_iota(jnp.int32, (HEAD_DIM, BLOCK), 0)
    out_ref[HOT, :] = (ids == segment_ref[...]).astype(BF16)


def last_kernel(at_ref, s_ref, s_2_ref, w_ref, *rest):
    outs, att_ref = rest[:6], rest[6]
    for h in range(4):
        rows = slice(h * HEAD_DIM, (h + 1) * HEAD_DIM)
        tops = [r[TOP + h : TOP + h + 1, :] for r in (s_ref, s_2_ref)]
        top = jnp.maximum(*tops)
        fades = [jnp.exp(t - top) for t in tops]
        total = sum(f * r[SUM + h : SUM + h + 1, :] for f, r in zip(fades, (s_ref, s_2_ref)))
        value = sum(f * r[rows, :] for f, r in zip(fades, (s_ref, s_2_ref)))
        att_ref[:, rows] = jnp.transpose(value / total).astype(BF16)
    section = at_ref[1]
    for sides in itertools.product((0, 1), repeat=3):
        away = 0
        for step, side in zip(CHAINS[0][1], sides):
            away ^= step * side
        cols = pl.ds(pl.multiple_of((section ^ away) * COLS, 128), COLS)
        part = jnp.dot(att_ref[...], w_ref[:, cols], preferred_element_type=F32).astype(BF16)
        crossed = dict(zip(CHAINS[0][1], sides))
        for i, (rows, order) in enumerate(CHAINS):
            first, second, third = (crossed[step] for step in order)
            outs[2 * i + 1 - first][2 * second + third] = part[rows]


VMEM = pl.BlockSpec(memory_space=pltpu.VMEM)
SMEM = pl.BlockSpec(memory_space=pltpu.SMEM)
STATE = jax.ShapeDtypeStruct((4 * HEAD_DIM + 16, BLOCK), F32)
LIMIT = pltpu.CompilerParams(vmem_limit_bytes=24 * 1024 * 1024)


def cost(n):
    return pl.CostEstimate(
        flops=n * 4 * 4 * BLOCK * BLOCK * HEAD_DIM,
        bytes_accessed=n * PACK * HEAD_DIM * 2,
        transcendentals=n * 4 * BLOCK * BLOCK,
    )


def per_device(hidden, k_cache, v_cache, segment, w_query, w_out):
    ctx = lax.axis_index("ctx")

    smaller = jnp.sum(
        (segment[:, None] < jnp.arange(HEAD_DIM, dtype=jnp.int32)[None, :]).astype(F32), axis=0
    ).astype(BF16)
    own = jnp.concatenate([k_cache, v_cache, jnp.broadcast_to(smaller[None, :], (16, HEAD_DIM))], axis=0)[None]

    other = swap_cores(own)
    pair = jnp.concatenate([own, other], axis=0)
    z_near = along_z(pair)
    y_near = along_y(pair)
    y_far = move(pair, lambda y, z, c: (y + 2, z, c) if y < 2 else None)

    q = pl.pallas_call(
        query_kernel,
        out_shape=jax.ShapeDtypeStruct((5 * HEAD_DIM, BLOCK), BF16),
        in_specs=[VMEM] * 3,
        out_specs=VMEM,
        scratch_shapes=[pltpu.VMEM(hidden.shape, BF16)],
        compiler_params=LIMIT,
        cost_estimate=pl.CostEstimate(flops=2 * hidden.size * w_query.shape[1], bytes_accessed=8 * 10**6, transcendentals=0),
        name="project_queries",
    )(hidden, w_query, segment[None, :])

    (z_near, y_near), q = lax.optimization_barrier(((z_near, y_near), q))
    q_2 = swap_cores(q)
    z_far = along_z(z_near[:1])
    up_near = up_y(z_near)
    around_near = round_y(z_near)
    y_far, z_far = lax.optimization_barrier((y_far, z_far))
    up_far = up_y(z_far)
    around_far = round_y(z_far)
    far_near = along_z(y_far, 2)

    at = jnp.stack([ctx, lax.axis_index("section")]).astype(jnp.int32)

    def attend(kernel, slots, n, pieces, state, name):
        return pl.pallas_call(
            functools.partial(kernel, slots, len(pieces)),
            out_shape=(STATE, STATE),
            in_specs=[SMEM] + [VMEM] * (len(pieces) + 2 + len(state)),
            out_specs=(VMEM,) * 2,
            scratch_shapes=[pltpu.VMEM((n, PACK, HEAD_DIM), BF16), pltpu.SMEM((16,), jnp.int32)],
            compiler_params=LIMIT,
            cost_estimate=cost(1),
            name=name,
        )(at, *pieces, q, q_2, *state)

    state = attend(start_kernel, first_slots, 7, [own, z_near, z_far, y_near, y_far], (), "attend_first")
    far_near, state = lax.optimization_barrier((far_near, state))
    far_far = along_z(far_near[:1], 2)
    nexts = (up_near, around_near, up_far, around_far)
    nexts, state = lax.optimization_barrier((nexts, state))
    state = attend(more_kernel, next_slots, 6, nexts, state, "attend_next")
    far_far, state = lax.optimization_barrier((far_far, state))
    state, state_2 = attend(more_kernel, far_slots, 3, [far_near, far_far], state, "attend_far")
    state_2 = swap_cores(state_2)

    out_shape = []
    for rows, _ in CHAINS:
        out_shape += [jax.ShapeDtypeStruct((4, rows.stop - rows.start, COLS), BF16)] * 2
    outs = pl.pallas_call(
        last_kernel,
        out_shape=tuple(out_shape),
        in_specs=[SMEM] + [VMEM] * 3,
        out_specs=(VMEM,) * 6,
        scratch_shapes=[pltpu.VMEM((BLOCK, 4 * HEAD_DIM), BF16)],
        compiler_params=LIMIT,
        cost_estimate=cost(12),
        name="project_attended",
    )(at, state, state_2, w_out)

    def exchange(x, step):
        return lax.ppermute(x, "section", [(i, i ^ step) for i in range(8)])

    mixed = []
    for i, (_, (first, second, third)) in enumerate(CHAINS):
        sent, kept = outs[2 * i], outs[2 * i + 1]
        four = kept.astype(F32) + exchange(sent, first).astype(F32)
        two = four[:2] + exchange(four[2:].astype(BF16), second).astype(F32)
        mixed.append(two[0] + exchange(two[1].astype(BF16), third).astype(F32))
    return jnp.concatenate(mixed, axis=0).astype(BF16)


def solution(mesh):
    return jax.shard_map(
        per_device,
        mesh=mesh,
        in_specs=(
            P("ctx", None),
            P("ctx", "section"),
            P("ctx", "section"),
            P("ctx"),
            P(None, "section"),
            P("section", None),
        ),
        out_specs=P("ctx", "section"),
        check_vma=False,
    )
```

```python
import functools
import itertools

import jax
import jax.numpy as jnp
from jax import lax
from jax.experimental import pallas as pl
from jax.experimental.pallas import tpu as pltpu
from jax.sharding import PartitionSpec as P
import numpy as np

HEAD_DIM = 128
BLOCK = 256
PACK = 2 * BLOCK + 16
CHAINS = ((slice(0, 96), (1, 3, 4)), (slice(96, 176), (3, 4, 1)), (slice(176, 256), (4, 1, 3)))
REACH = 24
COLS = 640
TOP, SUM = 4 * HEAD_DIM, 4 * HEAD_DIM + 8
HOT = slice(4 * HEAD_DIM, 5 * HEAD_DIM)
FLOOR = -1e30
HIDDEN = -2e30

F32 = jnp.float32
BF16 = jnp.bfloat16


def ctx_id(y, z, c):
    return ((y + 8) % 4) * 8 + ((z + 8) % 4) * 2 + c


def ctx_pairs(step, planes=None):
    pairs = []
    for y in range(4):
        for z in range(4):
            for c in range(2):
                to = step(y, z, c)
                if to is not None:
                    pairs.append((ctx_id(y, z, c), ctx_id(*to)))
    return pairs


def move(x, step):
    return lax.ppermute(x, "ctx", ctx_pairs(step))


def swap_cores(x):
    return move(x, lambda y, z, c: (y, z, 1 - c))


def along_z(x, first_plane=0):
    def step(y, z, c):
        return (y, z + 1 if c == 0 else z - 1, c) if y >= first_plane else None

    return move(x, step)


def along_y(x):
    def step(y, z, c):
        if c == 0:
            return (y + 1, z, c) if y < 3 else None
        return (3, z, c) if y == 0 else None

    return move(x, step)


def up_y(x):
    return move(x, lambda y, z, c: (y + 1, z, c) if y < 3 else None)


def round_y(x):
    return move(x, lambda y, z, c: (3, z, c) if y == 0 else None)


def first_slots(y, z, c):
    d = 2 * c - 1
    row = [[(y, z, c)], [(y, z + d, c), (y, z + d, 1 - c)], [(y, z + 2, c)]]
    return row + [[(y + d, z, c), (y + d, z, 1 - c)], [(y + 2, z, c)]]


def next_slots(y, z, c):
    d = 2 * c - 1
    return [[(y + e, z + d, c), (y + e, z + d, 1 - c), (y + e, z + 2, c)] for e in (-1, 1)]


def far_slots(y, z, c):
    d = 2 * c - 1
    return [[(y + 2, z + d, c), (y + 2, z + d, 1 - c)], [(y + 2, z + 2, c)]]


def attend_blocks(kv_ref, places, diagonal, q_ref, state_ref):
    heads = [slice(h * HEAD_DIM, (h + 1) * HEAD_DIM) for h in range(4)]
    keys, values, visible = [], [], []
    for at, low in places:
        keys.append(kv_ref[at, 0:BLOCK, :])
        values.append(jnp.transpose(kv_ref[at, BLOCK : 2 * BLOCK, :]))
        counts = kv_ref[at, 2 * BLOCK : PACK, :]
        first = jnp.dot(counts, q_ref[HOT, :], preferred_element_type=F32)[0:1, :].astype(jnp.int32)
        row = lax.broadcasted_iota(jnp.int32, (BLOCK, BLOCK), 0)
        seen = row >= jnp.maximum(first, low)
        if diagonal:
            seen &= row <= lax.broadcasted_iota(jnp.int32, (BLOCK, BLOCK), 1)
        visible.append(seen)
    scores = [[jnp.dot(k, q_ref[rows, :], preferred_element_type=F32) for k in keys] for rows in heads]
    old = [(state_ref[TOP + h : TOP + h + 1, :], state_ref[SUM + h : SUM + h + 1, :]) for h in range(4)]
    new = []
    for h in range(4):
        masked = [jnp.where(seen, s, HIDDEN) for seen, s in zip(visible, scores[h])]
        m_old, total = old[h]
        m_new = m_old
        for s in masked:
            m_new = jnp.maximum(m_new, jnp.max(s, axis=0, keepdims=True))
        weights = [jnp.exp(s - m_new) for s in masked]
        fade = jnp.exp(m_old - m_new)
        total = fade * total
        for p in weights:
            total = total + jnp.sum(p, axis=0, keepdims=True)
        added = sum(jnp.dot(v, p.astype(BF16), preferred_element_type=F32) for v, p in zip(values, weights))
        new.append((m_new, total, fade, added))
    for h, rows in enumerate(heads):
        m_new, total, fade, added = new[h]
        state_ref[TOP + h : TOP + h + 1, :] = m_new
        state_ref[SUM + h : SUM + h + 1, :] = total
        state_ref[rows, :] = fade * state_ref[rows, :] + added


def where_am_i(at_ref):
    own = at_ref[0]
    return own // 8, (own // 2) % 4, own % 2


def attend_pieces(at_ref, slots, piece_refs, all_ref, order_ref, sets):
    y, z, c = where_am_i(at_ref)
    blocks = []
    for piece_ref, places_of in zip(piece_refs, slots(y, z, c)):
        for i, place in enumerate(places_of):
            all_ref[len(blocks)] = piece_ref[i]
            blocks.append(ctx_id(*place))
    for core, q_ref, state_ref in zip((c, 1 - c), sets[::2], sets[1::2]):
        own = ctx_id(y, z, core)
        count = jnp.int32(0)
        for n, block in enumerate(blocks):
            order_ref[count] = n
            count += ((block < own) & (block >= own - REACH)).astype(jnp.int32)

        @pl.loop(0, (count + 1) // 2)
        def _(g, count=count, q_ref=q_ref, state_ref=state_ref):
            one = order_ref[2 * g]
            both = 2 * g + 1 < count
            two = jnp.where(both, order_ref[2 * g + 1], one)
            attend_blocks(all_ref, [(one, 0), (two, jnp.where(both, 0, BLOCK))], False, q_ref, state_ref)


def start_kernel(slots, n, at_ref, *rest):
    pieces, (q_ref, q_2_ref, s_ref, s_2_ref, all_ref, order_ref) = rest[:n], rest[n:]
    for state_ref in (s_ref, s_2_ref):
        state_ref[...] = jnp.zeros_like(state_ref)
        state_ref[TOP : TOP + 8, :] = jnp.full((8, BLOCK), FLOOR, F32)
    attend_blocks(pieces[0], [(0, 0)], True, q_ref, s_ref)
    attend_pieces(at_ref, slots, pieces, all_ref, order_ref, (q_ref, s_ref, q_2_ref, s_2_ref))


def more_kernel(slots, n, at_ref, *rest):
    pieces, (q_ref, q_2_ref, s_in, s_2_in) = rest[:n], rest[n : n + 4]
    s_ref, s_2_ref, all_ref, order_ref = rest[-4:]
    s_ref[...] = s_in[...]
    s_2_ref[...] = s_2_in[...]
    attend_pieces(at_ref, slots, pieces, all_ref, order_ref, (q_ref, s_ref, q_2_ref, s_2_ref))


def last_kernel(at_ref, s_ref, s_2_ref, w_ref, *rest):
    outs, att_ref = rest[:6], rest[6]
    for h in range(4):
        rows = slice(h * HEAD_DIM, (h + 1) * HEAD_DIM)
        tops = [r[TOP + h : TOP + h + 1, :] for r in (s_ref, s_2_ref)]
        top = jnp.maximum(*tops)
        fades = [jnp.exp(t - top) for t in tops]
        total = sum(f * r[SUM + h : SUM + h + 1, :] for f, r in zip(fades, (s_ref, s_2_ref)))
        value = sum(f * r[rows, :] for f, r in zip(fades, (s_ref, s_2_ref)))
        att_ref[:, rows] = jnp.transpose(value / total).astype(BF16)
    section = at_ref[1]
    for sides in itertools.product((0, 1), repeat=3):
        away = 0
        for step, side in zip(CHAINS[0][1], sides):
            away ^= step * side
        cols = pl.ds(pl.multiple_of((section ^ away) * COLS, 128), COLS)
        part = jnp.dot(att_ref[...], w_ref[:, cols], preferred_element_type=F32).astype(BF16)
        crossed = dict(zip(CHAINS[0][1], sides))
        for i, (rows, order) in enumerate(CHAINS):
            first, second, third = (crossed[step] for step in order)
            outs[2 * i + 1 - first][2 * second + third] = part[rows]


VMEM = pl.BlockSpec(memory_space=pltpu.VMEM)
SMEM = pl.BlockSpec(memory_space=pltpu.SMEM)
STATE = jax.ShapeDtypeStruct((4 * HEAD_DIM + 16, BLOCK), F32)
LIMIT = pltpu.CompilerParams(vmem_limit_bytes=24 * 1024 * 1024)


def cost(n):
    return pl.CostEstimate(
        flops=n * 4 * 4 * BLOCK * BLOCK * HEAD_DIM,
        bytes_accessed=n * PACK * HEAD_DIM * 2,
        transcendentals=n * 4 * BLOCK * BLOCK,
    )


def per_device(hidden, k_cache, v_cache, segment, w_query, w_out):
    ctx = lax.axis_index("ctx")

    smaller = jnp.sum(
        (segment[:, None] < jnp.arange(HEAD_DIM, dtype=jnp.int32)[None, :]).astype(F32), axis=0
    ).astype(BF16)
    own = jnp.concatenate([k_cache, v_cache, jnp.broadcast_to(smaller[None, :], (16, HEAD_DIM))], axis=0)[None]

    own, other, hidden = lax.optimization_barrier((own, swap_cores(own), hidden))
    pair = jnp.concatenate([own, other], axis=0)
    z_near = along_z(pair)
    y_near = along_y(pair)
    y_far = move(pair, lambda y, z, c: (y + 2, z, c) if y < 2 else None)
    z_far = move(own, lambda y, z, c: (y, z + 2, c))

    widened = hidden.astype(F32)
    normed = (widened * lax.rsqrt(jnp.mean(widened * widened, axis=-1, keepdims=True) + 1e-06)).astype(BF16)
    q_t = (
        lax.dot_general(w_query, normed, (((0,), (1,)), ((), ())), preferred_element_type=F32) * HEAD_DIM ** (-0.5)
    ).astype(BF16)
    hot = (jnp.arange(HEAD_DIM, dtype=jnp.int32)[:, None] == segment[None, :]).astype(BF16)
    q = jnp.concatenate([q_t, hot], axis=0)

    (z_near, z_far, y_near, y_far), q = lax.optimization_barrier(((z_near, z_far, y_near, y_far), q))
    row = jnp.concatenate([z_near, z_far], axis=0)
    up = up_y(row)
    around = round_y(row)
    far_near = along_z(y_far, 2)
    far_far = move(y_far[:1], lambda y, z, c: (y, z + 2, c) if y >= 2 else None)
    q_2 = swap_cores(q)

    at = jnp.stack([ctx, lax.axis_index("section")]).astype(jnp.int32)

    def attend(kernel, slots, n, pieces, state, name):
        return pl.pallas_call(
            functools.partial(kernel, slots, len(pieces)),
            out_shape=(STATE, STATE),
            in_specs=[SMEM] + [VMEM] * (len(pieces) + 2 + len(state)),
            out_specs=(VMEM,) * 2,
            scratch_shapes=[pltpu.VMEM((n, PACK, HEAD_DIM), BF16), pltpu.SMEM((16,), jnp.int32)],
            compiler_params=LIMIT,
            cost_estimate=cost(1),
            name=name,
        )(at, *pieces, q, q_2, *state)

    state = attend(start_kernel, first_slots, 7, [own, z_near, z_far, y_near, y_far], (), "attend_first")
    (up, around), state = lax.optimization_barrier(((up, around), state))
    state = attend(more_kernel, next_slots, 6, [up, around], (*state, w_out), "attend_next")
    (far_near, far_far), state = lax.optimization_barrier(((far_near, far_far), state))
    state, state_2 = attend(more_kernel, far_slots, 3, [far_near, far_far], state, "attend_far")
    state_2 = swap_cores(state_2)

    out_shape = []
    for rows, _ in CHAINS:
        out_shape += [jax.ShapeDtypeStruct((4, rows.stop - rows.start, COLS), BF16)] * 2
    outs = pl.pallas_call(
        last_kernel,
        out_shape=tuple(out_shape),
        in_specs=[SMEM] + [VMEM] * 3,
        out_specs=(VMEM,) * 6,
        scratch_shapes=[pltpu.VMEM((BLOCK, 4 * HEAD_DIM), BF16)],
        compiler_params=LIMIT,
        cost_estimate=cost(12),
        name="project_attended",
    )(at, state, state_2, w_out)

    def exchange(x, step):
        return lax.ppermute(x, "section", [(i, i ^ step) for i in range(8)])

    mixed = []
    for i, (_, (first, second, third)) in enumerate(CHAINS):
        sent, kept = outs[2 * i], outs[2 * i + 1]
        four = kept.astype(F32) + exchange(sent, first).astype(F32)
        two = four[:2] + exchange(four[2:].astype(BF16), second).astype(F32)
        mixed.append(two[0] + exchange(two[1].astype(BF16), third).astype(F32))
    return jnp.concatenate(mixed, axis=0).astype(BF16)


def solution(mesh):
    return jax.shard_map(
        per_device,
        mesh=mesh,
        in_specs=(
            P("ctx", None),
            P("ctx", "section"),
            P("ctx", "section"),
            P("ctx"),
            P(None, "section"),
            P("section", None),
        ),
        out_specs=P("ctx", "section"),
        check_vma=False,
    )
```

```python
import functools
import itertools

import jax
import jax.numpy as jnp
from jax import lax
from jax.experimental import pallas as pl
from jax.experimental.pallas import tpu as pltpu
from jax.sharding import PartitionSpec as P
import numpy as np

HEAD_DIM = 128
BLOCK = 256
PACK = 2 * BLOCK + 16
CHAINS = ((slice(0, 80), (1, 3, 4)), (slice(80, 176), (3, 4, 1)), (slice(176, 256), (4, 1, 3)))
SIDES = tuple(itertools.product((0, 1), repeat=3))
REACH = 24
COLS = 640
TOP, SUM = 4 * HEAD_DIM, 4 * HEAD_DIM + 8
HOT = slice(4 * HEAD_DIM, 5 * HEAD_DIM)
FLOOR = -1e30
HIDDEN = -2e30

F32 = jnp.float32
BF16 = jnp.bfloat16


def away(sides):
    return sum(step * side for step, side in zip((1, 3, 4), sides)) if sides[:2] != (1, 1) else 2 + 4 * sides[2]


def ctx_id(y, z, c):
    return ((y + 8) % 4) * 8 + ((z + 8) % 4) * 2 + c


def ctx_pairs(step, planes=None):
    pairs = []
    for y in range(4):
        for z in range(4):
            for c in range(2):
                to = step(y, z, c)
                if to is not None:
                    pairs.append((ctx_id(y, z, c), ctx_id(*to)))
    return pairs


def move(x, step):
    return lax.ppermute(x, "ctx", ctx_pairs(step))


def swap_cores(x):
    return move(x, lambda y, z, c: (y, z, 1 - c))


def along_z(x, first_plane=0):
    def step(y, z, c):
        return (y, z + 1 if c == 0 else z - 1, c) if y >= first_plane else None

    return move(x, step)


def along_y(x):
    def step(y, z, c):
        if c == 0:
            return (y + 1, z, c) if y < 3 else None
        return (3, z, c) if y == 0 else None

    return move(x, step)


def up_y(x):
    return move(x, lambda y, z, c: (y + 1, z, c) if y < 3 else None)


def round_y(x):
    return move(x, lambda y, z, c: (3, z, c) if y == 0 else None)


def first_slots(y, z, c):
    d = 2 * c - 1
    row = [[(y, z, c)], [(y, z + d, c), (y, z + d, 1 - c)], [(y, z + 2, c)]]
    return row + [[(y + d, z, c), (y + d, z, 1 - c)], [(y + 2, z, c)]]


def rest_slots(y, z, c):
    d = 2 * c - 1
    near = [[(y + e, z + d, c), (y + e, z + d, 1 - c), (y + e, z + 2, c)] for e in (-1, 1)]
    return near + [[(y + 2, z + d, c), (y + 2, z + d, 1 - c)], [(y + 2, z + 2, c)]]


def attend_blocks(kv_ref, places, diagonal, q_ref, state_ref):
    heads = [slice(h * HEAD_DIM, (h + 1) * HEAD_DIM) for h in range(4)]
    keys, values, visible = [], [], []
    for at in places:
        keys.append(kv_ref[at, 0:BLOCK, :])
        values.append(jnp.transpose(kv_ref[at, BLOCK : 2 * BLOCK, :]))
        counts = kv_ref[at, 2 * BLOCK : PACK, :]
        first = jnp.dot(counts, q_ref[HOT, :], preferred_element_type=F32)[0:1, :].astype(jnp.int32)
        row = lax.broadcasted_iota(jnp.int32, (BLOCK, BLOCK), 0)
        seen = row >= first
        if diagonal:
            seen &= row <= lax.broadcasted_iota(jnp.int32, (BLOCK, BLOCK), 1)
        visible.append(seen)
    scores = [[jnp.dot(k, q_ref[rows, :], preferred_element_type=F32) for k in keys] for rows in heads]
    old = [(state_ref[TOP + h : TOP + h + 1, :], state_ref[SUM + h : SUM + h + 1, :]) for h in range(4)]
    new = []
    for h in range(4):
        masked = [jnp.where(seen, s, HIDDEN) for seen, s in zip(visible, scores[h])]
        m_old, total = old[h]
        m_new = m_old
        for s in masked:
            m_new = jnp.maximum(m_new, jnp.max(s, axis=0, keepdims=True))
        weights = [jnp.exp(s - m_new) for s in masked]
        fade = jnp.exp(m_old - m_new)
        total = fade * total
        for p in weights:
            total = total + jnp.sum(p, axis=0, keepdims=True)
        added = sum(jnp.dot(v, p.astype(BF16), preferred_element_type=F32) for v, p in zip(values, weights))
        new.append((m_new, total, fade, added))
    for h, rows in enumerate(heads):
        m_new, total, fade, added = new[h]
        state_ref[TOP + h : TOP + h + 1, :] = m_new
        state_ref[SUM + h : SUM + h + 1, :] = total
        state_ref[rows, :] = fade * state_ref[rows, :] + added


def where_am_i(at_ref):
    own = at_ref[0]
    return own // 8, (own // 2) % 4, own % 2


def attend_pieces(at_ref, slots, piece_refs, all_ref, order_ref, sets, others=(0, 1)):
    y, z, c = where_am_i(at_ref)
    blocks = []
    for piece_ref, places_of in zip(piece_refs, slots(y, z, c)):
        for i, place in enumerate(places_of):
            all_ref[len(blocks)] = piece_ref[i]
            blocks.append(ctx_id(*place))
    for other, q_ref, state_ref in zip(others, sets[::2], sets[1::2]):
        own = ctx_id(y, z, c + other - 2 * other * c)
        count = jnp.int32(0)
        for n, block in enumerate(blocks):
            order_ref[count] = n
            count += ((block < own) & (block >= own - REACH)).astype(jnp.int32)

        @pl.loop(0, count // 2)
        def _(g, q_ref=q_ref, state_ref=state_ref):
            attend_blocks(all_ref, [order_ref[2 * g], order_ref[2 * g + 1]], False, q_ref, state_ref)

        @pl.when(count % 2 == 1)
        def _(count=count, q_ref=q_ref, state_ref=state_ref):
            attend_blocks(all_ref, [order_ref[count - 1]], False, q_ref, state_ref)


def start_kernel(slots, n, at_ref, *rest):
    pieces, (q_ref, q_2_ref, s_ref, s_2_ref, all_ref, order_ref) = rest[:n], rest[n:]
    for state_ref in (s_ref, s_2_ref):
        state_ref[...] = jnp.zeros_like(state_ref)
        state_ref[TOP : TOP + 8, :] = jnp.full((8, BLOCK), FLOOR, F32)
    attend_blocks(pieces[0], [0], True, q_ref, s_ref)
    attend_pieces(at_ref, slots, pieces, all_ref, order_ref, (q_ref, s_ref, q_2_ref, s_2_ref))


def more_kernel(slots, n, other, at_ref, *rest):
    pieces, (q_ref, s_in, s_ref, all_ref, order_ref) = rest[:n], rest[n:]
    s_ref[...] = s_in[...]
    attend_pieces(at_ref, slots, pieces, all_ref, order_ref, (q_ref, s_ref), (other,))


def last_kernel(at_ref, s_ref, s_2_ref, w_hbm, *rest):
    outs, (att_ref, w_ref, sems) = rest[:6], rest[6:]
    section = at_ref[1]
    fetched = []
    for n, sides in enumerate(SIDES):
        cols = pl.ds(pl.multiple_of((section ^ away(sides)) * COLS, 128), COLS)
        fetched.append(pltpu.make_async_copy(w_hbm.at[:, cols], w_ref.at[n], sems.at[n]))
        fetched[-1].start()
    for h in range(4):
        rows = slice(h * HEAD_DIM, (h + 1) * HEAD_DIM)
        tops = [r[TOP + h : TOP + h + 1, :] for r in (s_ref, s_2_ref)]
        top = jnp.maximum(*tops)
        fades = [jnp.exp(t - top) for t in tops]
        total = sum(f * r[SUM + h : SUM + h + 1, :] for f, r in zip(fades, (s_ref, s_2_ref)))
        value = sum(f * r[rows, :] for f, r in zip(fades, (s_ref, s_2_ref)))
        att_ref[:, rows] = jnp.transpose(value / total).astype(BF16)
    for n, sides in enumerate(SIDES):
        fetched[n].wait()
        part = jnp.dot(att_ref[...], w_ref[n], preferred_element_type=F32).astype(BF16)
        crossed = dict(zip(CHAINS[0][1], sides))
        for i, (rows, order) in enumerate(CHAINS):
            first, second, third = (crossed[step] for step in order)
            outs[2 * i + 1 - first][2 * second + third] = part[rows]


VMEM = pl.BlockSpec(memory_space=pltpu.VMEM)
SMEM = pl.BlockSpec(memory_space=pltpu.SMEM)
STATE = jax.ShapeDtypeStruct((4 * HEAD_DIM + 16, BLOCK), F32)
LAST_LIMIT = 48
LIMIT = pltpu.CompilerParams(vmem_limit_bytes=24 * 1024 * 1024)


def cost(n):
    return pl.CostEstimate(
        flops=n * 4 * 4 * BLOCK * BLOCK * HEAD_DIM,
        bytes_accessed=n * PACK * HEAD_DIM * 2,
        transcendentals=n * 4 * BLOCK * BLOCK,
    )


def per_device(hidden, k_cache, v_cache, segment, w_query, w_out):
    ctx = lax.axis_index("ctx")

    smaller = jnp.sum(
        (segment[:, None] < jnp.arange(HEAD_DIM, dtype=jnp.int32)[None, :]).astype(F32), axis=0
    ).astype(BF16)
    own = jnp.concatenate([k_cache, v_cache, jnp.broadcast_to(smaller[None, :], (16, HEAD_DIM))], axis=0)[None]

    own, other, hidden = lax.optimization_barrier((own, swap_cores(own), hidden))
    pair = jnp.concatenate([own, other], axis=0)
    z_near = along_z(pair)
    y_near = along_y(pair)
    y_far = move(pair, lambda y, z, c: (y + 2, z, c) if y < 2 else None)
    z_far = move(own, lambda y, z, c: (y, z + 2, c))

    widened = hidden.astype(F32)
    normed = (widened * lax.rsqrt(jnp.mean(widened * widened, axis=-1, keepdims=True) + 1e-06)).astype(BF16)
    q_t = (
        lax.dot_general(w_query, normed, (((0,), (1,)), ((), ())), preferred_element_type=F32) * HEAD_DIM ** (-0.5)
    ).astype(BF16)
    hot = (jnp.arange(HEAD_DIM, dtype=jnp.int32)[:, None] == segment[None, :]).astype(BF16)
    q = jnp.concatenate([q_t, hot], axis=0)

    (z_near, z_far, y_near, y_far), q = lax.optimization_barrier(((z_near, z_far, y_near, y_far), q))
    row = jnp.concatenate([z_near, z_far], axis=0)
    up = up_y(row)
    around = round_y(row)
    far_near = along_z(y_far, 2)
    far_far = move(z_far, lambda y, z, c: (y + 2, z, c) if y < 2 else None)
    q_2 = swap_cores(q)

    at = jnp.stack([ctx, lax.axis_index("section")]).astype(jnp.int32)

    def attend(kernel, n, pieces, queries, states, name):
        out_shape = (STATE,) * len(queries)
        return pl.pallas_call(
            kernel,
            out_shape=out_shape,
            in_specs=[SMEM] + [VMEM] * (len(pieces) + len(queries) + len(states)),
            out_specs=(VMEM,) * len(out_shape),
            scratch_shapes=[pltpu.VMEM((n, PACK, HEAD_DIM), BF16), pltpu.SMEM((16,), jnp.int32)],
            compiler_params=LIMIT,
            cost_estimate=cost(1),
            name=name,
        )(at, *pieces, *queries, *states)

    pieces = [own, z_near, z_far, y_near, y_far]
    first = functools.partial(start_kernel, first_slots, len(pieces))
    state, state_2 = attend(first, 7, pieces, (q, q_2), (), "attend_first")
    pieces, state, state_2 = lax.optimization_barrier(((up, around, far_near, far_far), state, state_2))
    rest = [functools.partial(more_kernel, rest_slots, len(pieces), other) for other in (0, 1)]
    (state_2,) = attend(rest[1], 9, pieces, (q_2,), (state_2,), "attend_rest_other")
    state_2, state = lax.optimization_barrier((state_2, state))
    (state,) = attend(rest[0], 9, pieces, (q,), (state,), "attend_rest_own")
    state_2 = swap_cores(state_2)

    out_shape = []
    for rows, _ in CHAINS:
        out_shape += [jax.ShapeDtypeStruct((4, rows.stop - rows.start, COLS), BF16)] * 2
    outs = pl.pallas_call(
        last_kernel,
        out_shape=tuple(out_shape),
        in_specs=[SMEM, VMEM, VMEM, pl.BlockSpec(memory_space=pltpu.HBM)],
        out_specs=(VMEM,) * 6,
        scratch_shapes=[
            pltpu.VMEM((BLOCK, 4 * HEAD_DIM), BF16),
            pltpu.VMEM((8, w_out.shape[0], COLS), BF16),
            pltpu.SemaphoreType.DMA((8,)),
        ],
        compiler_params=pltpu.CompilerParams(vmem_limit_bytes=LAST_LIMIT * 1024 * 1024),
        cost_estimate=cost(12),
        name="project_attended",
    )(at, state, state_2, w_out)

    def exchange(x, step):
        return lax.ppermute(x, "section", [(i, i ^ step) for i in range(8)])

    mixed = []
    for i, (_, (first, second, third)) in enumerate(CHAINS):
        sent, kept = outs[2 * i], outs[2 * i + 1]
        four = kept.astype(F32) + exchange(sent, first).astype(F32)
        two = four[:2] + exchange(four[2:].astype(BF16), second).astype(F32)
        mixed.append(two[0] + exchange(two[1].astype(BF16), third).astype(F32))
    return jnp.concatenate(mixed, axis=0).astype(BF16)


def solution(mesh):
    return jax.shard_map(
        per_device,
        mesh=mesh,
        in_specs=(
            P("ctx", None),
            P("ctx", "section"),
            P("ctx", "section"),
            P("ctx"),
            P(None, "section"),
            P("section", None),
        ),
        out_specs=P("ctx", "section"),
        check_vma=False,
    )
```

```python
import functools
import itertools

import jax
import jax.numpy as jnp
from jax import lax
from jax.experimental import pallas as pl
from jax.experimental.pallas import tpu as pltpu
from jax.sharding import PartitionSpec as P
import numpy as np

HEAD_DIM = 128
BLOCK = 256
PACK = 2 * BLOCK + 16
CHAINS = ((slice(0, 80), (1, 3, 4)), (slice(80, 176), (3, 4, 1)), (slice(176, 256), (4, 1, 3)))
SIDES = tuple(itertools.product((0, 1), repeat=3))
REACH = 24
COLS = 640
TOP, SUM = 4 * HEAD_DIM, 4 * HEAD_DIM + 8
HOT = slice(4 * HEAD_DIM, 5 * HEAD_DIM)
FLOOR = -1e30
HIDDEN = -2e30

F32 = jnp.float32
BF16 = jnp.bfloat16


def away(sides):
    return sum(step * side for step, side in zip((1, 3, 4), sides)) if sides[:2] != (1, 1) else 2 + 4 * sides[2]


def ctx_id(y, z, c):
    return ((y + 8) % 4) * 8 + ((z + 8) % 4) * 2 + c


def ctx_pairs(step, planes=None):
    pairs = []
    for y in range(4):
        for z in range(4):
            for c in range(2):
                to = step(y, z, c)
                if to is not None:
                    pairs.append((ctx_id(y, z, c), ctx_id(*to)))
    return pairs


def move(x, step):
    return lax.ppermute(x, "ctx", ctx_pairs(step))


def swap_cores(x):
    return move(x, lambda y, z, c: (y, z, 1 - c))


def along_z(x, first_plane=0):
    def step(y, z, c):
        return (y, z + 1 if c == 0 else z - 1, c) if y >= first_plane else None

    return move(x, step)


def along_y(x):
    def step(y, z, c):
        if c == 0:
            return (y + 1, z, c) if y < 3 else None
        return (3, z, c) if y == 0 else None

    return move(x, step)


def up_y(x):
    return move(x, lambda y, z, c: (y + 1, z, c) if y < 3 else None)


def round_y(x):
    return move(x, lambda y, z, c: (3, z, c) if y == 0 else None)


def first_slots(y, z, c):
    d = 2 * c - 1
    row = [[(y, z, c)], [(y, z + d, c), (y, z + d, 1 - c)], [(y, z + 2, c)]]
    return row + [[(y + d, z, c), (y + d, z, 1 - c)], [(y + 2, z, c)]]


def rest_slots(y, z, c):
    d = 2 * c - 1
    near = [[(y + e, z + d, c), (y + e, z + d, 1 - c), (y + e, z + 2, c)] for e in (-1, 1)]
    return near + [[(y + 2, z + d, c), (y + 2, z + d, 1 - c)], [(y + 2, z + 2, c)]]


def attend_blocks(kv_ref, places, diagonal, q_ref, state_ref):
    heads = [slice(h * HEAD_DIM, (h + 1) * HEAD_DIM) for h in range(4)]
    keys, values, visible = [], [], []
    for at in places:
        keys.append(kv_ref[at, 0:BLOCK, :])
        ones = jnp.ones((16, BLOCK), BF16)
        values.append(jnp.concatenate([jnp.transpose(kv_ref[at, BLOCK : 2 * BLOCK, :]), ones], axis=0))
        counts = kv_ref[at, 2 * BLOCK : PACK, :]
        first = jnp.dot(counts, q_ref[HOT, :], preferred_element_type=F32)[0:1, :].astype(jnp.int32)
        row = lax.broadcasted_iota(jnp.int32, (BLOCK, BLOCK), 0)
        seen = row >= first
        if diagonal:
            seen &= row <= lax.broadcasted_iota(jnp.int32, (BLOCK, BLOCK), 1)
        visible.append(seen)
    scores = [[jnp.dot(k, q_ref[rows, :], preferred_element_type=F32) for k in keys] for rows in heads]
    old = [(state_ref[TOP + h : TOP + h + 1, :], state_ref[SUM + h : SUM + h + 1, :]) for h in range(4)]
    new = []
    for h in range(4):
        masked = [jnp.where(seen, s, HIDDEN) for seen, s in zip(visible, scores[h])]
        m_old, total = old[h]
        m_new = m_old
        for s in masked:
            m_new = jnp.maximum(m_new, jnp.max(s, axis=0, keepdims=True))
        weights = [jnp.exp(s - m_new) for s in masked]
        fade = jnp.exp(m_old - m_new)
        added = sum(jnp.dot(v, p.astype(BF16), preferred_element_type=F32) for v, p in zip(values, weights))
        new.append((m_new, fade * total + added[HEAD_DIM : HEAD_DIM + 1], fade, added[:HEAD_DIM]))
    for h, rows in enumerate(heads):
        m_new, total, fade, added = new[h]
        state_ref[TOP + h : TOP + h + 1, :] = m_new
        state_ref[SUM + h : SUM + h + 1, :] = total
        state_ref[rows, :] = fade * state_ref[rows, :] + added


def where_am_i(at_ref):
    own = at_ref[0]
    return own // 8, (own // 2) % 4, own % 2


def attend_pieces(at_ref, slots, piece_refs, all_ref, order_ref, sets, others=(0, 1)):
    y, z, c = where_am_i(at_ref)
    blocks = []
    for piece_ref, places_of in zip(piece_refs, slots(y, z, c)):
        for i, place in enumerate(places_of):
            all_ref[len(blocks)] = piece_ref[i]
            blocks.append(ctx_id(*place))
    for other, q_ref, state_ref in zip(others, sets[::2], sets[1::2]):
        own = ctx_id(y, z, c + other - 2 * other * c)
        count = jnp.int32(0)
        for n, block in enumerate(blocks):
            order_ref[count] = n
            count += ((block < own) & (block >= own - REACH)).astype(jnp.int32)

        threes = count // 3

        @pl.loop(0, threes)
        def _(g, q_ref=q_ref, state_ref=state_ref):
            attend_blocks(all_ref, [order_ref[3 * g + i] for i in range(3)], False, q_ref, state_ref)

        @pl.loop(3 * threes, count)
        def _(i, q_ref=q_ref, state_ref=state_ref):
            attend_blocks(all_ref, [order_ref[i]], False, q_ref, state_ref)


def start_kernel(slots, n, at_ref, *rest):
    pieces, (q_ref, q_2_ref, s_ref, s_2_ref, all_ref, order_ref) = rest[:n], rest[n:]
    for state_ref in (s_ref, s_2_ref):
        state_ref[...] = jnp.zeros_like(state_ref)
        state_ref[TOP : TOP + 8, :] = jnp.full((8, BLOCK), FLOOR, F32)
    attend_blocks(pieces[0], [0], True, q_ref, s_ref)
    attend_pieces(at_ref, slots, pieces, all_ref, order_ref, (q_ref, s_ref, q_2_ref, s_2_ref))


def more_kernel(slots, n, other, at_ref, *rest):
    pieces, (q_ref, s_in, s_ref, all_ref, order_ref) = rest[:n], rest[n:]
    s_ref[...] = s_in[...]
    attend_pieces(at_ref, slots, pieces, all_ref, order_ref, (q_ref, s_ref), (other,))


def more_and_fetch_kernel(slots, n, other, at_ref, *rest):
    w_hbm, s_ref, w_ref, all_ref, order_ref, sem = rest[n + 2 :]
    copy = pltpu.make_async_copy(w_hbm, w_ref, sem)
    copy.start()
    more_kernel(slots, n, other, at_ref, *rest[: n + 2], s_ref, all_ref, order_ref)
    copy.wait()


def last_kernel(at_ref, s_ref, s_2_ref, w_ref, *rest):
    outs, att_ref = rest[:6], rest[6]
    section = at_ref[1]
    for h in range(4):
        rows = slice(h * HEAD_DIM, (h + 1) * HEAD_DIM)
        tops = [r[TOP + h : TOP + h + 1, :] for r in (s_ref, s_2_ref)]
        top = jnp.maximum(*tops)
        fades = [jnp.exp(t - top) for t in tops]
        total = sum(f * r[SUM + h : SUM + h + 1, :] for f, r in zip(fades, (s_ref, s_2_ref)))
        value = sum(f * r[rows, :] for f, r in zip(fades, (s_ref, s_2_ref)))
        att_ref[:, rows] = jnp.transpose(value / total).astype(BF16)
    for sides in SIDES:
        cols = pl.ds(pl.multiple_of((section ^ away(sides)) * COLS, 128), COLS)
        part = jnp.dot(att_ref[...], w_ref[:, cols], preferred_element_type=F32).astype(BF16)
        crossed = dict(zip(CHAINS[0][1], sides))
        for i, (rows, order) in enumerate(CHAINS):
            first, second, third = (crossed[step] for step in order)
            outs[2 * i + 1 - first][2 * second + third] = part[rows]


VMEM = pl.BlockSpec(memory_space=pltpu.VMEM)
SMEM = pl.BlockSpec(memory_space=pltpu.SMEM)
STATE = jax.ShapeDtypeStruct((4 * HEAD_DIM + 16, BLOCK), F32)
LAST_LIMIT = 44
LIMIT = pltpu.CompilerParams(vmem_limit_bytes=24 * 1024 * 1024)


def cost(n):
    return pl.CostEstimate(
        flops=n * 4 * 4 * BLOCK * BLOCK * HEAD_DIM,
        bytes_accessed=n * PACK * HEAD_DIM * 2,
        transcendentals=n * 4 * BLOCK * BLOCK,
    )


def per_device(hidden, k_cache, v_cache, segment, w_query, w_out):
    ctx = lax.axis_index("ctx")

    smaller = jnp.sum(
        (segment[:, None] < jnp.arange(HEAD_DIM, dtype=jnp.int32)[None, :]).astype(F32), axis=0
    ).astype(BF16)
    own = jnp.concatenate([k_cache, v_cache, jnp.broadcast_to(smaller[None, :], (16, HEAD_DIM))], axis=0)[None]

    own, other, hidden = lax.optimization_barrier((own, swap_cores(own), hidden))
    pair = jnp.concatenate([own, other], axis=0)
    z_near = along_z(pair)
    y_near = along_y(pair)
    y_far = move(pair, lambda y, z, c: (y + 2, z, c) if y < 2 else None)
    z_far = move(own, lambda y, z, c: (y, z + 2, c))

    widened = hidden.astype(F32)
    normed = (widened * lax.rsqrt(jnp.mean(widened * widened, axis=-1, keepdims=True) + 1e-06)).astype(BF16)
    q_t = (
        lax.dot_general(w_query, normed, (((0,), (1,)), ((), ())), preferred_element_type=F32) * HEAD_DIM ** (-0.5)
    ).astype(BF16)
    hot = (jnp.arange(HEAD_DIM, dtype=jnp.int32)[:, None] == segment[None, :]).astype(BF16)
    q = jnp.concatenate([q_t, hot], axis=0)

    (z_near, z_far, y_near, y_far), q = lax.optimization_barrier(((z_near, z_far, y_near, y_far), q))
    row = jnp.concatenate([z_near, z_far], axis=0)
    up = up_y(row)
    around = round_y(row)
    far_near = along_z(y_far, 2)
    far_far = move(z_far, lambda y, z, c: (y + 2, z, c) if y < 2 else None)
    q_2 = swap_cores(q)

    at = jnp.stack([ctx, lax.axis_index("section")]).astype(jnp.int32)

    def attend(kernel, n, pieces, queries, states, name):
        out_shape = (STATE,) * len(queries)
        return pl.pallas_call(
            kernel,
            out_shape=out_shape,
            in_specs=[SMEM] + [VMEM] * (len(pieces) + len(queries) + len(states)),
            out_specs=(VMEM,) * len(out_shape),
            scratch_shapes=[pltpu.VMEM((n, PACK, HEAD_DIM), BF16), pltpu.SMEM((16,), jnp.int32)],
            compiler_params=LIMIT,
            cost_estimate=cost(1),
            name=name,
        )(at, *pieces, *queries, *states)

    pieces = [own, z_near, z_far, y_near, y_far]
    first = functools.partial(start_kernel, first_slots, len(pieces))
    state, state_2 = attend(first, 7, pieces, (q, q_2), (), "attend_first")
    pieces, state, state_2 = lax.optimization_barrier(((up, around, far_near, far_far), state, state_2))
    rest = functools.partial(more_kernel, rest_slots, len(pieces), 1)
    (state_2,) = attend(rest, 9, pieces, (q_2,), (state_2,), "attend_rest_other")
    state_2, state = lax.optimization_barrier((state_2, state))
    state, w_held = pl.pallas_call(
        functools.partial(more_and_fetch_kernel, rest_slots, len(pieces), 0),
        out_shape=(STATE, jax.ShapeDtypeStruct(w_out.shape, BF16)),
        in_specs=[SMEM] + [VMEM] * (len(pieces) + 2) + [pl.BlockSpec(memory_space=pltpu.HBM)],
        out_specs=(VMEM,) * 2,
        scratch_shapes=[
            pltpu.VMEM((9, PACK, HEAD_DIM), BF16),
            pltpu.SMEM((16,), jnp.int32),
            pltpu.SemaphoreType.DMA,
        ],
        compiler_params=pltpu.CompilerParams(vmem_limit_bytes=LAST_LIMIT * 1024 * 1024),
        cost_estimate=cost(1),
        name="attend_rest_own",
    )(at, *pieces, q, state, w_out)
    state_2 = swap_cores(state_2)

    out_shape = []
    for rows, _ in CHAINS:
        out_shape += [jax.ShapeDtypeStruct((4, rows.stop - rows.start, COLS), BF16)] * 2
    outs = pl.pallas_call(
        last_kernel,
        out_shape=tuple(out_shape),
        in_specs=[SMEM, VMEM, VMEM, VMEM],
        out_specs=(VMEM,) * 6,
        scratch_shapes=[pltpu.VMEM((BLOCK, 4 * HEAD_DIM), BF16)],
        compiler_params=LIMIT,
        cost_estimate=cost(12),
        name="project_attended",
    )(at, state, state_2, w_held)

    def exchange(x, step):
        return lax.ppermute(x, "section", [(i, i ^ step) for i in range(8)])

    mixed = []
    for i, (_, (first, second, third)) in enumerate(CHAINS):
        sent, kept = outs[2 * i], outs[2 * i + 1]
        four = kept.astype(F32) + exchange(sent, first).astype(F32)
        two = four[:2] + exchange(four[2:].astype(BF16), second).astype(F32)
        mixed.append(two[0] + exchange(two[1].astype(BF16), third).astype(F32))
    return jnp.concatenate(mixed, axis=0).astype(BF16)


def solution(mesh):
    return jax.shard_map(
        per_device,
        mesh=mesh,
        in_specs=(
            P("ctx", None),
            P("ctx", "section"),
            P("ctx", "section"),
            P("ctx"),
            P(None, "section"),
            P("section", None),
        ),
        out_specs=P("ctx", "section"),
        check_vma=False,
    )
```

```python
import functools
import itertools

import jax
import jax.numpy as jnp
from jax import lax
from jax.experimental import pallas as pl
from jax.experimental.pallas import tpu as pltpu
from jax.sharding import PartitionSpec as P
import numpy as np

HEAD_DIM = 128
BLOCK = 256
PACK = 2 * BLOCK + 16
CHAINS = ((slice(0, 96), (1, 3, 4)), (slice(96, 176), (3, 4, 1)), (slice(176, 256), (4, 1, 3)))
LINKS = (1, 3, 4)
SIDES = tuple(itertools.product((0, 1), repeat=3))
REACH = 24
COLS = 640
TOP, SUM = 4 * HEAD_DIM, 4 * HEAD_DIM + 8
HOT = slice(4 * HEAD_DIM, 5 * HEAD_DIM)
FLOOR = -1e30
HIDDEN = -2e30

F32 = jnp.float32
BF16 = jnp.bfloat16


def away(sides):
    return sum(step * side for step, side in zip(LINKS, sides)) if sides[:2] != (1, 1) else 2 + 4 * sides[2]


def ctx_id(y, z, c):
    return ((y + 8) % 4) * 8 + ((z + 8) % 4) * 2 + c


def ctx_pairs(step, planes=None):
    pairs = []
    for y in range(4):
        for z in range(4):
            for c in range(2):
                to = step(y, z, c)
                if to is not None:
                    pairs.append((ctx_id(y, z, c), ctx_id(*to)))
    return pairs


def move(x, step):
    return lax.ppermute(x, "ctx", ctx_pairs(step))


def swap_cores(x):
    return move(x, lambda y, z, c: (y, z, 1 - c))


def along_z(x, first_plane=0):
    def step(y, z, c):
        return (y, z + 1 if c == 0 else z - 1, c) if y >= first_plane else None

    return move(x, step)


def along_y(x):
    def step(y, z, c):
        if c == 0:
            return (y + 1, z, c) if y < 3 else None
        return (3, z, c) if y == 0 else None

    return move(x, step)


def up_y(x):
    return move(x, lambda y, z, c: (y + 1, z, c) if y < 3 else None)


def round_y(x):
    return move(x, lambda y, z, c: (3, z, c) if y == 0 else None)


def first_slots(y, z, c):
    d = 2 * c - 1
    row = [[(y, z, c)], [(y, z + d, c), (y, z + d, 1 - c)], [(y, z + 2, c)]]
    return row + [[(y + d, z, c), (y + d, z, 1 - c)], [(y + 2, z, c)]]


def rest_slots(y, z, c):
    d = 2 * c - 1
    return [[(y + e, z + d, c), (y + e, z + d, 1 - c), (y + e, z + 2, c)] for e in (-1, 1)] + [[(y + 2, z + 2, c)]]


def far_slots(y, z, c):
    d = 2 * c - 1
    return [[(y + 2, z + d, c), (y + 2, z + d, 1 - c)]]


def attend_blocks(kv_ref, places, diagonal, q_ref, state_ref):
    heads = [slice(h * HEAD_DIM, (h + 1) * HEAD_DIM) for h in range(4)]
    keys, values, visible = [], [], []
    for at in places:
        keys.append(kv_ref[at, 0:BLOCK, :])
        ones = jnp.ones((16, BLOCK), BF16)
        values.append(jnp.concatenate([jnp.transpose(kv_ref[at, BLOCK : 2 * BLOCK, :]), ones], axis=0))
        counts = kv_ref[at, 2 * BLOCK : PACK, :]
        first = jnp.dot(counts, q_ref[HOT, :], preferred_element_type=F32)[0:1, :].astype(jnp.int32)
        row = lax.broadcasted_iota(jnp.int32, (BLOCK, BLOCK), 0)
        seen = row >= first
        if diagonal:
            seen &= row <= lax.broadcasted_iota(jnp.int32, (BLOCK, BLOCK), 1)
        visible.append(seen)
    scores = [[jnp.dot(k, q_ref[rows, :], preferred_element_type=F32) for k in keys] for rows in heads]
    old = [(state_ref[TOP + h : TOP + h + 1, :], state_ref[SUM + h : SUM + h + 1, :]) for h in range(4)]
    new = []
    for h in range(4):
        masked = [jnp.where(seen, s, HIDDEN) for seen, s in zip(visible, scores[h])]
        m_old, total = old[h]
        m_new = m_old
        for s in masked:
            m_new = jnp.maximum(m_new, jnp.max(s, axis=0, keepdims=True))
        weights = [jnp.exp(s - m_new) for s in masked]
        fade = jnp.exp(m_old - m_new)
        added = sum(jnp.dot(v, p.astype(BF16), preferred_element_type=F32) for v, p in zip(values, weights))
        new.append((m_new, fade * total + added[HEAD_DIM : HEAD_DIM + 1], fade, added[:HEAD_DIM]))
    for h, rows in enumerate(heads):
        m_new, total, fade, added = new[h]
        state_ref[TOP + h : TOP + h + 1, :] = m_new
        state_ref[SUM + h : SUM + h + 1, :] = total
        state_ref[rows, :] = fade * state_ref[rows, :] + added


def where_am_i(at_ref):
    own = at_ref[0]
    return own // 8, (own // 2) % 4, own % 2


def attend_pieces(at_ref, slots, piece_refs, all_ref, order_ref, sets, others=(0, 1)):
    y, z, c = where_am_i(at_ref)
    blocks = []
    for piece_ref, places_of in zip(piece_refs, slots(y, z, c)):
        for i, place in enumerate(places_of):
            all_ref[len(blocks)] = piece_ref[i]
            blocks.append(ctx_id(*place))
    for other, q_ref, state_ref in zip(others, sets[::2], sets[1::2]):
        own = ctx_id(y, z, c + other - 2 * other * c)
        count = jnp.int32(0)
        for n, block in enumerate(blocks):
            order_ref[count] = n
            count += ((block < own) & (block >= own - REACH)).astype(jnp.int32)

        threes = count // 3

        @pl.loop(0, threes)
        def _(g, q_ref=q_ref, state_ref=state_ref):
            attend_blocks(all_ref, [order_ref[3 * g + i] for i in range(3)], False, q_ref, state_ref)

        @pl.loop(3 * threes, count)
        def _(i, q_ref=q_ref, state_ref=state_ref):
            attend_blocks(all_ref, [order_ref[i]], False, q_ref, state_ref)


def start_kernel(slots, n, at_ref, *rest):
    pieces, (q_ref, q_2_ref, s_ref, s_2_ref, all_ref, order_ref) = rest[:n], rest[n:]
    for state_ref in (s_ref, s_2_ref):
        state_ref[...] = jnp.zeros_like(state_ref)
        state_ref[TOP : TOP + 8, :] = jnp.full((8, BLOCK), FLOOR, F32)
    attend_blocks(pieces[0], [0], True, q_ref, s_ref)
    attend_pieces(at_ref, slots, pieces, all_ref, order_ref, (q_ref, s_ref, q_2_ref, s_2_ref))


def more_kernel(slots, n, others, at_ref, *rest):
    k = len(others)
    pieces, queries, before, after = rest[:n], rest[n : n + k], rest[n + k : n + 2 * k], rest[n + 2 * k : n + 3 * k]
    all_ref, order_ref = rest[n + 3 * k :]
    for s_in, s_ref in zip(before, after):
        s_ref[...] = s_in[...]
    sets = [ref for pair in zip(queries, after) for ref in pair]
    attend_pieces(at_ref, slots, pieces, all_ref, order_ref, sets, others)


def more_and_fetch_kernel(slots, n, others, at_ref, *rest):
    w_hbm, s_ref, w_ref, all_ref, order_ref, sem = rest[n + 2 :]
    copy = pltpu.make_async_copy(w_hbm, w_ref, sem)
    copy.start()
    more_kernel(slots, n, others, at_ref, *rest[: n + 2], s_ref, all_ref, order_ref)
    copy.wait()


def last_kernel(at_ref, s_ref, s_2_ref, w_ref, *rest):
    outs, att_ref = rest[:6], rest[6]
    section = at_ref[1]
    for h in range(4):
        rows = slice(h * HEAD_DIM, (h + 1) * HEAD_DIM)
        tops = [r[TOP + h : TOP + h + 1, :] for r in (s_ref, s_2_ref)]
        top = jnp.maximum(*tops)
        fades = [jnp.exp(t - top) for t in tops]
        total = sum(f * r[SUM + h : SUM + h + 1, :] for f, r in zip(fades, (s_ref, s_2_ref)))
        value = sum(f * r[rows, :] for f, r in zip(fades, (s_ref, s_2_ref)))
        att_ref[:, rows] = jnp.transpose(value / total).astype(BF16)
    for sides in SIDES:
        cols = pl.ds(pl.multiple_of((section ^ away(sides)) * COLS, 128), COLS)
        part = jnp.dot(att_ref[...], w_ref[:, cols], preferred_element_type=F32).astype(BF16)
        crossed = dict(zip(LINKS, sides))
        for i, (rows, order) in enumerate(CHAINS):
            first, second, third = (crossed[step] for step in order)
            outs[2 * i + 1 - first][2 * second + third] = part[rows]


VMEM = pl.BlockSpec(memory_space=pltpu.VMEM)
SMEM = pl.BlockSpec(memory_space=pltpu.SMEM)
STATE = jax.ShapeDtypeStruct((4 * HEAD_DIM + 16, BLOCK), F32)
LAST_LIMIT = 44
LIMIT = pltpu.CompilerParams(vmem_limit_bytes=24 * 1024 * 1024)


def cost(n):
    return pl.CostEstimate(
        flops=n * 4 * 4 * BLOCK * BLOCK * HEAD_DIM,
        bytes_accessed=n * PACK * HEAD_DIM * 2,
        transcendentals=n * 4 * BLOCK * BLOCK,
    )


def per_device(hidden, k_cache, v_cache, segment, w_query, w_out):
    ctx = lax.axis_index("ctx")

    smaller = jnp.sum(
        (segment[:, None] < jnp.arange(HEAD_DIM, dtype=jnp.int32)[None, :]).astype(F32), axis=0
    ).astype(BF16)
    own = jnp.concatenate([k_cache, v_cache, jnp.broadcast_to(smaller[None, :], (16, HEAD_DIM))], axis=0)[None]

    own, other, hidden = lax.optimization_barrier((own, swap_cores(own), hidden))
    pair = lax.optimization_barrier(jnp.concatenate([own, other], axis=0))
    z_near = along_z(pair)
    y_near = along_y(pair)
    y_far = move(pair, lambda y, z, c: (y + 2, z, c) if y < 2 else None)
    z_far = move(pair[:1], lambda y, z, c: (y, z + 2, c))

    widened = hidden.astype(F32)
    normed = (widened * lax.rsqrt(jnp.mean(widened * widened, axis=-1, keepdims=True) + 1e-06)).astype(BF16)
    q_t = (
        lax.dot_general(w_query, normed, (((0,), (1,)), ((), ())), preferred_element_type=F32) * HEAD_DIM ** (-0.5)
    ).astype(BF16)
    hot = (jnp.arange(HEAD_DIM, dtype=jnp.int32)[:, None] == segment[None, :]).astype(BF16)
    q = jnp.concatenate([q_t, hot], axis=0)

    (z_near, z_far, y_near, y_far), q = lax.optimization_barrier(((z_near, z_far, y_near, y_far), q))
    row = jnp.concatenate([z_near, z_far], axis=0)
    up = up_y(row)
    around = round_y(row)
    far_near = along_z(y_far, 2)
    far_far = move(z_far, lambda y, z, c: (y + 2, z, c) if y < 2 else None)
    q_2 = swap_cores(q)

    at = jnp.stack([ctx, lax.axis_index("section")]).astype(jnp.int32)

    def attend(kernel, n, pieces, queries, states, name):
        out_shape = (STATE,) * len(queries)
        return pl.pallas_call(
            kernel,
            out_shape=out_shape,
            in_specs=[SMEM] + [VMEM] * (len(pieces) + len(queries) + len(states)),
            out_specs=(VMEM,) * len(out_shape),
            scratch_shapes=[pltpu.VMEM((n, PACK, HEAD_DIM), BF16), pltpu.SMEM((16,), jnp.int32)],
            compiler_params=LIMIT,
            cost_estimate=cost(1),
            name=name,
        )(at, *pieces, *queries, *states)

    pieces = [own, z_near, z_far, y_near, y_far]
    first = functools.partial(start_kernel, first_slots, len(pieces))
    state, state_2 = attend(first, 7, pieces, (q, q_2), (), "attend_first")
    far_near, state, state_2 = lax.optimization_barrier((far_near, state, state_2))
    far = functools.partial(more_kernel, far_slots, 1, (0, 1))
    state, state_2 = attend(far, 2, [far_near], (q, q_2), (state, state_2), "attend_far")
    pieces, state, state_2 = lax.optimization_barrier(((up, around, far_far), state, state_2))
    rest = functools.partial(more_kernel, rest_slots, len(pieces), (1,))
    (state_2,) = attend(rest, 7, pieces, (q_2,), (state_2,), "attend_rest_other")
    state_2, state = lax.optimization_barrier((state_2, state))
    state, w_held = pl.pallas_call(
        functools.partial(more_and_fetch_kernel, rest_slots, len(pieces), (0,)),
        out_shape=(STATE, jax.ShapeDtypeStruct(w_out.shape, BF16)),
        in_specs=[SMEM] + [VMEM] * (len(pieces) + 2) + [pl.BlockSpec(memory_space=pltpu.HBM)],
        out_specs=(VMEM,) * 2,
        scratch_shapes=[
            pltpu.VMEM((7, PACK, HEAD_DIM), BF16),
            pltpu.SMEM((16,), jnp.int32),
            pltpu.SemaphoreType.DMA,
        ],
        compiler_params=pltpu.CompilerParams(vmem_limit_bytes=LAST_LIMIT * 1024 * 1024),
        cost_estimate=cost(1),
        name="attend_rest_own",
    )(at, *pieces, q, state, w_out)
    state_2 = swap_cores(state_2)

    out_shape = []
    for rows, _ in CHAINS:
        out_shape += [jax.ShapeDtypeStruct((4, rows.stop - rows.start, COLS), BF16)] * 2
    outs = pl.pallas_call(
        last_kernel,
        out_shape=tuple(out_shape),
        in_specs=[SMEM, VMEM, VMEM, VMEM],
        out_specs=(VMEM,) * 6,
        scratch_shapes=[pltpu.VMEM((BLOCK, 4 * HEAD_DIM), BF16)],
        compiler_params=LIMIT,
        cost_estimate=cost(12),
        name="project_attended",
    )(at, state, state_2, w_held)

    def exchange(x, step):
        return lax.ppermute(x, "section", [(i, i ^ step) for i in range(8)])

    mixed = []
    for i, (_, (first, second, third)) in enumerate(CHAINS):
        sent, kept = outs[2 * i], outs[2 * i + 1]
        four = kept.astype(F32) + exchange(sent, first).astype(F32)
        two = four[:2] + exchange(four[2:].astype(BF16), second).astype(F32)
        mixed.append(two[0] + exchange(two[1].astype(BF16), third).astype(F32))
    return jnp.concatenate(mixed, axis=0).astype(BF16)


def solution(mesh):
    return jax.shard_map(
        per_device,
        mesh=mesh,
        in_specs=(
            P("ctx", None),
            P("ctx", "section"),
            P("ctx", "section"),
            P("ctx"),
            P(None, "section"),
            P("section", None),
        ),
        out_specs=P("ctx", "section"),
        check_vma=False,
    )
```

```python
import functools
import itertools

import jax
import jax.numpy as jnp
from jax import lax
from jax.experimental import pallas as pl
from jax.experimental.pallas import tpu as pltpu
from jax.sharding import PartitionSpec as P
import numpy as np

HEAD_DIM = 128
BLOCK = 256
PACK = 2 * BLOCK + 16
CHAINS = ((slice(0, 96), (1, 3, 4)), (slice(96, 176), (3, 4, 1)), (slice(176, 256), (4, 1, 3)))
SIDES = tuple(itertools.product((0, 1), repeat=3))
REACH = 24
COLS = 640
TOP, SUM = 4 * HEAD_DIM, 4 * HEAD_DIM + 8
HOT = slice(4 * HEAD_DIM, 5 * HEAD_DIM)
FLOOR = -1e30
HIDDEN = -2e30

F32 = jnp.float32
BF16 = jnp.bfloat16


def away(sides):
    return sum(step * side for step, side in zip((1, 3, 4), sides)) if sides[:2] != (1, 1) else 2 + 4 * sides[2]


def ctx_id(y, z, c):
    return ((y + 8) % 4) * 8 + ((z + 8) % 4) * 2 + c


def ctx_pairs(step, planes=None):
    pairs = []
    for y in range(4):
        for z in range(4):
            for c in range(2):
                to = step(y, z, c)
                if to is not None:
                    pairs.append((ctx_id(y, z, c), ctx_id(*to)))
    return pairs


def move(x, step):
    return lax.ppermute(x, "ctx", ctx_pairs(step))


def swap_cores(x):
    return move(x, lambda y, z, c: (y, z, 1 - c))


def along_z(x, first_plane=0):
    def step(y, z, c):
        return (y, z + 1 if c == 0 else z - 1, c) if y >= first_plane else None

    return move(x, step)


def along_y(x):
    def step(y, z, c):
        if c == 0:
            return (y + 1, z, c) if y < 3 else None
        return (3, z, c) if y == 0 else None

    return move(x, step)


def up_y(x):
    return move(x, lambda y, z, c: (y + 1, z, c) if y < 3 else None)


def round_y(x):
    return move(x, lambda y, z, c: (3, z, c) if y == 0 else None)


def first_slots(y, z, c):
    d = 2 * c - 1
    row = [[(y, z, c)], [(y, z + d, c), (y, z + d, 1 - c)], [(y, z + 2, c)]]
    return row + [[(y + d, z, c), (y + d, z, 1 - c)], [(y + 2, z, c)]]


def rest_slots(y, z, c):
    d = 2 * c - 1
    near = [[(y + e, z + d, c), (y + e, z + d, 1 - c), (y + e, z + 2, c)] for e in (-1, 1)]
    return near + [[(y + 2, z + d, c), (y + 2, z + d, 1 - c)], [(y + 2, z + 2, c)]]


def attend_blocks(kv_ref, places, diagonal, q_ref, state_ref):
    heads = [slice(h * HEAD_DIM, (h + 1) * HEAD_DIM) for h in range(4)]
    keys, values, visible = [], [], []
    for at in places:
        keys.append(kv_ref[at, 0:BLOCK, :])
        ones = jnp.ones((16, BLOCK), BF16)
        values.append(jnp.concatenate([jnp.transpose(kv_ref[at, BLOCK : 2 * BLOCK, :]), ones], axis=0))
        counts = kv_ref[at, 2 * BLOCK : PACK, :]
        first = jnp.dot(counts, q_ref[HOT, :], preferred_element_type=F32)[0:1, :].astype(jnp.int32)
        row = lax.broadcasted_iota(jnp.int32, (BLOCK, BLOCK), 0)
        seen = row >= first
        if diagonal:
            seen &= row <= lax.broadcasted_iota(jnp.int32, (BLOCK, BLOCK), 1)
        visible.append(seen)
    scores = [[jnp.dot(k, q_ref[rows, :], preferred_element_type=F32) for k in keys] for rows in heads]
    old = [(state_ref[TOP + h : TOP + h + 1, :], state_ref[SUM + h : SUM + h + 1, :]) for h in range(4)]
    new = []
    for h in range(4):
        masked = [jnp.where(seen, s, HIDDEN) for seen, s in zip(visible, scores[h])]
        m_old, total = old[h]
        m_new = m_old
        for s in masked:
            m_new = jnp.maximum(m_new, jnp.max(s, axis=0, keepdims=True))
        weights = [jnp.exp(s - m_new) for s in masked]
        fade = jnp.exp(m_old - m_new)
        added = sum(jnp.dot(v, p.astype(BF16), preferred_element_type=F32) for v, p in zip(values, weights))
        new.append((m_new, fade * total + added[HEAD_DIM : HEAD_DIM + 1], fade, added[:HEAD_DIM]))
    for h, rows in enumerate(heads):
        m_new, total, fade, added = new[h]
        state_ref[TOP + h : TOP + h + 1, :] = m_new
        state_ref[SUM + h : SUM + h + 1, :] = total
        state_ref[rows, :] = fade * state_ref[rows, :] + added


def where_am_i(at_ref):
    own = at_ref[0]
    return own // 8, (own // 2) % 4, own % 2


def attend_pieces(at_ref, slots, piece_refs, all_ref, order_ref, sets, others=(0, 1)):
    y, z, c = where_am_i(at_ref)
    blocks = []
    for piece_ref, places_of in zip(piece_refs, slots(y, z, c)):
        for i, place in enumerate(places_of):
            all_ref[len(blocks)] = piece_ref[i]
            blocks.append(ctx_id(*place))
    for other, q_ref, state_ref in zip(others, sets[::2], sets[1::2]):
        own = ctx_id(y, z, c + other - 2 * other * c)
        count = jnp.int32(0)
        for n, block in enumerate(blocks):
            order_ref[count] = n
            count += ((block < own) & (block >= own - REACH)).astype(jnp.int32)

        threes = count // 3

        @pl.loop(0, threes)
        def _(g, q_ref=q_ref, state_ref=state_ref):
            attend_blocks(all_ref, [order_ref[3 * g + i] for i in range(3)], False, q_ref, state_ref)

        @pl.loop(3 * threes, count)
        def _(i, q_ref=q_ref, state_ref=state_ref):
            attend_blocks(all_ref, [order_ref[i]], False, q_ref, state_ref)


def start_kernel(slots, n, at_ref, *rest):
    pieces, (q_ref, q_2_ref, s_ref, s_2_ref, all_ref, order_ref) = rest[:n], rest[n:]
    for state_ref in (s_ref, s_2_ref):
        state_ref[...] = jnp.zeros_like(state_ref)
        state_ref[TOP : TOP + 8, :] = jnp.full((8, BLOCK), FLOOR, F32)
    attend_blocks(pieces[0], [0], True, q_ref, s_ref)
    attend_pieces(at_ref, slots, pieces, all_ref, order_ref, (q_ref, s_ref, q_2_ref, s_2_ref))


def more_kernel(slots, n, other, at_ref, *rest):
    pieces, (q_ref, s_in, s_ref, all_ref, order_ref) = rest[:n], rest[n:]
    s_ref[...] = s_in[...]
    attend_pieces(at_ref, slots, pieces, all_ref, order_ref, (q_ref, s_ref), (other,))


def more_and_fetch_kernel(slots, n, other, at_ref, *rest):
    w_hbm, s_ref, w_ref, all_ref, order_ref, sem = rest[n + 2 :]
    copy = pltpu.make_async_copy(w_hbm, w_ref, sem)
    copy.start()
    more_kernel(slots, n, other, at_ref, *rest[: n + 2], s_ref, all_ref, order_ref)
    copy.wait()


def last_kernel(at_ref, s_ref, s_2_ref, w_ref, *rest):
    outs, att_ref = rest[:6], rest[6]
    section = at_ref[1]
    for h in range(4):
        rows = slice(h * HEAD_DIM, (h + 1) * HEAD_DIM)
        tops = [r[TOP + h : TOP + h + 1, :] for r in (s_ref, s_2_ref)]
        top = jnp.maximum(*tops)
        fades = [jnp.exp(t - top) for t in tops]
        total = sum(f * r[SUM + h : SUM + h + 1, :] for f, r in zip(fades, (s_ref, s_2_ref)))
        value = sum(f * r[rows, :] for f, r in zip(fades, (s_ref, s_2_ref)))
        att_ref[:, rows] = jnp.transpose(value / total).astype(BF16)
    for sides in SIDES:
        cols = pl.ds(pl.multiple_of((section ^ away(sides)) * COLS, 128), COLS)
        part = jnp.dot(att_ref[...], w_ref[:, cols], preferred_element_type=F32).astype(BF16)
        crossed = dict(zip(CHAINS[0][1], sides))
        for i, (rows, order) in enumerate(CHAINS):
            first, second, third = (crossed[step] for step in order)
            outs[2 * i + 1 - first][2 * second + third] = part[rows]


VMEM = pl.BlockSpec(memory_space=pltpu.VMEM)
SMEM = pl.BlockSpec(memory_space=pltpu.SMEM)
STATE = jax.ShapeDtypeStruct((4 * HEAD_DIM + 16, BLOCK), F32)
LAST_LIMIT = 44
LIMIT = pltpu.CompilerParams(vmem_limit_bytes=24 * 1024 * 1024)


def cost(n):
    return pl.CostEstimate(
        flops=n * 4 * 4 * BLOCK * BLOCK * HEAD_DIM,
        bytes_accessed=n * PACK * HEAD_DIM * 2,
        transcendentals=n * 4 * BLOCK * BLOCK,
    )


def per_device(hidden, k_cache, v_cache, segment, w_query, w_out):
    ctx = lax.axis_index("ctx")

    smaller = jnp.sum(
        (segment[:, None] < jnp.arange(HEAD_DIM, dtype=jnp.int32)[None, :]).astype(F32), axis=0
    ).astype(BF16)
    own = jnp.concatenate([k_cache, v_cache, jnp.broadcast_to(smaller[None, :], (16, HEAD_DIM))], axis=0)[None]

    own, other, hidden = lax.optimization_barrier((own, swap_cores(own), hidden))
    pair = lax.optimization_barrier(jnp.concatenate([own, other], axis=0))
    z_near = along_z(pair)
    y_near = along_y(pair)
    y_far = move(pair, lambda y, z, c: (y + 2, z, c) if y < 2 else None)
    z_far = move(pair[:1], lambda y, z, c: (y, z + 2, c))

    widened = hidden.astype(F32)
    normed = (widened * lax.rsqrt(jnp.mean(widened * widened, axis=-1, keepdims=True) + 1e-06)).astype(BF16)
    q_t = (
        lax.dot_general(w_query, normed, (((0,), (1,)), ((), ())), preferred_element_type=F32) * HEAD_DIM ** (-0.5)
    ).astype(BF16)
    hot = (jnp.arange(HEAD_DIM, dtype=jnp.int32)[:, None] == segment[None, :]).astype(BF16)
    q = jnp.concatenate([q_t, hot], axis=0)

    (y_far, y_near, z_far, z_near), q = lax.optimization_barrier(((y_far, y_near, z_far, z_near), q))
    row = jnp.concatenate([z_near, z_far], axis=0)
    up = up_y(row)
    around = round_y(row)
    far_near = along_z(y_far, 2)
    far_far = move(z_far, lambda y, z, c: (y + 2, z, c) if y < 2 else None)
    q_2 = swap_cores(q)

    at = jnp.stack([ctx, lax.axis_index("section")]).astype(jnp.int32)

    def attend(kernel, n, pieces, queries, states, name):
        out_shape = (STATE,) * len(queries)
        return pl.pallas_call(
            kernel,
            out_shape=out_shape,
            in_specs=[SMEM] + [VMEM] * (len(pieces) + len(queries) + len(states)),
            out_specs=(VMEM,) * len(out_shape),
            scratch_shapes=[pltpu.VMEM((n, PACK, HEAD_DIM), BF16), pltpu.SMEM((16,), jnp.int32)],
            compiler_params=LIMIT,
            cost_estimate=cost(1),
            name=name,
        )(at, *pieces, *queries, *states)

    pieces = [own, z_near, z_far, y_near, y_far]
    first = functools.partial(start_kernel, first_slots, len(pieces))
    state, state_2 = attend(first, 7, pieces, (q, q_2), (), "attend_first")
    pieces, state, state_2 = lax.optimization_barrier(((up, around, far_near, far_far), state, state_2))
    rest = functools.partial(more_kernel, rest_slots, len(pieces), 1)
    (state_2,) = attend(rest, 9, pieces, (q_2,), (state_2,), "attend_rest_other")
    state_2, state = lax.optimization_barrier((state_2, state))
    state, w_held = pl.pallas_call(
        functools.partial(more_and_fetch_kernel, rest_slots, len(pieces), 0),
        out_shape=(STATE, jax.ShapeDtypeStruct(w_out.shape, BF16)),
        in_specs=[SMEM] + [VMEM] * (len(pieces) + 2) + [pl.BlockSpec(memory_space=pltpu.HBM)],
        out_specs=(VMEM,) * 2,
        scratch_shapes=[
            pltpu.VMEM((9, PACK, HEAD_DIM), BF16),
            pltpu.SMEM((16,), jnp.int32),
            pltpu.SemaphoreType.DMA,
        ],
        compiler_params=pltpu.CompilerParams(vmem_limit_bytes=LAST_LIMIT * 1024 * 1024),
        cost_estimate=cost(1),
        name="attend_rest_own",
    )(at, *pieces, q, state, w_out)
    state_2 = swap_cores(state_2)

    out_shape = []
    for rows, _ in CHAINS:
        out_shape += [jax.ShapeDtypeStruct((4, rows.stop - rows.start, COLS), BF16)] * 2
    outs = pl.pallas_call(
        last_kernel,
        out_shape=tuple(out_shape),
        in_specs=[SMEM, VMEM, VMEM, VMEM],
        out_specs=(VMEM,) * 6,
        scratch_shapes=[pltpu.VMEM((BLOCK, 4 * HEAD_DIM), BF16)],
        compiler_params=LIMIT,
        cost_estimate=cost(12),
        name="project_attended",
    )(at, state, state_2, w_held)

    def exchange(x, step):
        return lax.ppermute(x, "section", [(i, i ^ step) for i in range(8)])

    mixed = []
    for i, (_, (first, second, third)) in enumerate(CHAINS):
        sent, kept = outs[2 * i], outs[2 * i + 1]
        four = kept.astype(F32) + exchange(sent, first).astype(F32)
        two = four[:2] + exchange(four[2:].astype(BF16), second).astype(F32)
        mixed.append(two[0] + exchange(two[1].astype(BF16), third).astype(F32))
    return jnp.concatenate(mixed, axis=0).astype(BF16)


def solution(mesh):
    return jax.shard_map(
        per_device,
        mesh=mesh,
        in_specs=(
            P("ctx", None),
            P("ctx", "section"),
            P("ctx", "section"),
            P("ctx"),
            P(None, "section"),
            P("section", None),
        ),
        out_specs=P("ctx", "section"),
        check_vma=False,
    )
```

```python
import functools
import itertools

import jax
import jax.numpy as jnp
from jax import lax
from jax.experimental import pallas as pl
from jax.experimental.pallas import tpu as pltpu
from jax.sharding import PartitionSpec as P
import numpy as np

HEAD_DIM = 128
BLOCK = 256
PACK = 2 * BLOCK + 16
CHAINS = ((slice(0, 96), (1, 3, 4)), (slice(96, 176), (3, 4, 1)), (slice(176, 256), (4, 1, 3)))
SIDES = tuple(itertools.product((0, 1), repeat=3))
REACH = 24
COLS = 640
TOP, SUM = 4 * HEAD_DIM, 4 * HEAD_DIM + 8
HOT = slice(4 * HEAD_DIM, 5 * HEAD_DIM)
FLOOR = -1e30
HIDDEN = -2e30

F32 = jnp.float32
BF16 = jnp.bfloat16


def away(sides):
    return sum(step * side for step, side in zip((1, 3, 4), sides)) if sides[:2] != (1, 1) else 2 + 4 * sides[2]


def ctx_id(y, z, c):
    return ((y + 8) % 4) * 8 + ((z + 8) % 4) * 2 + c


def ctx_pairs(step, planes=None):
    pairs = []
    for y in range(4):
        for z in range(4):
            for c in range(2):
                to = step(y, z, c)
                if to is not None:
                    pairs.append((ctx_id(y, z, c), ctx_id(*to)))
    return pairs


def move(x, step):
    return lax.ppermute(x, "ctx", ctx_pairs(step))


def swap_cores(x):
    return move(x, lambda y, z, c: (y, z, 1 - c))


def along_z(x, first_plane=0):
    def step(y, z, c):
        return (y, z + 1 if c == 0 else z - 1, c) if y >= first_plane else None

    return move(x, step)


def along_y(x):
    def step(y, z, c):
        if c == 0:
            return (y + 1, z, c) if y < 3 else None
        return (3, z, c) if y == 0 else None

    return move(x, step)


def up_y(x):
    return move(x, lambda y, z, c: (y + 1, z, c) if y < 3 else None)


def round_y(x):
    return move(x, lambda y, z, c: (3, z, c) if y == 0 else None)


def first_slots(y, z, c):
    d = 2 * c - 1
    row = [[(y, z, c)], [(y, z + d, c), (y, z + d, 1 - c)], [(y, z + 2, c)]]
    return row + [[(y + d, z, c), (y + d, z, 1 - c)], [(y + 2, z, c)]]


def up_slots(y, z, c):
    d = 2 * c - 1
    return [[(y - 1, z + d, c), (y - 1, z + d, 1 - c), (y - 1, z + 2, c)]]


def rest_slots(y, z, c):
    d = 2 * c - 1
    around = [(y + 1, z + d, c), (y + 1, z + d, 1 - c), (y + 1, z + 2, c)]
    return [around, [(y + 2, z + d, c), (y + 2, z + d, 1 - c)], [(y + 2, z + 2, c)]]


def attend_blocks(kv_ref, places, diagonal, q_ref, state_ref):
    heads = [slice(h * HEAD_DIM, (h + 1) * HEAD_DIM) for h in range(4)]
    keys, values, visible = [], [], []
    for at in places:
        keys.append(kv_ref[at, 0:BLOCK, :])
        ones = jnp.ones((16, BLOCK), BF16)
        values.append(jnp.concatenate([jnp.transpose(kv_ref[at, BLOCK : 2 * BLOCK, :]), ones], axis=0))
        counts = kv_ref[at, 2 * BLOCK : PACK, :]
        first = jnp.dot(counts, q_ref[HOT, :], preferred_element_type=F32)[0:1, :].astype(jnp.int32)
        row = lax.broadcasted_iota(jnp.int32, (BLOCK, BLOCK), 0)
        seen = row >= first
        if diagonal:
            seen &= row <= lax.broadcasted_iota(jnp.int32, (BLOCK, BLOCK), 1)
        visible.append(seen)
    scores = [[jnp.dot(k, q_ref[rows, :], preferred_element_type=F32) for k in keys] for rows in heads]
    old = [(state_ref[TOP + h : TOP + h + 1, :], state_ref[SUM + h : SUM + h + 1, :]) for h in range(4)]
    new = []
    for h in range(4):
        masked = [jnp.where(seen, s, HIDDEN) for seen, s in zip(visible, scores[h])]
        m_old, total = old[h]
        m_new = m_old
        for s in masked:
            m_new = jnp.maximum(m_new, jnp.max(s, axis=0, keepdims=True))
        weights = [jnp.exp(s - m_new) for s in masked]
        fade = jnp.exp(m_old - m_new)
        added = sum(jnp.dot(v, p.astype(BF16), preferred_element_type=F32) for v, p in zip(values, weights))
        new.append((m_new, fade * total + added[HEAD_DIM : HEAD_DIM + 1], fade, added[:HEAD_DIM]))
    for h, rows in enumerate(heads):
        m_new, total, fade, added = new[h]
        state_ref[TOP + h : TOP + h + 1, :] = m_new
        state_ref[SUM + h : SUM + h + 1, :] = total
        state_ref[rows, :] = fade * state_ref[rows, :] + added


def where_am_i(at_ref):
    own = at_ref[0]
    return own // 8, (own // 2) % 4, own % 2


def attend_pieces(at_ref, slots, piece_refs, all_ref, order_ref, sets, others=(0, 1)):
    y, z, c = where_am_i(at_ref)
    blocks = []
    for piece_ref, places_of in zip(piece_refs, slots(y, z, c)):
        for i, place in enumerate(places_of):
            all_ref[len(blocks)] = piece_ref[i]
            blocks.append(ctx_id(*place))
    for other, q_ref, state_ref in zip(others, sets[::2], sets[1::2]):
        own = ctx_id(y, z, c + other - 2 * other * c)
        count = jnp.int32(0)
        for n, block in enumerate(blocks):
            order_ref[count] = n
            count += ((block < own) & (block >= own - REACH)).astype(jnp.int32)

        threes = count // 3

        @pl.loop(0, threes)
        def _(g, q_ref=q_ref, state_ref=state_ref):
            attend_blocks(all_ref, [order_ref[3 * g + i] for i in range(3)], False, q_ref, state_ref)

        @pl.loop(3 * threes, count)
        def _(i, q_ref=q_ref, state_ref=state_ref):
            attend_blocks(all_ref, [order_ref[i]], False, q_ref, state_ref)


def start_kernel(slots, n, at_ref, *rest):
    pieces, (q_ref, q_2_ref, s_ref, s_2_ref, all_ref, order_ref) = rest[:n], rest[n:]
    for state_ref in (s_ref, s_2_ref):
        state_ref[...] = jnp.zeros_like(state_ref)
        state_ref[TOP : TOP + 8, :] = jnp.full((8, BLOCK), FLOOR, F32)
    attend_blocks(pieces[0], [0], True, q_ref, s_ref)
    attend_pieces(at_ref, slots, pieces, all_ref, order_ref, (q_ref, s_ref, q_2_ref, s_2_ref))


def more_kernel(slots, n, others, at_ref, *rest):
    k = len(others)
    pieces, queries, before, after = rest[:n], rest[n : n + k], rest[n + k : n + 2 * k], rest[n + 2 * k : n + 3 * k]
    all_ref, order_ref = rest[n + 3 * k :]
    for s_in, s_ref in zip(before, after):
        s_ref[...] = s_in[...]
    sets = [ref for pair in zip(queries, after) for ref in pair]
    attend_pieces(at_ref, slots, pieces, all_ref, order_ref, sets, others)


def more_and_fetch_kernel(slots, n, others, at_ref, *rest):
    w_hbm, s_ref, w_ref, all_ref, order_ref, sem = rest[n + 2 :]
    copy = pltpu.make_async_copy(w_hbm, w_ref, sem)
    copy.start()
    more_kernel(slots, n, others, at_ref, *rest[: n + 2], s_ref, all_ref, order_ref)
    copy.wait()


def last_kernel(at_ref, s_ref, s_2_ref, w_ref, *rest):
    outs, att_ref = rest[:6], rest[6]
    section = at_ref[1]
    for h in range(4):
        rows = slice(h * HEAD_DIM, (h + 1) * HEAD_DIM)
        tops = [r[TOP + h : TOP + h + 1, :] for r in (s_ref, s_2_ref)]
        top = jnp.maximum(*tops)
        fades = [jnp.exp(t - top) for t in tops]
        total = sum(f * r[SUM + h : SUM + h + 1, :] for f, r in zip(fades, (s_ref, s_2_ref)))
        value = sum(f * r[rows, :] for f, r in zip(fades, (s_ref, s_2_ref)))
        att_ref[:, rows] = jnp.transpose(value / total).astype(BF16)
    for sides in SIDES:
        cols = pl.ds(pl.multiple_of((section ^ away(sides)) * COLS, 128), COLS)
        part = jnp.dot(att_ref[...], w_ref[:, cols], preferred_element_type=F32).astype(BF16)
        crossed = dict(zip(CHAINS[0][1], sides))
        for i, (rows, order) in enumerate(CHAINS):
            first, second, third = (crossed[step] for step in order)
            outs[2 * i + 1 - first][2 * second + third] = part[rows]


VMEM = pl.BlockSpec(memory_space=pltpu.VMEM)
SMEM = pl.BlockSpec(memory_space=pltpu.SMEM)
STATE = jax.ShapeDtypeStruct((4 * HEAD_DIM + 16, BLOCK), F32)
LAST_LIMIT = 44
LIMIT = pltpu.CompilerParams(vmem_limit_bytes=24 * 1024 * 1024)


def cost(n):
    return pl.CostEstimate(
        flops=n * 4 * 4 * BLOCK * BLOCK * HEAD_DIM,
        bytes_accessed=n * PACK * HEAD_DIM * 2,
        transcendentals=n * 4 * BLOCK * BLOCK,
    )


def per_device(hidden, k_cache, v_cache, segment, w_query, w_out):
    ctx = lax.axis_index("ctx")

    smaller = jnp.sum(
        (segment[:, None] < jnp.arange(HEAD_DIM, dtype=jnp.int32)[None, :]).astype(F32), axis=0
    ).astype(BF16)
    own = jnp.concatenate([k_cache, v_cache, jnp.broadcast_to(smaller[None, :], (16, HEAD_DIM))], axis=0)[None]

    own, other, hidden = lax.optimization_barrier((own, swap_cores(own), hidden))
    pair = jnp.concatenate([own, other], axis=0)
    z_near = along_z(pair)
    y_near = along_y(pair)
    y_far = move(pair, lambda y, z, c: (y + 2, z, c) if y < 2 else None)
    z_far = move(own, lambda y, z, c: (y, z + 2, c))

    widened = hidden.astype(F32)
    normed = (widened * lax.rsqrt(jnp.mean(widened * widened, axis=-1, keepdims=True) + 1e-06)).astype(BF16)
    q_t = (
        lax.dot_general(w_query, normed, (((0,), (1,)), ((), ())), preferred_element_type=F32) * HEAD_DIM ** (-0.5)
    ).astype(BF16)
    hot = (jnp.arange(HEAD_DIM, dtype=jnp.int32)[:, None] == segment[None, :]).astype(BF16)
    q = jnp.concatenate([q_t, hot], axis=0)

    (z_near, z_far, y_near, y_far), q = lax.optimization_barrier(((z_near, z_far, y_near, y_far), q))
    row = jnp.concatenate([z_near, z_far], axis=0)
    up = up_y(row)
    around = round_y(row)
    far_near = along_z(y_far, 2)
    far_far = move(z_far, lambda y, z, c: (y + 2, z, c) if y < 2 else None)
    q_2 = swap_cores(q)

    at = jnp.stack([ctx, lax.axis_index("section")]).astype(jnp.int32)

    def attend(kernel, n, pieces, queries, states, name):
        out_shape = (STATE,) * len(queries)
        return pl.pallas_call(
            kernel,
            out_shape=out_shape,
            in_specs=[SMEM] + [VMEM] * (len(pieces) + len(queries) + len(states)),
            out_specs=(VMEM,) * len(out_shape),
            scratch_shapes=[pltpu.VMEM((n, PACK, HEAD_DIM), BF16), pltpu.SMEM((16,), jnp.int32)],
            compiler_params=LIMIT,
            cost_estimate=cost(1),
            name=name,
        )(at, *pieces, *queries, *states)

    pieces = [own, z_near, z_far, y_near, y_far]
    first = functools.partial(start_kernel, first_slots, len(pieces))
    state, state_2 = attend(first, 7, pieces, (q, q_2), (), "attend_first")
    up, state, state_2 = lax.optimization_barrier((up, state, state_2))
    near = functools.partial(more_kernel, up_slots, 1, (0, 1))
    state, state_2 = attend(near, 3, [up], (q, q_2), (state, state_2), "attend_up")
    pieces, state, state_2 = lax.optimization_barrier(((around, far_near, far_far), state, state_2))
    rest = functools.partial(more_kernel, rest_slots, len(pieces), (1,))
    (state_2,) = attend(rest, 6, pieces, (q_2,), (state_2,), "attend_rest_other")
    state_2, state = lax.optimization_barrier((state_2, state))
    state, w_held = pl.pallas_call(
        functools.partial(more_and_fetch_kernel, rest_slots, len(pieces), (0,)),
        out_shape=(STATE, jax.ShapeDtypeStruct(w_out.shape, BF16)),
        in_specs=[SMEM] + [VMEM] * (len(pieces) + 2) + [pl.BlockSpec(memory_space=pltpu.HBM)],
        out_specs=(VMEM,) * 2,
        scratch_shapes=[
            pltpu.VMEM((6, PACK, HEAD_DIM), BF16),
            pltpu.SMEM((16,), jnp.int32),
            pltpu.SemaphoreType.DMA,
        ],
        compiler_params=pltpu.CompilerParams(vmem_limit_bytes=LAST_LIMIT * 1024 * 1024),
        cost_estimate=cost(1),
        name="attend_rest_own",
    )(at, *pieces, q, state, w_out)
    state_2 = swap_cores(state_2)

    out_shape = []
    for rows, _ in CHAINS:
        out_shape += [jax.ShapeDtypeStruct((4, rows.stop - rows.start, COLS), BF16)] * 2
    outs = pl.pallas_call(
        last_kernel,
        out_shape=tuple(out_shape),
        in_specs=[SMEM, VMEM, VMEM, VMEM],
        out_specs=(VMEM,) * 6,
        scratch_shapes=[pltpu.VMEM((BLOCK, 4 * HEAD_DIM), BF16)],
        compiler_params=LIMIT,
        cost_estimate=cost(12),
        name="project_attended",
    )(at, state, state_2, w_held)

    def exchange(x, step):
        return lax.ppermute(x, "section", [(i, i ^ step) for i in range(8)])

    mixed = []
    for i, (_, (first, second, third)) in enumerate(CHAINS):
        sent, kept = outs[2 * i], outs[2 * i + 1]
        four = kept.astype(F32) + exchange(sent, first).astype(F32)
        two = four[:2] + exchange(four[2:].astype(BF16), second).astype(F32)
        mixed.append(two[0] + exchange(two[1].astype(BF16), third).astype(F32))
    return jnp.concatenate(mixed, axis=0).astype(BF16)


def solution(mesh):
    return jax.shard_map(
        per_device,
        mesh=mesh,
        in_specs=(
            P("ctx", None),
            P("ctx", "section"),
            P("ctx", "section"),
            P("ctx"),
            P(None, "section"),
            P("section", None),
        ),
        out_specs=P("ctx", "section"),
        check_vma=False,
    )
```

```python
import functools
import itertools

import jax
import jax.numpy as jnp
from jax import lax
from jax.experimental import pallas as pl
from jax.experimental.pallas import tpu as pltpu
from jax.sharding import PartitionSpec as P
import numpy as np

HEAD_DIM = 128
BLOCK = 256
PACK = 2 * BLOCK + 16
CHAINS = ((slice(0, 96), (1, 3, 4)), (slice(96, 176), (3, 4, 1)), (slice(176, 256), (4, 1, 3)))
SIDES = tuple(itertools.product((0, 1), repeat=3))
REACH = 24
COLS = 640
TOP, SUM = 4 * HEAD_DIM, 4 * HEAD_DIM + 8
HOT = slice(4 * HEAD_DIM, 5 * HEAD_DIM)
FLOOR = -1e30
HIDDEN = -2e30

F32 = jnp.float32
BF16 = jnp.bfloat16


def away(sides):
    return sum(step * side for step, side in zip((1, 3, 4), sides)) if sides[:2] != (1, 1) else 2 + 4 * sides[2]


def ctx_id(y, z, c):
    return ((y + 8) % 4) * 8 + ((z + 8) % 4) * 2 + c


def ctx_pairs(step, planes=None):
    pairs = []
    for y in range(4):
        for z in range(4):
            for c in range(2):
                to = step(y, z, c)
                if to is not None:
                    pairs.append((ctx_id(y, z, c), ctx_id(*to)))
    return pairs


def move(x, step):
    return lax.ppermute(x, "ctx", ctx_pairs(step))


def swap_cores(x):
    return move(x, lambda y, z, c: (y, z, 1 - c))


def along_z(x, first_plane=0):
    def step(y, z, c):
        return (y, z + 1 if c == 0 else z - 1, c) if y >= first_plane else None

    return move(x, step)


def along_y(x):
    def step(y, z, c):
        if c == 0:
            return (y + 1, z, c) if y < 3 else None
        return (3, z, c) if y == 0 else None

    return move(x, step)


def up_y(x):
    return move(x, lambda y, z, c: (y + 1, z, c) if y < 3 else None)


def round_y(x):
    return move(x, lambda y, z, c: (3, z, c) if y == 0 else None)


def first_slots(y, z, c):
    d = 2 * c - 1
    row = [[(y, z, c)], [(y, z + d, c), (y, z + d, 1 - c)], [(y, z + 2, c)]]
    return row + [[(y + d, z, c), (y + d, z, 1 - c)], [(y + 2, z, c)]]


def up_slots(y, z, c):
    d = 2 * c - 1
    return [[(y - 1, z + d, c), (y - 1, z + d, 1 - c), (y - 1, z + 2, c)]]


def rest_slots(y, z, c):
    d = 2 * c - 1
    return [[(y + 1, z + d, c), (y + 1, z + d, 1 - c), (y + 1, z + 2, c)]]


def far_slots(y, z, c):
    d = 2 * c - 1
    return [[(y + 2, z + d, c), (y + 2, z + d, 1 - c)], [(y + 2, z + 2, c)]]


def attend_blocks(kv_ref, places, diagonal, q_ref, state_ref):
    heads = [slice(h * HEAD_DIM, (h + 1) * HEAD_DIM) for h in range(4)]
    keys, values, visible = [], [], []
    for at in places:
        keys.append(kv_ref[at, 0:BLOCK, :])
        ones = jnp.ones((16, BLOCK), BF16)
        values.append(jnp.concatenate([jnp.transpose(kv_ref[at, BLOCK : 2 * BLOCK, :]), ones], axis=0))
        counts = kv_ref[at, 2 * BLOCK : PACK, :]
        first = jnp.dot(counts, q_ref[HOT, :], preferred_element_type=F32)[0:1, :].astype(jnp.int32)
        row = lax.broadcasted_iota(jnp.int32, (BLOCK, BLOCK), 0)
        seen = row >= first
        if diagonal:
            seen &= row <= lax.broadcasted_iota(jnp.int32, (BLOCK, BLOCK), 1)
        visible.append(seen)
    scores = [[jnp.dot(k, q_ref[rows, :], preferred_element_type=F32) for k in keys] for rows in heads]
    old = [(state_ref[TOP + h : TOP + h + 1, :], state_ref[SUM + h : SUM + h + 1, :]) for h in range(4)]
    new = []
    for h in range(4):
        masked = [jnp.where(seen, s, HIDDEN) for seen, s in zip(visible, scores[h])]
        m_old, total = old[h]
        m_new = m_old
        for s in masked:
            m_new = jnp.maximum(m_new, jnp.max(s, axis=0, keepdims=True))
        weights = [jnp.exp(s - m_new) for s in masked]
        fade = jnp.exp(m_old - m_new)
        added = sum(jnp.dot(v, p.astype(BF16), preferred_element_type=F32) for v, p in zip(values, weights))
        new.append((m_new, fade * total + added[HEAD_DIM : HEAD_DIM + 1], fade, added[:HEAD_DIM]))
    for h, rows in enumerate(heads):
        m_new, total, fade, added = new[h]
        state_ref[TOP + h : TOP + h + 1, :] = m_new
        state_ref[SUM + h : SUM + h + 1, :] = total
        state_ref[rows, :] = fade * state_ref[rows, :] + added


def where_am_i(at_ref):
    own = at_ref[0]
    return own // 8, (own // 2) % 4, own % 2


def attend_pieces(at_ref, slots, piece_refs, all_ref, order_ref, sets, others=(0, 1)):
    y, z, c = where_am_i(at_ref)
    blocks = []
    for piece_ref, places_of in zip(piece_refs, slots(y, z, c)):
        for i, place in enumerate(places_of):
            all_ref[len(blocks)] = piece_ref[i]
            blocks.append(ctx_id(*place))
    for other, q_ref, state_ref in zip(others, sets[::2], sets[1::2]):
        own = ctx_id(y, z, c + other - 2 * other * c)
        count = jnp.int32(0)
        for n, block in enumerate(blocks):
            order_ref[count] = n
            count += ((block < own) & (block >= own - REACH)).astype(jnp.int32)

        threes = count // 3

        @pl.loop(0, threes)
        def _(g, q_ref=q_ref, state_ref=state_ref):
            attend_blocks(all_ref, [order_ref[3 * g + i] for i in range(3)], False, q_ref, state_ref)

        @pl.loop(3 * threes, count)
        def _(i, q_ref=q_ref, state_ref=state_ref):
            attend_blocks(all_ref, [order_ref[i]], False, q_ref, state_ref)


def start_kernel(slots, n, at_ref, *rest):
    pieces, (q_ref, q_2_ref, s_ref, s_2_ref, all_ref, order_ref) = rest[:n], rest[n:]
    for state_ref in (s_ref, s_2_ref):
        state_ref[...] = jnp.zeros_like(state_ref)
        state_ref[TOP : TOP + 8, :] = jnp.full((8, BLOCK), FLOOR, F32)
    attend_blocks(pieces[0], [0], True, q_ref, s_ref)
    attend_pieces(at_ref, slots, pieces, all_ref, order_ref, (q_ref, s_ref, q_2_ref, s_2_ref))


def more_kernel(slots, n, others, at_ref, *rest):
    k = len(others)
    pieces, queries, before, after = rest[:n], rest[n : n + k], rest[n + k : n + 2 * k], rest[n + 2 * k : n + 3 * k]
    all_ref, order_ref = rest[n + 3 * k :]
    for s_in, s_ref in zip(before, after):
        s_ref[...] = s_in[...]
    sets = [ref for pair in zip(queries, after) for ref in pair]
    attend_pieces(at_ref, slots, pieces, all_ref, order_ref, sets, others)


def more_and_fetch_kernel(slots, n, others, at_ref, *rest):
    w_hbm, s_ref, w_ref, all_ref, order_ref, sem = rest[n + 2 :]
    copy = pltpu.make_async_copy(w_hbm, w_ref, sem)
    copy.start()
    more_kernel(slots, n, others, at_ref, *rest[: n + 2], s_ref, all_ref, order_ref)
    copy.wait()


def last_kernel(at_ref, s_ref, s_2_ref, w_ref, *rest):
    outs, att_ref = rest[:6], rest[6]
    section = at_ref[1]
    for h in range(4):
        rows = slice(h * HEAD_DIM, (h + 1) * HEAD_DIM)
        tops = [r[TOP + h : TOP + h + 1, :] for r in (s_ref, s_2_ref)]
        top = jnp.maximum(*tops)
        fades = [jnp.exp(t - top) for t in tops]
        total = sum(f * r[SUM + h : SUM + h + 1, :] for f, r in zip(fades, (s_ref, s_2_ref)))
        value = sum(f * r[rows, :] for f, r in zip(fades, (s_ref, s_2_ref)))
        att_ref[:, rows] = jnp.transpose(value / total).astype(BF16)
    for sides in SIDES:
        cols = pl.ds(pl.multiple_of((section ^ away(sides)) * COLS, 128), COLS)
        part = jnp.dot(att_ref[...], w_ref[:, cols], preferred_element_type=F32).astype(BF16)
        crossed = dict(zip(CHAINS[0][1], sides))
        for i, (rows, order) in enumerate(CHAINS):
            first, second, third = (crossed[step] for step in order)
            outs[2 * i + 1 - first][2 * second + third] = part[rows]


VMEM = pl.BlockSpec(memory_space=pltpu.VMEM)
SMEM = pl.BlockSpec(memory_space=pltpu.SMEM)
STATE = jax.ShapeDtypeStruct((4 * HEAD_DIM + 16, BLOCK), F32)
LAST_LIMIT = 44
LIMIT = pltpu.CompilerParams(vmem_limit_bytes=24 * 1024 * 1024)


def cost(n):
    return pl.CostEstimate(
        flops=n * 4 * 4 * BLOCK * BLOCK * HEAD_DIM,
        bytes_accessed=n * PACK * HEAD_DIM * 2,
        transcendentals=n * 4 * BLOCK * BLOCK,
    )


def per_device(hidden, k_cache, v_cache, segment, w_query, w_out):
    ctx = lax.axis_index("ctx")

    smaller = jnp.sum(
        (segment[:, None] < jnp.arange(HEAD_DIM, dtype=jnp.int32)[None, :]).astype(F32), axis=0
    ).astype(BF16)
    own = jnp.concatenate([k_cache, v_cache, jnp.broadcast_to(smaller[None, :], (16, HEAD_DIM))], axis=0)[None]

    own, other, hidden = lax.optimization_barrier((own, swap_cores(own), hidden))
    pair = jnp.concatenate([own, other], axis=0)
    z_near = along_z(pair)
    y_near = along_y(pair)
    y_far = move(pair, lambda y, z, c: (y + 2, z, c) if y < 2 else None)
    z_far = move(own, lambda y, z, c: (y, z + 2, c))

    widened = hidden.astype(F32)
    normed = (widened * lax.rsqrt(jnp.mean(widened * widened, axis=-1, keepdims=True) + 1e-06)).astype(BF16)
    q_t = (
        lax.dot_general(w_query, normed, (((0,), (1,)), ((), ())), preferred_element_type=F32) * HEAD_DIM ** (-0.5)
    ).astype(BF16)
    hot = (jnp.arange(HEAD_DIM, dtype=jnp.int32)[:, None] == segment[None, :]).astype(BF16)
    q = jnp.concatenate([q_t, hot], axis=0)

    (z_near, z_far, y_near, y_far), q = lax.optimization_barrier(((z_near, z_far, y_near, y_far), q))
    row = jnp.concatenate([z_near, z_far], axis=0)
    up = up_y(row)
    around = round_y(row)
    far_near = along_z(y_far, 2)
    far_far = move(z_far, lambda y, z, c: (y + 2, z, c) if y < 2 else None)
    q_2 = swap_cores(q)

    at = jnp.stack([ctx, lax.axis_index("section")]).astype(jnp.int32)

    def attend(kernel, n, pieces, queries, states, name):
        out_shape = (STATE,) * len(queries)
        return pl.pallas_call(
            kernel,
            out_shape=out_shape,
            in_specs=[SMEM] + [VMEM] * (len(pieces) + len(queries) + len(states)),
            out_specs=(VMEM,) * len(out_shape),
            scratch_shapes=[pltpu.VMEM((n, PACK, HEAD_DIM), BF16), pltpu.SMEM((16,), jnp.int32)],
            compiler_params=LIMIT,
            cost_estimate=cost(1),
            name=name,
        )(at, *pieces, *queries, *states)

    pieces = [own, z_near, z_far, y_near, y_far]
    first = functools.partial(start_kernel, first_slots, len(pieces))
    state, state_2 = attend(first, 7, pieces, (q, q_2), (), "attend_first")
    up, state, state_2 = lax.optimization_barrier((up, state, state_2))
    near = functools.partial(more_kernel, up_slots, 1, (0, 1))
    state, state_2 = attend(near, 3, [up], (q, q_2), (state, state_2), "attend_up")
    fars, state, state_2 = lax.optimization_barrier(((far_near, far_far), state, state_2))
    far = functools.partial(more_kernel, far_slots, 2, (0, 1))
    state, state_2 = attend(far, 3, fars, (q, q_2), (state, state_2), "attend_far")
    pieces, state, state_2 = lax.optimization_barrier(((around,), state, state_2))
    rest = functools.partial(more_kernel, rest_slots, len(pieces), (1,))
    (state_2,) = attend(rest, 3, pieces, (q_2,), (state_2,), "attend_rest_other")
    state_2, state = lax.optimization_barrier((state_2, state))
    state, w_held = pl.pallas_call(
        functools.partial(more_and_fetch_kernel, rest_slots, len(pieces), (0,)),
        out_shape=(STATE, jax.ShapeDtypeStruct(w_out.shape, BF16)),
        in_specs=[SMEM] + [VMEM] * (len(pieces) + 2) + [pl.BlockSpec(memory_space=pltpu.HBM)],
        out_specs=(VMEM,) * 2,
        scratch_shapes=[
            pltpu.VMEM((3, PACK, HEAD_DIM), BF16),
            pltpu.SMEM((16,), jnp.int32),
            pltpu.SemaphoreType.DMA,
        ],
        compiler_params=pltpu.CompilerParams(vmem_limit_bytes=LAST_LIMIT * 1024 * 1024),
        cost_estimate=cost(1),
        name="attend_rest_own",
    )(at, *pieces, q, state, w_out)
    state_2 = swap_cores(state_2)

    out_shape = []
    for rows, _ in CHAINS:
        out_shape += [jax.ShapeDtypeStruct((4, rows.stop - rows.start, COLS), BF16)] * 2
    outs = pl.pallas_call(
        last_kernel,
        out_shape=tuple(out_shape),
        in_specs=[SMEM, VMEM, VMEM, VMEM],
        out_specs=(VMEM,) * 6,
        scratch_shapes=[pltpu.VMEM((BLOCK, 4 * HEAD_DIM), BF16)],
        compiler_params=LIMIT,
        cost_estimate=cost(12),
        name="project_attended",
    )(at, state, state_2, w_held)

    def exchange(x, step):
        return lax.ppermute(x, "section", [(i, i ^ step) for i in range(8)])

    mixed = []
    for i, (_, (first, second, third)) in enumerate(CHAINS):
        sent, kept = outs[2 * i], outs[2 * i + 1]
        four = kept.astype(F32) + exchange(sent, first).astype(F32)
        two = four[:2] + exchange(four[2:].astype(BF16), second).astype(F32)
        mixed.append(two[0] + exchange(two[1].astype(BF16), third).astype(F32))
    return jnp.concatenate(mixed, axis=0).astype(BF16)


def solution(mesh):
    return jax.shard_map(
        per_device,
        mesh=mesh,
        in_specs=(
            P("ctx", None),
            P("ctx", "section"),
            P("ctx", "section"),
            P("ctx"),
            P(None, "section"),
            P("section", None),
        ),
        out_specs=P("ctx", "section"),
        check_vma=False,
    )
```

```python
import functools
import itertools

import jax
import jax.numpy as jnp
from jax import lax
from jax.experimental import pallas as pl
from jax.experimental.pallas import tpu as pltpu
from jax.sharding import PartitionSpec as P
import numpy as np

HEAD_DIM = 128
BLOCK = 256
PACK = 2 * BLOCK + 16
CHAINS = ((slice(0, 96), (1, 3, 4)), (slice(96, 176), (3, 4, 1)), (slice(176, 256), (4, 1, 3)))
SIDES = tuple(itertools.product((0, 1), repeat=3))
REACH = 24
COLS = 640
TOP, SUM = 4 * HEAD_DIM, 4 * HEAD_DIM + 8
HOT = slice(4 * HEAD_DIM, 5 * HEAD_DIM)
FLOOR = -1e30
HIDDEN = -2e30

F32 = jnp.float32
BF16 = jnp.bfloat16


def away(sides):
    return sum(step * side for step, side in zip((1, 3, 4), sides)) if sides[:2] != (1, 1) else 2 + 4 * sides[2]


def ctx_id(y, z, c):
    return ((y + 8) % 4) * 8 + ((z + 8) % 4) * 2 + c


def ctx_pairs(step, planes=None):
    pairs = []
    for y in range(4):
        for z in range(4):
            for c in range(2):
                to = step(y, z, c)
                if to is not None:
                    pairs.append((ctx_id(y, z, c), ctx_id(*to)))
    return pairs


def move(x, step):
    return lax.ppermute(x, "ctx", ctx_pairs(step))


def swap_cores(x):
    return move(x, lambda y, z, c: (y, z, 1 - c))


def along_z(x, first_plane=0):
    def step(y, z, c):
        return (y, z + 1 if c == 0 else z - 1, c) if y >= first_plane else None

    return move(x, step)


def along_y(x):
    def step(y, z, c):
        if c == 0:
            return (y + 1, z, c) if y < 3 else None
        return (3, z, c) if y == 0 else None

    return move(x, step)


def up_y(x):
    return move(x, lambda y, z, c: (y + 1, z, c) if y < 3 else None)


def round_y(x):
    return move(x, lambda y, z, c: (3, z, c) if y == 0 else None)


def first_slots(y, z, c):
    d = 2 * c - 1
    row = [[(y, z, c)], [(y, z + d, c), (y, z + d, 1 - c)], [(y, z + 2, c)]]
    return row + [[(y + d, z, c), (y + d, z, 1 - c)], [(y + 2, z, c)]]


def up_slots(y, z, c):
    d = 2 * c - 1
    return [[(y - 1, z + d, c), (y - 1, z + d, 1 - c), (y - 1, z + 2, c)]]


def rest_slots(y, z, c):
    d = 2 * c - 1
    return [[(y + 1, z + d, c), (y + 1, z + d, 1 - c), (y + 1, z + 2, c)]]


def far_slots(y, z, c):
    d = 2 * c - 1
    return [[(y + 2, z + d, c), (y + 2, z + d, 1 - c)], [(y + 2, z + 2, c)]]


def attend_blocks(kv_ref, places, diagonal, q_ref, state_ref):
    heads = [slice(h * HEAD_DIM, (h + 1) * HEAD_DIM) for h in range(4)]
    keys, values, visible = [], [], []
    for at in places:
        keys.append(kv_ref[at, 0:BLOCK, :])
        ones = jnp.ones((16, BLOCK), BF16)
        values.append(jnp.concatenate([jnp.transpose(kv_ref[at, BLOCK : 2 * BLOCK, :]), ones], axis=0))
        counts = kv_ref[at, 2 * BLOCK : PACK, :]
        first = jnp.dot(counts, q_ref[HOT, :], preferred_element_type=F32)[0:1, :].astype(jnp.int32)
        row = lax.broadcasted_iota(jnp.int32, (BLOCK, BLOCK), 0)
        seen = row >= first
        if diagonal:
            seen &= row <= lax.broadcasted_iota(jnp.int32, (BLOCK, BLOCK), 1)
        visible.append(seen)
    scores = [[jnp.dot(k, q_ref[rows, :], preferred_element_type=F32) for k in keys] for rows in heads]
    old = [(state_ref[TOP + h : TOP + h + 1, :], state_ref[SUM + h : SUM + h + 1, :]) for h in range(4)]
    new = []
    for h in range(4):
        masked = [jnp.where(seen, s, HIDDEN) for seen, s in zip(visible, scores[h])]
        m_old, total = old[h]
        m_new = m_old
        for s in masked:
            m_new = jnp.maximum(m_new, jnp.max(s, axis=0, keepdims=True))
        weights = [jnp.exp(s - m_new) for s in masked]
        fade = jnp.exp(m_old - m_new)
        added = sum(jnp.dot(v, p.astype(BF16), preferred_element_type=F32) for v, p in zip(values, weights))
        new.append((m_new, fade * total + added[HEAD_DIM : HEAD_DIM + 1], fade, added[:HEAD_DIM]))
    for h, rows in enumerate(heads):
        m_new, total, fade, added = new[h]
        state_ref[TOP + h : TOP + h + 1, :] = m_new
        state_ref[SUM + h : SUM + h + 1, :] = total
        state_ref[rows, :] = fade * state_ref[rows, :] + added


def where_am_i(at_ref):
    own = at_ref[0]
    return own // 8, (own // 2) % 4, own % 2


def attend_pieces(at_ref, slots, piece_refs, all_ref, order_ref, sets, others=(0, 1)):
    y, z, c = where_am_i(at_ref)
    blocks = []
    for piece_ref, places_of in zip(piece_refs, slots(y, z, c)):
        for i, place in enumerate(places_of):
            all_ref[len(blocks)] = piece_ref[i]
            blocks.append(ctx_id(*place))
    for other, q_ref, state_ref in zip(others, sets[::2], sets[1::2]):
        own = ctx_id(y, z, c + other - 2 * other * c)
        count = jnp.int32(0)
        for n, block in enumerate(blocks):
            order_ref[count] = n
            count += ((block < own) & (block >= own - REACH)).astype(jnp.int32)

        threes = count // 3

        @pl.loop(0, threes)
        def _(g, q_ref=q_ref, state_ref=state_ref):
            attend_blocks(all_ref, [order_ref[3 * g + i] for i in range(3)], False, q_ref, state_ref)

        @pl.loop(3 * threes, count)
        def _(i, q_ref=q_ref, state_ref=state_ref):
            attend_blocks(all_ref, [order_ref[i]], False, q_ref, state_ref)


def start_kernel(slots, n, at_ref, *rest):
    pieces, (q_ref, q_2_ref, s_ref, s_2_ref, all_ref, order_ref) = rest[:n], rest[n:]
    for state_ref in (s_ref, s_2_ref):
        state_ref[...] = jnp.zeros_like(state_ref)
        state_ref[TOP : TOP + 8, :] = jnp.full((8, BLOCK), FLOOR, F32)
    attend_blocks(pieces[0], [0], True, q_ref, s_ref)
    attend_pieces(at_ref, slots, pieces, all_ref, order_ref, (q_ref, s_ref, q_2_ref, s_2_ref))


def more_kernel(slots, n, others, at_ref, *rest):
    k = len(others)
    pieces, queries, before, after = rest[:n], rest[n : n + k], rest[n + k : n + 2 * k], rest[n + 2 * k : n + 3 * k]
    all_ref, order_ref = rest[n + 3 * k :]
    for s_in, s_ref in zip(before, after):
        s_ref[...] = s_in[...]
    sets = [ref for pair in zip(queries, after) for ref in pair]
    attend_pieces(at_ref, slots, pieces, all_ref, order_ref, sets, others)


def more_and_fetch_kernel(slots, n, others, at_ref, *rest):
    given = n + 2 * len(others)
    w_hbm, (w_ref, all_ref, order_ref, sem) = rest[given], rest[-4:]
    copy = pltpu.make_async_copy(w_hbm, w_ref, sem)
    copy.start()
    more_kernel(slots, n, others, at_ref, *rest[:given], *rest[given + 1 : -4], all_ref, order_ref)
    copy.wait()


def last_kernel(at_ref, s_ref, s_2_ref, w_ref, *rest):
    outs, att_ref = rest[:6], rest[6]
    section = at_ref[1]
    for h in range(4):
        rows = slice(h * HEAD_DIM, (h + 1) * HEAD_DIM)
        tops = [r[TOP + h : TOP + h + 1, :] for r in (s_ref, s_2_ref)]
        top = jnp.maximum(*tops)
        fades = [jnp.exp(t - top) for t in tops]
        total = sum(f * r[SUM + h : SUM + h + 1, :] for f, r in zip(fades, (s_ref, s_2_ref)))
        value = sum(f * r[rows, :] for f, r in zip(fades, (s_ref, s_2_ref)))
        att_ref[:, rows] = jnp.transpose(value / total).astype(BF16)
    for sides in SIDES:
        cols = pl.ds(pl.multiple_of((section ^ away(sides)) * COLS, 128), COLS)
        part = jnp.dot(att_ref[...], w_ref[:, cols], preferred_element_type=F32).astype(BF16)
        crossed = dict(zip(CHAINS[0][1], sides))
        for i, (rows, order) in enumerate(CHAINS):
            first, second, third = (crossed[step] for step in order)
            outs[2 * i + 1 - first][2 * second + third] = part[rows]


VMEM = pl.BlockSpec(memory_space=pltpu.VMEM)
SMEM = pl.BlockSpec(memory_space=pltpu.SMEM)
STATE = jax.ShapeDtypeStruct((4 * HEAD_DIM + 16, BLOCK), F32)
LAST_LIMIT = 44
LIMIT = pltpu.CompilerParams(vmem_limit_bytes=24 * 1024 * 1024)


def cost(n):
    return pl.CostEstimate(
        flops=n * 4 * 4 * BLOCK * BLOCK * HEAD_DIM,
        bytes_accessed=n * PACK * HEAD_DIM * 2,
        transcendentals=n * 4 * BLOCK * BLOCK,
    )


def per_device(hidden, k_cache, v_cache, segment, w_query, w_out):
    ctx = lax.axis_index("ctx")

    smaller = jnp.sum(
        (segment[:, None] < jnp.arange(HEAD_DIM, dtype=jnp.int32)[None, :]).astype(F32), axis=0
    ).astype(BF16)
    own = jnp.concatenate([k_cache, v_cache, jnp.broadcast_to(smaller[None, :], (16, HEAD_DIM))], axis=0)[None]

    own, other, hidden = lax.optimization_barrier((own, swap_cores(own), hidden))
    pair = jnp.concatenate([own, other], axis=0)
    z_near = along_z(pair)
    y_near = along_y(pair)
    y_far = move(pair, lambda y, z, c: (y + 2, z, c) if y < 2 else None)
    z_far = move(own, lambda y, z, c: (y, z + 2, c))

    widened = hidden.astype(F32)
    normed = (widened * lax.rsqrt(jnp.mean(widened * widened, axis=-1, keepdims=True) + 1e-06)).astype(BF16)
    q_t = (
        lax.dot_general(w_query, normed, (((0,), (1,)), ((), ())), preferred_element_type=F32) * HEAD_DIM ** (-0.5)
    ).astype(BF16)
    hot = (jnp.arange(HEAD_DIM, dtype=jnp.int32)[:, None] == segment[None, :]).astype(BF16)
    q = jnp.concatenate([q_t, hot], axis=0)

    (z_near, z_far, y_near, y_far), q = lax.optimization_barrier(((z_near, z_far, y_near, y_far), q))
    row = jnp.concatenate([z_near, z_far], axis=0)
    up = up_y(row)
    around = round_y(row)
    far_near = along_z(y_far, 2)
    far_far = move(z_far, lambda y, z, c: (y + 2, z, c) if y < 2 else None)
    q_2 = swap_cores(q)

    at = jnp.stack([ctx, lax.axis_index("section")]).astype(jnp.int32)

    def attend(kernel, n, pieces, queries, states, name):
        out_shape = (STATE,) * len(queries)
        return pl.pallas_call(
            kernel,
            out_shape=out_shape,
            in_specs=[SMEM] + [VMEM] * (len(pieces) + len(queries) + len(states)),
            out_specs=(VMEM,) * len(out_shape),
            scratch_shapes=[pltpu.VMEM((n, PACK, HEAD_DIM), BF16), pltpu.SMEM((16,), jnp.int32)],
            compiler_params=LIMIT,
            cost_estimate=cost(1),
            name=name,
        )(at, *pieces, *queries, *states)

    pieces = [own, z_near, z_far, y_near, y_far]
    first = functools.partial(start_kernel, first_slots, len(pieces))
    state, state_2 = attend(first, 7, pieces, (q, q_2), (), "attend_first")
    up, state, state_2 = lax.optimization_barrier((up, state, state_2))
    near = functools.partial(more_kernel, up_slots, 1, (0, 1))
    state, state_2 = attend(near, 3, [up], (q, q_2), (state, state_2), "attend_up")
    fars, state, state_2 = lax.optimization_barrier(((far_near, far_far), state, state_2))
    state, state_2, w_held = pl.pallas_call(
        functools.partial(more_and_fetch_kernel, far_slots, 2, (0, 1)),
        out_shape=(STATE, STATE, jax.ShapeDtypeStruct(w_out.shape, BF16)),
        in_specs=[SMEM] + [VMEM] * 6 + [pl.BlockSpec(memory_space=pltpu.HBM)],
        out_specs=(VMEM,) * 3,
        scratch_shapes=[
            pltpu.VMEM((3, PACK, HEAD_DIM), BF16),
            pltpu.SMEM((16,), jnp.int32),
            pltpu.SemaphoreType.DMA,
        ],
        compiler_params=pltpu.CompilerParams(vmem_limit_bytes=LAST_LIMIT * 1024 * 1024),
        cost_estimate=cost(1),
        name="attend_far",
    )(at, *fars, q, q_2, state, state_2, w_out)
    pieces, state, state_2 = lax.optimization_barrier(((around,), state, state_2))
    rest = functools.partial(more_kernel, rest_slots, len(pieces), (1,))
    (state_2,) = attend(rest, 3, pieces, (q_2,), (state_2,), "attend_rest_other")
    state_2, state = lax.optimization_barrier((state_2, state))
    rest = functools.partial(more_kernel, rest_slots, len(pieces), (0,))
    (state,) = attend(rest, 3, pieces, (q,), (state,), "attend_rest_own")
    state_2 = swap_cores(state_2)

    out_shape = []
    for rows, _ in CHAINS:
        out_shape += [jax.ShapeDtypeStruct((4, rows.stop - rows.start, COLS), BF16)] * 2
    outs = pl.pallas_call(
        last_kernel,
        out_shape=tuple(out_shape),
        in_specs=[SMEM, VMEM, VMEM, VMEM],
        out_specs=(VMEM,) * 6,
        scratch_shapes=[pltpu.VMEM((BLOCK, 4 * HEAD_DIM), BF16)],
        compiler_params=LIMIT,
        cost_estimate=cost(12),
        name="project_attended",
    )(at, state, state_2, w_held)

    def exchange(x, step):
        return lax.ppermute(x, "section", [(i, i ^ step) for i in range(8)])

    mixed = []
    for i, (_, (first, second, third)) in enumerate(CHAINS):
        sent, kept = outs[2 * i], outs[2 * i + 1]
        four = kept.astype(F32) + exchange(sent, first).astype(F32)
        two = four[:2] + exchange(four[2:].astype(BF16), second).astype(F32)
        mixed.append(two[0] + exchange(two[1].astype(BF16), third).astype(F32))
    return jnp.concatenate(mixed, axis=0).astype(BF16)


def solution(mesh):
    return jax.shard_map(
        per_device,
        mesh=mesh,
        in_specs=(
            P("ctx", None),
            P("ctx", "section"),
            P("ctx", "section"),
            P("ctx"),
            P(None, "section"),
            P("section", None),
        ),
        out_specs=P("ctx", "section"),
        check_vma=False,
    )
```
